256 devices in a mesh: emb: 64 (over z_hi, x, y), rep: 4 (over z_lo, core).
Axes of the slice: x: 4, y: 4, z: 8 (z_hi: 4, z_lo: 2; z = z_hi * 2 + z_lo), core: 2. Of those that a mesh axis runs over, the one named last changes fastest.
Arguments:
- feature_ids: int32 [8192, 4, 128, 2], P(None, 'rep', 'emb'), may hold values from 0 to 511
- bag_lengths: int32 [8192, 4, 128], P(None, 'rep', 'emb'), may hold values from 1 to 2
- click_labels: int32 [8192, 4], P('emb', 'rep'), may hold values 0 or 1
- tables: bfloat16 [128, 512, 192], P('emb'), may hold values from -4 to 4
- projection: bfloat16 [128, 16], replicated, may hold values from -0.5 to 0.5
- compress: bfloat16 [32, 128], replicated, may hold values from -0.5 to 0.5
- w_in: bfloat16 [2048, 256], replicated, may hold values from -0.125 to 0.125
- w_out: bfloat16 [256, 768], replicated, may hold values from -0.375 to 0.375
- w_head: bfloat16 [6912], replicated, may hold values from -0.078125 to 0.078125
Outputs:
- loss: float32 [], replicated
- grad_projection: float32 [128, 16], replicated
- grad_compress: float32 [32, 128], replicated
- grad_w_in: float32 [2048, 256], replicated
- grad_w_out: float32 [256, 768], replicated
- grad_w_head: float32 [6912], replicated
- grad_tables: float32 [128, 512, 192], P('emb')
The draws below stay inside these ranges and needn't reach their ends.
All inputs are finite; a program needn't handle non-finite values. No bound on the sum of `click_labels` on one device may be relied on, other than what follows from the above.
Results may differ from the reference program's by a relative error of at most 0.0065.
Values may be sent and summed in bfloat16 or wider, within the bound.
A program may use at most 128 MiB of HBM per device.

```python
import jax
import jax.numpy as jnp
from jax import lax

D = 192
F = 128
RANK = 16
NL = 32
NF = 4
HID = 256
BAG = 2
ROWS = 512
B_DEV = 128
B_REP = 8192
TOTAL = 32768
N_REP = 4


def with_ends(result, stream_key, least, largest):
    extent = result.shape
    spot = [jax.random.randint(jax.random.fold_in(stream_key, axis), (), 0, extent[axis]) for axis in range(len(extent))]
    result = result.at[tuple(spot)].set(least)
    longest = extent.index(max(extent))
    spot[longest] = (spot[longest] + 1) % extent[longest]
    return result.at[tuple(spot)].set(largest)


def block_levels(rng, dims, pieces, smallest, largest):
    factor_of = 1.0
    for dim, blocks in pieces:
        heights = jax.random.uniform(jax.random.fold_in(jax.random.fold_in(rng, 6), dim), (blocks,), jnp.float32, smallest / len(pieces), largest / len(pieces))
        factor_of = factor_of * jnp.repeat(jnp.exp(heights), dims[dim] // blocks).reshape((-1,) + (1,) * (len(dims) - 1 - dim))
    return factor_of


def gaussian(own_key, extent, scale, most, shards=(), held_as=jnp.bfloat16):
    result = jax.random.normal(own_key, extent, jnp.float32) * scale
    if len(shards) > 0:
        result = block_levels(own_key, extent, shards, -0.22, 0.18) * result
    return jnp.clip(result, min=-most, max=most).astype(held_as)


def setup_inputs(seed: int = 0) -> dict:
    splits = jax.random.split(jax.random.key(seed), 10)
    feature_ids = with_ends(jax.random.randint(splits[0], (B_REP, N_REP, F, BAG), 0, ROWS), jax.random.fold_in(splits[0], 1), 0, ROWS - 1).astype(jnp.int32)
    bag_lengths = with_ends(jax.random.randint(splits[1], (B_REP, N_REP, F), 1, BAG + 1), jax.random.fold_in(splits[1], 1), 1, BAG).astype(jnp.int32)
    click_labels = with_ends((jax.random.randint(splits[2], (B_REP, N_REP), 0, 2) < 1).astype(jnp.int32), jax.random.fold_in(splits[2], 1), 0, 1)
    tables = gaussian(splits[3], (F, ROWS, D), 0.6, 4.0, ((0, 64),))
    projection = gaussian(splits[4], (F, RANK), F ** -0.5, 0.5)
    compress = gaussian(splits[5], (NL, F), F ** -0.5, 0.5)
    w_in = gaussian(splits[6], (F * RANK, HID), (F * RANK) ** -0.5, 0.125)
    w_out = gaussian(splits[7], (HID, NF * D), HID ** -0.5, 0.375)
    w_head = gaussian(splits[8], ((NF + NL) * D,), ((NF + NL) * D) ** -0.5, 0.078125)
    return dict(feature_ids=feature_ids, bag_lengths=bag_lengths, click_labels=click_labels, tables=tables, projection=projection, compress=compress, w_in=w_in, w_out=w_out, w_head=w_head)


EPS = 1e-05

def einmix(form, left, right):
    return jnp.einsum(form, left.astype(jnp.float32), right.astype(jnp.float32))

def block_pass(embedded, target, projection, compress, w_in, w_out, w_head, scale):
    count = embedded.shape[0]
    compact = einmix('bfd,fk->bdk', embedded, projection).astype(jnp.bfloat16)
    interact = einmix('bfd,bdk->bfk', embedded, compact)
    flat = interact.reshape(count, -1)
    center = lax.optimization_barrier(jnp.mean(flat, 1, keepdims=True))
    shifted = flat - center
    rstd = lax.rsqrt(lax.optimization_barrier(jnp.mean(shifted * shifted, 1, keepdims=True)) + EPS)
    normed = shifted * rstd
    normed_bf = normed.astype(jnp.bfloat16)
    pre_act = jnp.dot(normed_bf, w_in, preferred_element_type=jnp.float32)
    hidden = jax.nn.silu(pre_act).astype(jnp.bfloat16)
    factor_out = jnp.dot(hidden, w_out, preferred_element_type=jnp.float32)
    linear_out = einmix('lf,bfd->bld', compress, embedded)
    joined = jnp.concatenate([factor_out, linear_out.reshape(count, -1)], 1)
    head = w_head.astype(jnp.float32)
    logits = lax.optimization_barrier(jnp.sum(joined * head[None, :], 1))
    loss_terms = jax.nn.softplus(logits) - target * logits
    slope = scale * (jax.nn.sigmoid(logits) - target)
    grad_head = lax.optimization_barrier(jnp.sum(slope[:, None] * joined, 0))
    grad_joined = slope[:, None] * head[None, :]
    n_out = w_out.shape[1]
    grad_factor = grad_joined[:, :n_out].astype(jnp.bfloat16)
    grad_linear = grad_joined[:, n_out:].reshape(linear_out.shape).astype(jnp.bfloat16)
    grad_wout = jnp.dot(hidden.T, grad_factor, preferred_element_type=jnp.float32)
    grad_hidden = jnp.dot(grad_factor, w_out.T, preferred_element_type=jnp.float32)
    sigma = jax.nn.sigmoid(pre_act)
    grad_pre = (grad_hidden * sigma * (1.0 + pre_act * (1.0 - sigma))).astype(jnp.bfloat16)
    grad_win = jnp.dot(normed_bf.T, grad_pre, preferred_element_type=jnp.float32)
    grad_normed = jnp.dot(grad_pre, w_in.T, preferred_element_type=jnp.float32)
    grad_flat = rstd * (grad_normed - lax.optimization_barrier(jnp.mean(grad_normed, 1, keepdims=True)) - normed * lax.optimization_barrier(jnp.mean(grad_normed * normed, 1, keepdims=True)))
    grad_interact = grad_flat.astype(jnp.bfloat16).reshape(interact.shape)
    grad_compact = einmix('bfd,bfk->bdk', embedded, grad_interact).astype(jnp.bfloat16)
    grad_embedded = einmix('bfk,bdk->bfd', grad_interact, compact) + einmix('fk,bdk->bfd', projection, grad_compact) + einmix('lf,bld->bfd', compress, grad_linear)
    grad_proj = einmix('bfd,bdk->fk', embedded, grad_compact)
    grad_comp = einmix('bld,bfd->lf', grad_linear, embedded)
    return (grad_embedded.astype(jnp.bfloat16), jnp.sum(loss_terms), grad_proj, grad_comp, grad_win, grad_wout, grad_head)

def reference(feature_ids, bag_lengths, click_labels, tables, projection, compress, w_in, w_out, w_head):
    blocks = TOTAL // B_DEV
    ids_all = feature_ids.reshape(blocks, B_DEV, F, BAG)
    lens_all = bag_lengths.reshape(blocks, B_DEV, F)
    labels_all = click_labels.reshape(blocks, B_DEV).astype(jnp.float32)
    flat_tables = tables.reshape(F * ROWS, D)
    offsets = (jnp.arange(F, dtype=jnp.int32) * ROWS)[None, :]
    scale = 1.0 / TOTAL ** 0.5

    def step(carry, inputs):
        ids_now, lens_now, target = inputs
        pooled = jnp.zeros((B_DEV, F, D), jnp.float32)
        for slot in range(BAG):
            live = (lens_now > slot).astype(jnp.float32)[..., None]
            picked = jnp.take(flat_tables, (ids_now[:, :, slot] + offsets).astype(jnp.int32), axis=0)
            pooled = pooled + live * picked.astype(jnp.float32)
        embedded = pooled.astype(jnp.bfloat16)
        results = block_pass(embedded, target, projection, compress, w_in, w_out, w_head, scale)
        grad_rows = results[0].astype(jnp.float32)
        table_grad = carry[6]
        for slot in range(BAG):
            live = (lens_now > slot).astype(jnp.float32)[..., None]
            index = (ids_now[:, :, slot] + offsets).astype(jnp.int32).reshape(-1)
            table_grad = table_grad + jax.ops.segment_sum((live * grad_rows).reshape(-1, D), index, num_segments=F * ROWS)
        sums = tuple((carry[k] + results[k + 1] for k in range(6)))
        return (sums + (table_grad,), None)
    start = (jnp.zeros((), jnp.float32), jnp.zeros((F, RANK), jnp.float32), jnp.zeros((NL, F), jnp.float32), jnp.zeros((F * RANK, HID), jnp.float32), jnp.zeros((HID, NF * D), jnp.float32), jnp.zeros(((NF + NL) * D,), jnp.float32), jnp.zeros((F * ROWS, D), jnp.float32))
    final, unused = lax.scan(step, start, (ids_all, lens_all, labels_all))
    return (final[0] / TOTAL, final[1], final[2], final[3], final[4], final[5], final[6].reshape(F, ROWS, D))
```

```python
import functools
import math

import jax
import jax.numpy as jnp
from jax import lax
from jax.experimental import pallas as pl
from jax.experimental.pallas import tpu as pltpu
from jax.sharding import Mesh, PartitionSpec as P

EPS = 1e-05
BF = jnp.bfloat16
F32 = jnp.float32
NT = (((1,), (1,)), ((), ()))
TN = (((0,), (0,)), ((), ()))
VMEM_LIMIT = 60 * 1024 * 1024


def mm(a, b, dims=None):
    if dims is None:
        return jnp.dot(a, b, preferred_element_type=F32)
    return lax.dot_general(a, b, dims, preferred_element_type=F32)


def lookup_kernel(ids_ref, w1_ref, w2_ref, y_ref, col_ref):
    n_dest, n_f = y_ref.shape[:2]
    half = n_dest * 64
    rows = w1_ref.shape[1]
    for i in range(2 * half // 128):
        col_ref[pl.ds(i * 128, 128), :] = ids_ref[:, i * 128 : (i + 1) * 128].T
    group = 4

    def chunk(c, carry):
        base = pl.multiple_of(c * group * 64, group * 64)
        for f in range(n_f):
            parts = []
            for h, w_ref in ((0, w1_ref), (1, w2_ref)):
                both = col_ref[pl.ds(h * half + base, group * 64), 2 * f : 2 * f + 2]
                lane = lax.broadcasted_iota(jnp.int32, (group * 64, rows), 1)
                hot = jnp.where(lane == both[:, 0:1], 1.0, 0.0) + jnp.where(
                    lane == both[:, 1:2], 1.0, 0.0
                )
                parts.append(mm(hot.astype(BF), w_ref[f]))
            p1, p2 = parts
            rest = p1[:, 128:] + p2[:, 128:]
            for k, block in enumerate((p1[:, :128], p2[:, :128], rest)):
                y_ref[pl.ds(c * group, group), f, k * 64 : (k + 1) * 64, :] = block.astype(
                    BF
                ).reshape(group, 64, 128)
        return carry

    lax.fori_loop(0, n_dest // group, chunk, 0)


def scatter_kernel(ids_ref, g_ref, out_ref):
    n_src, n_f = g_ref.shape[:2]
    half = n_src * 64
    rows = out_ref.shape[1]
    group = 4
    for f in range(n_f):
        sums = [jnp.zeros((rows, 256), F32), jnp.zeros((rows, 256), F32)]
        for c in range(n_src // group):
            rest = g_ref[c * group : (c + 1) * group, f, 128:192, :].reshape(group * 64, 128)
            for h in range(2):
                base = h * half + c * group * 64
                row = lax.broadcasted_iota(jnp.int32, (rows, group * 64), 0)
                id0 = ids_ref[2 * f : 2 * f + 1, base : base + group * 64]
                id1 = ids_ref[2 * f + 1 : 2 * f + 2, base : base + group * 64]
                hot = jnp.where(row == id0, 1.0, 0.0) + jnp.where(row == id1, 1.0, 0.0)
                main = g_ref[c * group : (c + 1) * group, f, h * 64 : (h + 1) * 64, :].reshape(
                    group * 64, 128
                )
                sums[h] = sums[h] + mm(hot.astype(BF), jnp.concatenate([main, rest], 1))
        s1, s2 = sums
        out_ref[f, :, :128] = s1[:, :128] + s2[:, :128]
        tail = s1[:, 128:] + pltpu.roll(s2[:, 128:], 64, 1)
        out_ref[f, :, 128:192] = tail[:, :64]


def dense_kernel(
    scale,
    x_ref,
    wt_ref,
    win_ref,
    wout_ref,
    head_ref,
    hpair_ref,
    label_ref,
    g_ref,
    loss_ref,
    gw_ref,
    gwin_ref,
    gwout_ref,
    ghead_ref,
    ghl_ref,
    split_ref,
    xp_ref,
    mix_ref,
    inter_ref,
    nb_ref,
    ld_ref,
    slope_ref,
):
    n_f = x_ref.shape[0]
    n_b = 128
    n_k = 16
    tile = 16
    lane1 = lax.broadcasted_iota(jnp.int32, (n_k, 384), 1) < 192
    row_lane1 = lax.broadcasted_iota(jnp.int32, (1, 384), 1) < 192
    wt = wt_ref[...]

    def load_group(q, carry):
        for part in range(3):
            block = x_ref[:, pl.ds(pl.multiple_of(part * 64 + q * tile, tile), tile), :]
            split_ref[part] = block.astype(F32).reshape(n_f * tile, 128)

        def pair(j, inner):
            p = q * tile + j
            pieces = [
                split_ref[part, pl.ds(j, n_f, stride=tile), :].astype(BF) for part in (0, 2, 1)
            ]
            x3 = jnp.concatenate(pieces, 1)
            xp_ref[p] = x3
            mixed = mm(wt, x3)
            mix_ref[p] = mixed
            compact = mixed[:n_k]
            stacked = jnp.concatenate(
                [jnp.where(lane1, compact, 0.0), jnp.where(lane1, 0.0, compact)], 0
            ).astype(BF)
            inter = mm(stacked, x3, NT)
            inter_ref[pl.ds(p, n_k, stride=n_b), :] = inter[:n_k]
            inter_ref[pl.ds(64 + p, n_k, stride=n_b), :] = inter[n_k:]
            ld_ref[pl.ds(p, 1), :] = jnp.sum(mixed[n_k:] * hpair_ref[...], 0, keepdims=True)
            return inner

        lax.fori_loop(0, tile, pair, 0, unroll=2)
        return carry

    lax.fori_loop(0, 64 // tile, load_group, 0)

    total = jnp.zeros((n_b, n_f), F32)
    for k in range(n_k):
        total = total + inter_ref[k * n_b : (k + 1) * n_b, :]
    width = n_k * n_f
    center = jnp.sum(total, 1, keepdims=True) / width
    total = jnp.zeros((n_b, n_f), F32)
    for k in range(n_k):
        shifted = inter_ref[k * n_b : (k + 1) * n_b, :] - center
        total = total + shifted * shifted
    rstd = lax.rsqrt(jnp.sum(total, 1, keepdims=True) / width + EPS)
    for k in range(n_k):
        normed = (inter_ref[k * n_b : (k + 1) * n_b, :] - center) * rstd
        inter_ref[k * n_b : (k + 1) * n_b, :] = normed
        nb_ref[:, k * n_f : (k + 1) * n_f] = normed.astype(BF)
    pre_act = mm(nb_ref[...], win_ref[...])
    sigma = 1.0 / (1.0 + jnp.exp(-pre_act))
    hidden = (pre_act * sigma).astype(BF)
    factor = mm(hidden, wout_ref[...])
    head = head_ref[...]
    lin = ld_ref[...]
    lin1 = jnp.sum(jnp.where(row_lane1, lin, 0.0), 1, keepdims=True)
    lin2 = jnp.sum(jnp.where(row_lane1, 0.0, lin), 1, keepdims=True)
    logit = jnp.sum(factor * head, 1, keepdims=True) + jnp.concatenate([lin1, lin2], 0)
    target = label_ref[...]
    terms = jnp.maximum(logit, 0.0) + jnp.log1p(jnp.exp(-jnp.abs(logit))) - target * logit
    loss_ref[...] = jnp.sum(jnp.broadcast_to(terms, (n_b, 128)), 0, keepdims=True)
    slope = scale * (1.0 / (1.0 + jnp.exp(-logit)) - target)
    slope_ref[...] = jnp.broadcast_to(slope, (n_b, 128))
    ghead_ref[...] = jnp.sum(slope * factor, 0, keepdims=True)
    gfactor = (slope * head).astype(BF)
    gwout_ref[...] = mm(hidden, gfactor, TN)
    ghidden = mm(gfactor, wout_ref[...], NT)
    gpre = (ghidden * sigma * (1.0 + pre_act * (1.0 - sigma))).astype(BF)
    first = jnp.zeros((n_b, n_f), F32)
    second = jnp.zeros((n_b, n_f), F32)
    for k in range(n_k):
        rows = slice(k * n_f, (k + 1) * n_f)
        gwin_ref[rows, :] = mm(nb_ref[:, rows], gpre, TN)
        gnormed = mm(gpre, win_ref[rows, :], NT)
        first = first + gnormed
        second = second + gnormed * inter_ref[k * n_b : (k + 1) * n_b, :]
    mean1 = jnp.sum(first, 1, keepdims=True) / width
    mean2 = jnp.sum(second, 1, keepdims=True) / width
    for k in range(n_k):
        rows = slice(k * n_f, (k + 1) * n_f)
        span = slice(k * n_b, (k + 1) * n_b)
        gnormed = mm(gpre, win_ref[rows, :], NT)
        inter_ref[span, :] = rstd * (gnormed - mean1 - inter_ref[span, :] * mean2)

    gw_ref[...] = jnp.zeros_like(gw_ref)
    ghl_ref[...] = jnp.zeros_like(ghl_ref)

    def back_group(q, carry):
        def pair(j, inner):
            p = q * tile + j
            x3 = xp_ref[p]
            gi = jnp.concatenate(
                [
                    inter_ref[pl.ds(p, n_k, stride=n_b), :],
                    inter_ref[pl.ds(64 + p, n_k, stride=n_b), :],
                ],
                0,
            ).astype(BF)
            gc = mm(gi, x3)
            gc = jnp.where(lane1, gc[:n_k], gc[n_k:]).astype(BF)
            s1 = slope_ref[pl.ds(p, 1), :]
            s2 = slope_ref[pl.ds(64 + p, 1), :]
            srow = jnp.where(
                row_lane1,
                jnp.concatenate([s1, s1, s1], 1),
                jnp.concatenate([s2, s2, s2], 1),
            )
            gl = (srow * hpair_ref[...]).astype(BF)
            mixed = mix_ref[p]
            ghl_ref[...] += srow * mixed[n_k:]
            compact = mixed[:n_k]
            tail = jnp.concatenate([gc, gl], 0)
            right = jnp.concatenate(
                [
                    jnp.where(lane1, compact, 0.0).astype(BF),
                    jnp.where(lane1, 0.0, compact).astype(BF),
                    tail,
                ],
                0,
            )
            left = jnp.concatenate([gi, wt], 0)
            gp = mm(left, right, TN)
            gw_ref[...] += mm(tail, x3, NT)
            for part, at in ((0, 0), (2, 128), (1, 256)):
                split_ref[part, pl.ds(j, n_f, stride=tile), :] = gp[:, at : at + 128]
            return inner

        lax.fori_loop(0, tile, pair, 0, unroll=2)
        for part in range(3):
            g_ref[:, pl.ds(pl.multiple_of(part * 64 + q * tile, tile), tile), :] = (
                split_ref[part].reshape(n_f, tile, 128).astype(BF)
            )
        return carry

    lax.fori_loop(0, 64 // tile, back_group, 0)


def whole(n):
    return [pl.BlockSpec(memory_space=pltpu.VMEM)] * n


def lookup(ids, w1, w2, n_dest):
    n_f = w1.shape[0]
    return pl.pallas_call(
        lookup_kernel,
        out_shape=jax.ShapeDtypeStruct((n_dest, n_f, 192, 128), BF),
        in_specs=whole(3),
        out_specs=whole(1)[0],
        scratch_shapes=[pltpu.VMEM((ids.shape[1], ids.shape[0]), jnp.int32)],
        compiler_params=pltpu.CompilerParams(vmem_limit_bytes=VMEM_LIMIT),
        name="lookup",
    )(ids, w1, w2)


def scatter(ids, g, rows):
    n_f = g.shape[1]
    return pl.pallas_call(
        scatter_kernel,
        out_shape=jax.ShapeDtypeStruct((n_f, rows, 192), F32),
        in_specs=whole(2),
        out_specs=whole(1)[0],
        compiler_params=pltpu.CompilerParams(vmem_limit_bytes=VMEM_LIMIT),
        name="table_grad",
    )(ids, g)


def dense(scale, x, wt, win, wout, head, hpair, label):
    n_f = x.shape[0]
    shapes = [
        (x.shape, BF),
        ((1, 128), F32),
        ((48, n_f), F32),
        (win.shape, F32),
        (wout.shape, F32),
        (head.shape, F32),
        ((32, 384), F32),
    ]
    return pl.pallas_call(
        functools.partial(dense_kernel, scale),
        out_shape=[jax.ShapeDtypeStruct(*s) for s in shapes],
        in_specs=whole(7),
        out_specs=whole(7),
        scratch_shapes=[
            pltpu.VMEM((3, n_f * 16, 128), F32),
            pltpu.VMEM((64, n_f, 384), BF),
            pltpu.VMEM((64, 48, 384), F32),
            pltpu.VMEM((16 * 128, n_f), F32),
            pltpu.VMEM((128, 16 * n_f), BF),
            pltpu.VMEM((64, 384), F32),
            pltpu.VMEM((128, 128), F32),
        ],
        compiler_params=pltpu.CompilerParams(vmem_limit_bytes=VMEM_LIMIT),
        name="dense",
    )(x, wt, win, wout, head, hpair, label)


def table_weights(t):
    zeros = jnp.zeros(t.shape[:2] + (64,), t.dtype)
    w1 = jnp.concatenate([t, zeros], 2)
    w2 = jnp.concatenate([t[:, :, :128], zeros, t[:, :, 128:]], 2)
    return w1, w2


def order_ids(feature_ids, bag_lengths, n_zh, n_plane, rows):
    ids = feature_ids[:, 0].transpose(1, 2, 0)
    lens = bag_lengths[:, 0].T
    slots = jnp.arange(ids.shape[1], dtype=jnp.int32)[None, :, None]
    ids = jnp.where(lens[:, None, :] > slots, ids, rows)
    ids = ids.reshape(-1, n_zh, n_plane, 2, 64).transpose(1, 0, 3, 2, 4)
    return ids.reshape(n_zh, -1, n_plane * 128)


def pair_head(w_head, n_out):
    lin = w_head[n_out:].astype(F32).reshape(-1, 192)
    return jnp.concatenate([lin, lin[:, 128:], lin[:, :128]], 1)


def per_device(
    feature_ids, bag_lengths, click_labels, tables, projection, compress, w_in, w_out, w_head
):
    n_zh = lax.axis_size("zh")
    n_plane = lax.axis_size("x") * lax.axis_size("y")
    n_rep = lax.axis_size("zl") * lax.axis_size("c")
    f_dev, rows, width = tables.shape
    b_rep = feature_ids.shape[0]
    n_feat, n_rank = projection.shape
    n_lin = compress.shape[0]
    n_out = w_out.shape[1]
    total = b_rep * n_rep
    scale = 1.0 / math.sqrt(total)

    ids = order_ids(feature_ids, bag_lengths, n_zh, n_plane, rows)
    ids = lax.all_to_all(ids, "zh", split_axis=0, concat_axis=0, tiled=True)
    ids = ids.reshape(-1, n_plane * 128)
    all_tables = lax.all_gather(tables, "zh", axis=0, tiled=True)
    w1, w2 = table_weights(all_tables)
    y = lookup(ids, w1, w2, n_plane)
    x = lax.all_to_all(y, ("x", "y"), split_axis=0, concat_axis=0, tiled=True)
    x = x.reshape(n_feat, 192, 128)

    def mix_order(a):
        rest = a.shape[1:]
        a = a.reshape((n_zh, n_plane, f_dev) + rest)
        return jnp.swapaxes(a, 0, 1).reshape((n_feat,) + rest)

    wt = jnp.concatenate([mix_order(projection), mix_order(compress.T)], 1).T
    win = mix_order(w_in.reshape(n_feat, n_rank, -1)).transpose(1, 0, 2).reshape(w_in.shape)
    head = w_head[:n_out].astype(F32)[None, :]
    hpair = pair_head(w_head, n_out)
    label = click_labels.astype(F32)
    g, loss, gw, gwin, gwout, ghead, ghl = dense(
        scale, x, wt, win, w_out, head, hpair, label
    )
    back = lax.all_to_all(
        g.reshape(y.shape), ("x", "y"), split_axis=0, concat_axis=0, tiled=True
    )
    partial = scatter(ids, back, rows)
    partial = lax.psum(partial, ("zl", "c"))
    table_grad = lax.psum_scatter(partial, "zh", scatter_dimension=0, tiled=True)

    ghl = ghl[:, :192] + jnp.concatenate([ghl[:, 256:], ghl[:, 192:256]], 1)
    sums = lax.psum(
        (loss[0, 0], gw, gwin, gwout, ghead[0], ghl), ("zh", "x", "y", "zl", "c")
    )
    loss, gw, gwin, gwout, ghead, ghl = sums

    def natural(a):
        rest = a.shape[1:]
        a = a.reshape((n_plane, n_zh, f_dev) + rest)
        return jnp.swapaxes(a, 0, 1).reshape((n_feat,) + rest)

    gw = natural(gw.T)
    gwin = natural(gwin.reshape(n_rank, n_feat, -1).transpose(1, 0, 2)).reshape(w_in.shape)
    ghead = jnp.concatenate([ghead, ghl.reshape(-1)])
    return (loss / total, gw[:, :n_rank], gw[:, n_rank:].T, gwin, gwout, ghead, table_grad)


def solution(mesh):
    fine = Mesh(mesh.devices.reshape(4, 4, 4, 2, 2), ("zh", "x", "y", "zl", "c"))
    emb = ("zh", "x", "y")
    rep = ("zl", "c")
    placed = (
        P(None, rep, emb, None),
        P(None, rep, emb),
        P(emb, rep),
        P(emb, None, None),
        P(),
        P(),
        P(),
        P(),
        P(),
    )
    return jax.shard_map(
        per_device,
        mesh=fine,
        in_specs=placed,
        out_specs=(P(), P(), P(), P(), P(), P(), P(emb, None, None)),
        check_vma=False,
    )
```

```python
import functools
import math

import jax
import jax.numpy as jnp
from jax import lax
from jax.experimental import pallas as pl
from jax.experimental.pallas import tpu as pltpu
from jax.sharding import Mesh, PartitionSpec as P

EPS = 1e-05
BF = jnp.bfloat16
F32 = jnp.float32
NT = (((1,), (1,)), ((), ()))
TN = (((0,), (0,)), ((), ()))
VMEM_LIMIT = 60 * 1024 * 1024
MESH = pl.DeviceIdType.MESH
AT_WOUT = 4096
AT_GW = AT_WOUT + 1536
AT_LIN = AT_GW + 48
AT_HEAD = AT_LIN + 64
DEN_ROWS = 6144


def mm(a, b, dims=None):
    if dims is None:
        return jnp.dot(a, b, preferred_element_type=F32)
    return lax.dot_general(a, b, dims, preferred_element_type=F32)


def lookup_kernel(ids_ref, w1_ref, w2_ref, y_ref, col_ref):
    n_dest, n_f = y_ref.shape[:2]
    half = n_dest * 64
    rows = w1_ref.shape[1]
    for i in range(2 * half // 128):
        col_ref[pl.ds(i * 128, 128), :] = ids_ref[:, i * 128 : (i + 1) * 128].T
    group = 4

    def chunk(c, carry):
        base = pl.multiple_of(c * group * 64, group * 64)
        for f in range(n_f):
            parts = []
            for h, w_ref in ((0, w1_ref), (1, w2_ref)):
                both = col_ref[pl.ds(h * half + base, group * 64), 2 * f : 2 * f + 2]
                lane = lax.broadcasted_iota(jnp.int32, (group * 64, rows), 1)
                hot = jnp.where(lane == both[:, 0:1], 1.0, 0.0) + jnp.where(
                    lane == both[:, 1:2], 1.0, 0.0
                )
                parts.append(mm(hot.astype(BF), w_ref[f]))
            p1, p2 = parts
            rest = p1[:, 128:] + p2[:, 128:]
            for k, block in enumerate((p1[:, :128], p2[:, :128], rest)):
                y_ref[pl.ds(c * group, group), f, k * 64 : (k + 1) * 64, :] = block.astype(
                    BF
                ).reshape(group, 64, 128)
        return carry

    lax.fori_loop(0, n_dest // group, chunk, 0)


def scatter_kernel(ids_ref, g_ref, out_ref):
    n_src, n_f = g_ref.shape[:2]
    half = n_src * 64
    rows = out_ref.shape[1] * 2 // 3
    group = 4
    for f in range(n_f):
        sums = [jnp.zeros((rows, 256), F32), jnp.zeros((rows, 256), F32)]
        for c in range(n_src // group):
            rest = g_ref[c * group : (c + 1) * group, f, 128:192, :].reshape(group * 64, 128)
            for h in range(2):
                base = h * half + c * group * 64
                row = lax.broadcasted_iota(jnp.int32, (rows, group * 64), 0)
                id0 = ids_ref[2 * f : 2 * f + 1, base : base + group * 64]
                id1 = ids_ref[2 * f + 1 : 2 * f + 2, base : base + group * 64]
                hot = jnp.where(row == id0, 1.0, 0.0) + jnp.where(row == id1, 1.0, 0.0)
                main = g_ref[c * group : (c + 1) * group, f, h * 64 : (h + 1) * 64, :].reshape(
                    group * 64, 128
                )
                sums[h] = sums[h] + mm(hot.astype(BF), jnp.concatenate([main, rest], 1))
        s1, s2 = sums
        out_ref[f, :rows, :] = s1[:, :128] + s2[:, :128]
        tail = s1[:, 128:] + pltpu.roll(s2[:, 128:], 64, 1)
        low, high = tail[: rows // 2], pltpu.roll(tail[rows // 2 :], 64, 1)
        lane = lax.broadcasted_iota(jnp.int32, low.shape, 1)
        out_ref[f, rows:, :] = jnp.where(lane < 64, low, high)


def dense_kernel(
    scale,
    x_ref,
    wt_ref,
    win_ref,
    wout_ref,
    head_ref,
    hpair_ref,
    label_ref,
    g_ref,
    loss_ref,
    den_ref,
    gw_ref,
    ghl_ref,
    split_ref,
    xp_ref,
    mix_ref,
    inter_ref,
    nb_ref,
    ld_ref,
    slope_ref,
):
    n_f = x_ref.shape[0]
    n_b = 128
    n_k = 16
    tile = 16
    lane1 = lax.broadcasted_iota(jnp.int32, (n_k, 384), 1) < 192
    row_lane1 = lax.broadcasted_iota(jnp.int32, (1, 384), 1) < 192
    wt = wt_ref[...]

    def load_group(q, carry):
        for part in range(3):
            block = x_ref[:, pl.ds(pl.multiple_of(part * 64 + q * tile, tile), tile), :]
            split_ref[part] = block.astype(F32).reshape(n_f * tile, 128)

        def pair(j, inner):
            p = q * tile + j
            pieces = [
                split_ref[part, pl.ds(j, n_f, stride=tile), :].astype(BF) for part in (0, 2, 1)
            ]
            x3 = jnp.concatenate(pieces, 1)
            xp_ref[p] = x3
            mixed = mm(wt, x3)
            mix_ref[p] = mixed
            compact = mixed[:n_k]
            stacked = jnp.concatenate(
                [jnp.where(lane1, compact, 0.0), jnp.where(lane1, 0.0, compact)], 0
            ).astype(BF)
            inter = mm(stacked, x3, NT)
            inter_ref[pl.ds(p, n_k, stride=n_b), :] = inter[:n_k]
            inter_ref[pl.ds(64 + p, n_k, stride=n_b), :] = inter[n_k:]
            ld_ref[pl.ds(p, 1), :] = jnp.sum(mixed[n_k:] * hpair_ref[...], 0, keepdims=True)
            return inner

        lax.fori_loop(0, tile, pair, 0, unroll=2)
        return carry

    lax.fori_loop(0, 64 // tile, load_group, 0)

    total = jnp.zeros((n_b, n_f), F32)
    for k in range(n_k):
        total = total + inter_ref[k * n_b : (k + 1) * n_b, :]
    width = n_k * n_f
    center = jnp.sum(total, 1, keepdims=True) / width
    total = jnp.zeros((n_b, n_f), F32)
    for k in range(n_k):
        shifted = inter_ref[k * n_b : (k + 1) * n_b, :] - center
        total = total + shifted * shifted
    rstd = lax.rsqrt(jnp.sum(total, 1, keepdims=True) / width + EPS)
    for k in range(n_k):
        normed = (inter_ref[k * n_b : (k + 1) * n_b, :] - center) * rstd
        inter_ref[k * n_b : (k + 1) * n_b, :] = normed
        nb_ref[:, k * n_f : (k + 1) * n_f] = normed.astype(BF)
    pre_act = mm(nb_ref[...], win_ref[...])
    sigma = 1.0 / (1.0 + jnp.exp(-pre_act))
    hidden = (pre_act * sigma).astype(BF)
    factor = mm(hidden, wout_ref[...])
    head = head_ref[...]
    lin = ld_ref[...]
    lin1 = jnp.sum(jnp.where(row_lane1, lin, 0.0), 1, keepdims=True)
    lin2 = jnp.sum(jnp.where(row_lane1, 0.0, lin), 1, keepdims=True)
    logit = jnp.sum(factor * head, 1, keepdims=True) + jnp.concatenate([lin1, lin2], 0)
    target = label_ref[...]
    terms = jnp.maximum(logit, 0.0) + jnp.log1p(jnp.exp(-jnp.abs(logit))) - target * logit
    loss_ref[...] = jnp.broadcast_to(
        jnp.sum(jnp.broadcast_to(terms, (n_b, 128)), 0, keepdims=True), loss_ref.shape
    )
    slope = scale * (1.0 / (1.0 + jnp.exp(-logit)) - target)
    slope_ref[...] = jnp.broadcast_to(slope, (n_b, 128))
    den_ref[AT_HEAD:, :] = jnp.zeros((den_ref.shape[0] - AT_HEAD, 128), F32)
    ghead = jnp.sum(slope * factor, 0, keepdims=True)
    for i in range(ghead.shape[1] // 128):
        den_ref[AT_HEAD + i : AT_HEAD + i + 1, :] = ghead[:, i * 128 : (i + 1) * 128]
    gfactor = (slope * head).astype(BF)
    for i in range(gfactor.shape[1] // 128):
        den_ref[AT_WOUT + i * 256 : AT_WOUT + (i + 1) * 256, :] = mm(
            hidden, gfactor[:, i * 128 : (i + 1) * 128], TN
        )
    ghidden = mm(gfactor, wout_ref[...], NT)
    gpre = (ghidden * sigma * (1.0 + pre_act * (1.0 - sigma))).astype(BF)
    first = jnp.zeros((n_b, n_f), F32)
    second = jnp.zeros((n_b, n_f), F32)
    for k in range(n_k):
        rows = slice(k * n_f, (k + 1) * n_f)
        gwin = mm(nb_ref[:, rows], gpre, TN)
        den_ref[rows, :] = gwin[:, :128]
        den_ref[width + k * n_f : width + (k + 1) * n_f, :] = gwin[:, 128:]
        gnormed = mm(gpre, win_ref[rows, :], NT)
        first = first + gnormed
        second = second + gnormed * inter_ref[k * n_b : (k + 1) * n_b, :]
    mean1 = jnp.sum(first, 1, keepdims=True) / width
    mean2 = jnp.sum(second, 1, keepdims=True) / width
    for k in range(n_k):
        rows = slice(k * n_f, (k + 1) * n_f)
        span = slice(k * n_b, (k + 1) * n_b)
        gnormed = mm(gpre, win_ref[rows, :], NT)
        inter_ref[span, :] = rstd * (gnormed - mean1 - inter_ref[span, :] * mean2)

    gw_ref[...] = jnp.zeros_like(gw_ref)
    ghl_ref[...] = jnp.zeros_like(ghl_ref)

    def back_group(q, carry):
        def pair(j, inner):
            p = q * tile + j
            x3 = xp_ref[p]
            gi = jnp.concatenate(
                [
                    inter_ref[pl.ds(p, n_k, stride=n_b), :],
                    inter_ref[pl.ds(64 + p, n_k, stride=n_b), :],
                ],
                0,
            ).astype(BF)
            gc = mm(gi, x3)
            gc = jnp.where(lane1, gc[:n_k], gc[n_k:]).astype(BF)
            s1 = slope_ref[pl.ds(p, 1), :]
            s2 = slope_ref[pl.ds(64 + p, 1), :]
            srow = jnp.where(
                row_lane1,
                jnp.concatenate([s1, s1, s1], 1),
                jnp.concatenate([s2, s2, s2], 1),
            )
            gl = (srow * hpair_ref[...]).astype(BF)
            mixed = mix_ref[p]
            ghl_ref[...] += srow * mixed[n_k:]
            compact = mixed[:n_k]
            tail = jnp.concatenate([gc, gl], 0)
            right = jnp.concatenate(
                [
                    jnp.where(lane1, compact, 0.0).astype(BF),
                    jnp.where(lane1, 0.0, compact).astype(BF),
                    tail,
                ],
                0,
            )
            left = jnp.concatenate([gi, wt], 0)
            gp = mm(left, right, TN)
            gw_ref[...] += mm(tail, x3, NT)
            for part, at in ((0, 0), (2, 128), (1, 256)):
                split_ref[part, pl.ds(j, n_f, stride=tile), :] = gp[:, at : at + 128]
            return inner

        lax.fori_loop(0, tile, pair, 0, unroll=2)
        for part in range(3):
            g_ref[:, pl.ds(pl.multiple_of(part * 64 + q * tile, tile), tile), :] = (
                split_ref[part].reshape(n_f, tile, 128).astype(BF)
            )
        return carry

    lax.fori_loop(0, 64 // tile, back_group, 0)
    den_ref[AT_GW : AT_GW + 48, :] = gw_ref[...]
    ghl = ghl_ref[...]
    second = ghl[:, 128:256]
    lane = lax.broadcasted_iota(jnp.int32, second.shape, 1)
    den_ref[AT_LIN : AT_LIN + 32, :] = ghl[:, :128] + ghl[:, 256:]
    den_ref[AT_LIN + 32 : AT_LIN + 64, :] = jnp.where(
        lane < 64, second + pltpu.roll(second, 64, 1), 0.0
    )


def whole(n):
    return [pl.BlockSpec(memory_space=pltpu.VMEM)] * n


def lookup(ids, w1, w2, n_dest):
    n_f = w1.shape[0]
    return pl.pallas_call(
        lookup_kernel,
        out_shape=jax.ShapeDtypeStruct((n_dest, n_f, 192, 128), BF),
        in_specs=whole(3),
        out_specs=whole(1)[0],
        scratch_shapes=[pltpu.VMEM((ids.shape[1], ids.shape[0]), jnp.int32)],
        compiler_params=pltpu.CompilerParams(vmem_limit_bytes=VMEM_LIMIT),
        name="lookup",
    )(ids, w1, w2)


def scatter(ids, g, rows):
    n_f = g.shape[1]
    return pl.pallas_call(
        scatter_kernel,
        out_shape=jax.ShapeDtypeStruct((n_f, rows * 3 // 2, 128), F32),
        in_specs=whole(2),
        out_specs=whole(1)[0],
        compiler_params=pltpu.CompilerParams(vmem_limit_bytes=VMEM_LIMIT),
        name="table_grad",
    )(ids, g)


def dense(scale, x, wt, win, wout, head, hpair, label):
    n_f = x.shape[0]
    shapes = [
        (x.shape, BF),
        ((8, 128), F32),
        ((DEN_ROWS, 128), F32),
    ]
    return pl.pallas_call(
        functools.partial(dense_kernel, scale),
        out_shape=[jax.ShapeDtypeStruct(*s) for s in shapes],
        in_specs=whole(7),
        out_specs=whole(3),
        scratch_shapes=[
            pltpu.VMEM((48, n_f), F32),
            pltpu.VMEM((32, 384), F32),
            pltpu.VMEM((3, n_f * 16, 128), F32),
            pltpu.VMEM((64, n_f, 384), BF),
            pltpu.VMEM((64, 48, 384), F32),
            pltpu.VMEM((16 * 128, n_f), F32),
            pltpu.VMEM((128, 16 * n_f), BF),
            pltpu.VMEM((64, 384), F32),
            pltpu.VMEM((128, 128), F32),
        ],
        compiler_params=pltpu.CompilerParams(vmem_limit_bytes=VMEM_LIMIT),
        name="dense",
    )(x, wt, win, wout, head, hpair, label)


def reduce_kernel(
    tab_ref,
    den_ref,
    loss_ref,
    out_tab_ref,
    out_den_ref,
    out_loss_ref,
    ta_ref,
    tb_ref,
    tc_ref,
    td_ref,
    te_ref,
    da_ref,
    db_ref,
    dc_ref,
    dd_ref,
    de_ref,
    df_ref,
    la_ref,
    lb_ref,
    lc_ref,
    ls_ref,
    send_ref,
    core_sem,
    tz_sem,
    tr_sem,
    dp_sem,
    dz_sem,
    dg_sem,
    dh_sem,
    lc_sem,
    lp_sem,
    lz_sem,
):
    zh, x, y, zl, c = [lax.axis_index(name) for name in ("zh", "x", "y", "zl", "c")]
    n_y, n_z, n_p = 4, 8, 16
    z = zh * 2 + zl
    p = x * n_y + y
    other = 1 - c

    def at_plane(q):
        return (zh, q // n_y, q % n_y, zl, c)

    def at_z(v):
        return (v // 2, x, y, v % 2, c)

    sibling = (zh, x, y, zl, other)
    replicas = [sibling, (zh, x, y, 1 - zl, c), (zh, x, y, 1 - zl, other)]
    barrier = pltpu.get_barrier_semaphore()
    for d in range(1, n_p):
        pl.semaphore_signal(barrier, inc=1, device_id=at_plane((p + d) % n_p), device_id_type=MESH)
    for d in range(1, n_z):
        pl.semaphore_signal(barrier, inc=1, device_id=at_z((z + d) % n_z), device_id_type=MESH)
    for device in (replicas[0], replicas[2]):
        pl.semaphore_signal(barrier, inc=1, device_id=device, device_id_type=MESH)
    pl.semaphore_wait(barrier, n_p - 1 + n_z - 1 + 2)

    sends = []

    def send(src, dst, sem, device):
        k = len(sends)
        copy = pltpu.make_async_remote_copy(
            src_ref=src,
            dst_ref=dst,
            send_sem=send_ref.at[k],
            recv_sem=sem,
            device_id=device,
            device_id_type=MESH,
        )
        copy.start()
        sends.append(copy)

    def arrived(dst, sem):
        pltpu.make_async_copy(dst, dst, sem).wait()

    half = DEN_ROWS // 2
    for v in range(4):
        ta_ref[v] = tab_ref[2 * v + other].astype(BF)
    send(ta_ref, tb_ref, core_sem.at[0], sibling)
    da_ref[...] = den_ref[pl.ds(pl.multiple_of(other * half, half), half), :].astype(BF)
    send(da_ref, db_ref, core_sem.at[1], sibling)
    send(loss_ref, lc_ref, lc_sem, sibling)

    arrived(tb_ref, core_sem.at[0])
    for v in range(4):
        mine = tab_ref[2 * v + c] + tb_ref[v].astype(F32)
        tc_ref[2 * v] = mine[:384].astype(BF)
        tc_ref[2 * v + 1] = mine[384:].astype(BF)
    for d in range(1, n_z):
        to = (z + d) % n_z
        send(tc_ref.at[to], td_ref.at[z], tz_sem.at[z], at_z(to))

    chunk = half // n_p
    arrived(db_ref, core_sem.at[1])
    for i in range(n_p):
        rows = pl.ds(pl.multiple_of(c * half + i * chunk, chunk), chunk)
        dc_ref[i] = (
            den_ref[rows, :] + db_ref[i * chunk : (i + 1) * chunk, :].astype(F32)
        ).astype(BF)
    for d in range(1, n_p):
        to = (p + d) % n_p
        send(dc_ref.at[to], dd_ref.at[p], dp_sem.at[p], at_plane(to))
    arrived(lc_ref, lc_sem)
    loss = loss_ref[...] + lc_ref[...]
    ls_ref[0] = loss
    for d in range(1, n_p):
        to = (p + d) % n_p
        send(ls_ref.at[0], la_ref.at[p], lp_sem.at[p], at_plane(to))
    la_ref[p] = loss

    own = dc_ref[p].astype(F32)
    for d in range(1, n_p):
        q = (p + d) % n_p
        arrived(dd_ref.at[q], dp_sem.at[q])
        own = own + dd_ref[q].astype(F32)
    de_ref[z] = own.astype(BF)
    for d in range(1, n_z):
        send(de_ref.at[z], de_ref.at[z], dz_sem.at[z], at_z((z + d) % n_z))
    for d in range(1, n_p):
        q = (p + d) % n_p
        arrived(la_ref.at[q], lp_sem.at[q])
    loss = la_ref[0]
    for q in range(1, n_p):
        loss = loss + la_ref[q]
    ls_ref[1] = loss
    for d in range(1, n_z):
        send(ls_ref.at[1], lb_ref.at[z], lz_sem.at[z], at_z((z + d) % n_z))
    lb_ref[z] = loss

    own = tc_ref[z].astype(F32)
    for d in range(1, n_z):
        v = (z + d) % n_z
        arrived(td_ref.at[v], tz_sem.at[v])
        own = own + td_ref[v].astype(F32)
    te_ref[2 * c + zl] = own.astype(BF)
    for device in replicas:
        send(te_ref.at[2 * c + zl], te_ref.at[2 * c + zl], tr_sem.at[2 * c + zl], device)

    for d in range(1, n_z):
        v = (z + d) % n_z
        arrived(de_ref.at[v], dz_sem.at[v])
    own = de_ref[0].astype(F32)
    for v in range(1, n_z):
        own = own + de_ref[v].astype(F32)
    mine = c * n_p + p
    df_ref[mine] = own.astype(BF)
    for d in range(1, n_p):
        send(df_ref.at[mine], df_ref.at[mine], dg_sem.at[p], at_plane((p + d) % n_p))
    send(df_ref.at[mine], df_ref.at[mine], dh_sem.at[p], sibling)

    for d in range(1, 4):
        k = (2 * c + zl + d) % 4
        arrived(te_ref.at[k], tr_sem.at[k])
    n_rows = out_tab_ref.shape[1]
    for j in range(2):
        low, high = te_ref[2 * j].astype(F32), te_ref[2 * j + 1].astype(F32)
        out_tab_ref[j, :384, :128] = low
        out_tab_ref[j, 384:n_rows, :128] = high[: n_rows - 384]
        rest = high[n_rows - 384 :]
        out_tab_ref[j, : n_rows // 2, 128:192] = rest[:, :64]
        out_tab_ref[j, n_rows // 2 :, 128:192] = pltpu.roll(rest, 64, 1)[:, :64]

    for d in range(1, n_z):
        v = (z + d) % n_z
        arrived(lb_ref.at[v], lz_sem.at[v])
    loss = lb_ref[0]
    for v in range(1, n_z):
        loss = loss + lb_ref[v]
    out_loss_ref[...] = loss

    for d in range(1, n_p):
        q = (p + d) % n_p
        arrived(df_ref.at[c * n_p + q], dg_sem.at[q])
        send(df_ref.at[c * n_p + q], df_ref.at[c * n_p + q], dh_sem.at[q], sibling)
    for q in range(n_p):
        arrived(df_ref.at[other * n_p + q], dh_sem.at[q])
    for i in range(2 * n_p):
        out_den_ref[i * chunk : (i + 1) * chunk, :] = df_ref[i].astype(F32)
    for copy in sends:
        copy.wait_send()


def reduce_all(tab, den, loss, rows):
    n_f = tab.shape[0]
    half = DEN_ROWS // 2
    chunk = half // 16
    dma = pltpu.SemaphoreType.DMA
    return pl.pallas_call(
        reduce_kernel,
        out_shape=[
            jax.ShapeDtypeStruct((2, rows, 192), F32),
            jax.ShapeDtypeStruct(den.shape, F32),
            jax.ShapeDtypeStruct(loss.shape, F32),
        ],
        in_specs=whole(3),
        out_specs=whole(3),
        scratch_shapes=[
            pltpu.VMEM((4, 768, 128), BF),
            pltpu.VMEM((4, 768, 128), BF),
            pltpu.VMEM((8, 384, 128), BF),
            pltpu.VMEM((8, 384, 128), BF),
            pltpu.VMEM((4, 384, 128), BF),
            pltpu.VMEM((half, 128), BF),
            pltpu.VMEM((half, 128), BF),
            pltpu.VMEM((16, chunk, 128), BF),
            pltpu.VMEM((16, chunk, 128), BF),
            pltpu.VMEM((8, chunk, 128), BF),
            pltpu.VMEM((32, chunk, 128), BF),
            pltpu.VMEM((16, 8, 128), F32),
            pltpu.VMEM((8, 8, 128), F32),
            pltpu.VMEM((8, 128), F32),
            pltpu.VMEM((2, 8, 128), F32),
            dma((96,)),
            dma((2,)),
            dma((8,)),
            dma((4,)),
            dma((16,)),
            dma((8,)),
            dma((16,)),
            dma((16,)),
            dma,
            dma((16,)),
            dma((8,)),
        ],
        compiler_params=pltpu.CompilerParams(
            vmem_limit_bytes=VMEM_LIMIT, collective_id=0, has_side_effects=True
        ),
        name="reduce",
    )(tab, den, loss)


def table_weights(t):
    zeros = jnp.zeros(t.shape[:2] + (64,), t.dtype)
    w1 = jnp.concatenate([t, zeros], 2)
    w2 = jnp.concatenate([t[:, :, :128], zeros, t[:, :, 128:]], 2)
    return w1, w2


def order_ids(feature_ids, bag_lengths, n_zh, n_plane, rows):
    ids = feature_ids[:, 0].transpose(1, 2, 0)
    lens = bag_lengths[:, 0].T
    slots = jnp.arange(ids.shape[1], dtype=jnp.int32)[None, :, None]
    ids = jnp.where(lens[:, None, :] > slots, ids, rows)
    ids = ids.reshape(-1, n_zh, n_plane, 2, 64).transpose(1, 0, 3, 2, 4)
    return ids.reshape(n_zh, -1, n_plane * 128)


def pair_head(w_head, n_out):
    lin = w_head[n_out:].astype(F32).reshape(-1, 192)
    return jnp.concatenate([lin, lin[:, 128:], lin[:, :128]], 1)


def per_device(
    feature_ids, bag_lengths, click_labels, tables, projection, compress, w_in, w_out, w_head
):
    n_zh = lax.axis_size("zh")
    n_plane = lax.axis_size("x") * lax.axis_size("y")
    n_rep = lax.axis_size("zl") * lax.axis_size("c")
    f_dev, rows, width = tables.shape
    b_rep = feature_ids.shape[0]
    n_feat, n_rank = projection.shape
    n_lin = compress.shape[0]
    n_out = w_out.shape[1]
    total = b_rep * n_rep
    scale = 1.0 / math.sqrt(total)

    ids = order_ids(feature_ids, bag_lengths, n_zh, n_plane, rows)
    ids = lax.all_to_all(ids, "zh", split_axis=0, concat_axis=0, tiled=True)
    ids = ids.reshape(-1, n_plane * 128)
    all_tables = lax.all_gather(tables, "zh", axis=0, tiled=True)
    w1, w2 = table_weights(all_tables)
    y = lookup(ids, w1, w2, n_plane)
    x = lax.all_to_all(y, ("x", "y"), split_axis=0, concat_axis=0, tiled=True)
    x = x.reshape(n_feat, 192, 128)

    def mix_order(a):
        rest = a.shape[1:]
        a = a.reshape((n_zh, n_plane, f_dev) + rest)
        return jnp.swapaxes(a, 0, 1).reshape((n_feat,) + rest)

    wt = jnp.concatenate([mix_order(projection), mix_order(compress.T)], 1).T
    win = mix_order(w_in.reshape(n_feat, n_rank, -1)).transpose(1, 0, 2).reshape(w_in.shape)
    head = w_head[:n_out].astype(F32)[None, :]
    hpair = pair_head(w_head, n_out)
    label = click_labels.astype(F32)
    g, loss, den = dense(scale, x, wt, win, w_out, head, hpair, label)
    back = lax.all_to_all(
        g.reshape(y.shape), ("x", "y"), split_axis=0, concat_axis=0, tiled=True
    )
    partial = scatter(ids, back, rows)
    table_grad, den, loss = reduce_all(partial, den, loss, rows)
    loss = loss[0, 0]
    gwin = jnp.concatenate([den[:2048], den[2048:4096]], 1)
    gwout = den[AT_WOUT:AT_GW].reshape(-1, 256, 128).transpose(1, 0, 2).reshape(w_out.shape)
    gw = den[AT_GW:AT_LIN]
    lin = den[AT_LIN:AT_HEAD].reshape(2, n_lin, 128)
    lin = jnp.concatenate([lin[0], lin[1, :, :64]], 1)
    ghead = jnp.concatenate([den[AT_HEAD : AT_HEAD + n_out // 128].reshape(-1), lin.reshape(-1)])

    def natural(a):
        rest = a.shape[1:]
        a = a.reshape((n_plane, n_zh, f_dev) + rest)
        return jnp.swapaxes(a, 0, 1).reshape((n_feat,) + rest)

    gw = natural(gw.T)
    gwin = natural(gwin.reshape(n_rank, n_feat, -1).transpose(1, 0, 2)).reshape(w_in.shape)
    return (loss / total, gw[:, :n_rank], gw[:, n_rank:].T, gwin, gwout, ghead, table_grad)


def solution(mesh):
    fine = Mesh(mesh.devices.reshape(4, 4, 4, 2, 2), ("zh", "x", "y", "zl", "c"))
    emb = ("zh", "x", "y")
    rep = ("zl", "c")
    placed = (
        P(None, rep, emb, None),
        P(None, rep, emb),
        P(emb, rep),
        P(emb, None, None),
        P(),
        P(),
        P(),
        P(),
        P(),
    )
    return jax.shard_map(
        per_device,
        mesh=fine,
        in_specs=placed,
        out_specs=(P(), P(), P(), P(), P(), P(), P(emb, None, None)),
        check_vma=False,
    )
```

```python
import functools
import math

import jax
import jax.numpy as jnp
from jax import lax
from jax.experimental import pallas as pl
from jax.experimental.pallas import tpu as pltpu
from jax.sharding import Mesh, PartitionSpec as P

EPS = 1e-05
BF = jnp.bfloat16
F32 = jnp.float32
NT = (((1,), (1,)), ((), ()))
TN = (((0,), (0,)), ((), ()))
VMEM_LIMIT = 60 * 1024 * 1024
MESH = pl.DeviceIdType.MESH
AT_WOUT = 4096
AT_GW = AT_WOUT + 1536
AT_LIN = AT_GW + 48
AT_HEAD = AT_LIN + 64
DEN_ROWS = 6144


def mm(a, b, dims=None):
    if dims is None:
        return jnp.dot(a, b, preferred_element_type=F32)
    return lax.dot_general(a, b, dims, preferred_element_type=F32)


def plane_links(zh, zl, c, p):
    def copy(src, dst, send_sems, recv_sems, q, to):
        return pltpu.make_async_remote_copy(
            src_ref=src.at[q, :, to],
            dst_ref=dst.at[q, :, p],
            send_sem=send_sems.at[q, to],
            recv_sem=recv_sems.at[q, p],
            device_id=(zh, to // 4, to % 4, zl, c),
            device_id_type=MESH,
        )

    return copy


def arrived(dst, sem):
    pltpu.make_async_copy(dst, dst, sem).wait()


def main_kernel(
    scale,
    ids_ref,
    tab_ref,
    wt_ref,
    win_ref,
    wout_ref,
    head_ref,
    hpair_ref,
    label_ref,
    part_ref,
    den_ref,
    loss_ref,
    tz_ref,
    idz_ref,
    col_ref,
    w1_ref,
    w2_ref,
    y_ref,
    x_ref,
    bk_ref,
    winp_ref,
    acc_ref,
    gw_ref,
    ghl_ref,
    split_ref,
    xp_ref,
    mix_ref,
    inter_ref,
    nb_ref,
    ld_ref,
    slope_ref,
    zsend,
    zsem,
    fsem,
    isem,
    ysend,
    xrecv,
    gsend,
    brecv,
):
    zh, px, py, zl, c = [lax.axis_index(name) for name in ("zh", "x", "y", "zl", "c")]
    n_p, n_z = 16, 8
    z = zh * 2 + zl
    p = px * 4 + py
    other = 1 - c
    sibling = (zh, px, py, zl, other)
    n_f, n_b, n_k, tile = 128, 128, 16, 16
    rows = w1_ref.shape[1]
    width = n_k * n_f

    barrier = pltpu.get_barrier_semaphore()
    for d in range(1, n_p):
        q = (p + d) % n_p
        pl.semaphore_signal(
            barrier, inc=1, device_id=(zh, q // 4, q % 4, zl, c), device_id_type=MESH
        )
    for d in range(1, n_z):
        v = (z + d) % n_z
        pl.semaphore_signal(
            barrier, inc=1, device_id=(v // 2, px, py, v % 2, c), device_id_type=MESH
        )
    pl.semaphore_signal(barrier, inc=1, device_id=sibling, device_id_type=MESH)
    pl.semaphore_wait(barrier, n_p - 1 + n_z - 1 + 1)

    sends = []

    def send(src, dst, sem, device):
        copy = pltpu.make_async_remote_copy(
            src_ref=src,
            dst_ref=dst,
            send_sem=zsend.at[len(sends)],
            recv_sem=sem,
            device_id=device,
            device_id_type=MESH,
        )
        copy.start()
        sends.append(copy)

    for d in range(1, 4):
        to = (zh + d) % 4
        send(ids_ref.at[to], idz_ref.at[zh], isem.at[zh], (to, px, py, zl, c))
    near = (zh + 3 + 2 * zl) % 4
    for to, lo in ((near, 0), (near, 1), ((zh + 2) % 4, 1 - zl)):
        send(tab_ref.at[c], tz_ref.at[2 * zh + c], zsem.at[zh], (to, px, py, lo, c))
    idz_ref[zh] = ids_ref[zh]
    tz_ref[2 * zh] = tab_ref[0]
    tz_ref[2 * zh + 1] = tab_ref[1]
    for d in (1, 3, 2):
        v = (zh + d) % 4
        arrived(tz_ref.at[2 * v + c], zsem.at[v])
        send(tz_ref.at[2 * v + c], tz_ref.at[2 * v + c], fsem.at[v], sibling)
    for d in range(1, 4):
        v = (zh + d) % 4
        arrived(idz_ref.at[v], isem.at[v])
    for i in range(n_p):
        block = idz_ref[:, :, i * 128 : (i + 1) * 128].reshape(32, 128)
        col_ref[i * 128 : (i + 1) * 128, :] = block.T
    for d in range(1, 4):
        v = (zh + d) % 4
        arrived(tz_ref.at[2 * v + other], fsem.at[v])

    def weights(f, carry):
        main = tz_ref[f, :rows, :]
        rest = tz_ref[f, rows:, :].astype(F32)
        turned = pltpu.roll(rest, 64, 1)
        low = lax.broadcasted_iota(jnp.int32, rest.shape, 1) < 64
        w1_ref[f, :, :128] = main
        w2_ref[f, :, :128] = main
        w1_ref[f, : rows // 2, 128:] = jnp.where(low, rest, 0.0).astype(BF)
        w1_ref[f, rows // 2 :, 128:] = jnp.where(low, turned, 0.0).astype(BF)
        w2_ref[f, : rows // 2, 128:] = jnp.where(low, 0.0, turned).astype(BF)
        w2_ref[f, rows // 2 :, 128:] = jnp.where(low, 0.0, rest).astype(BF)
        return carry

    lax.fori_loop(0, 8, weights, 0)

    link = plane_links(zh, zl, c, p)

    def lookup(q, carry):
        for f in range(8):
            at = 8 * (f // 2) + 2 * (f % 2)
            parts = []
            for h, w_ref in ((0, w1_ref), (1, w2_ref)):
                first = pl.multiple_of((q * 2 + h) * 256, 256)
                both = col_ref[pl.ds(first, 256), at : at + 2]
                lane = lax.broadcasted_iota(jnp.int32, (256, rows), 1)
                hot = jnp.where(lane == both[:, 0:1], 1.0, 0.0) + jnp.where(
                    lane == both[:, 1:2], 1.0, 0.0
                )
                parts.append(mm(hot.astype(BF), w_ref[f]))
            p1, p2 = parts
            rest = p1[:, 128:] + p2[:, 128:]
            for k, block in enumerate((p1[:, :128], p2[:, :128], rest)):
                y_ref[q, f // 2, :, f % 2, k * tile : (k + 1) * tile, :] = block.astype(
                    BF
                ).reshape(n_p, tile, 128)
        for d in range(1, n_p):
            link(y_ref, x_ref, ysend, xrecv, q, (p + d) % n_p).start()
        x_ref[q, :, p] = y_ref[q, :, p]
        return carry

    lax.fori_loop(0, 4, lookup, 0)

    for side in range(2):
        cols = slice(side * 128, (side + 1) * 128)
        split_ref[side] = win_ref[:, cols].astype(F32)
        for k in range(n_k):
            winp_ref[k * n_f : (k + 1) * n_f, cols] = split_ref[
                side, pl.ds(k, n_f, stride=n_k), :
            ].astype(BF)

    lane1 = lax.broadcasted_iota(jnp.int32, (n_k, 384), 1) < 192
    row_lane1 = lax.broadcasted_iota(jnp.int32, (1, 384), 1) < 192
    wt = wt_ref[...]

    def load_group(q, carry):
        for d in range(1, n_p):
            src = (p + n_p - d) % n_p
            arrived(x_ref.at[q, :, src], xrecv.at[q, src])
        for part in range(3):
            block = x_ref[q, :, :, :, part * tile : (part + 1) * tile, :]
            split_ref[part] = block.astype(F32).reshape(n_f * tile, 128)
        def pair(j, inner):
            p = q * tile + j
            pieces = [
                split_ref[part, pl.ds(j, n_f, stride=tile), :].astype(BF) for part in (0, 2, 1)
            ]
            x3 = jnp.concatenate(pieces, 1)
            xp_ref[p] = x3
            mixed = mm(wt, x3)
            mix_ref[p] = mixed
            compact = mixed[:n_k]
            stacked = jnp.concatenate(
                [jnp.where(lane1, compact, 0.0), jnp.where(lane1, 0.0, compact)], 0
            ).astype(BF)
            inter = mm(stacked, x3, NT)
            inter_ref[pl.ds(p, n_k, stride=n_b), :] = inter[:n_k]
            inter_ref[pl.ds(64 + p, n_k, stride=n_b), :] = inter[n_k:]
            ld_ref[pl.ds(p, 1), :] = jnp.sum(mixed[n_k:] * hpair_ref[...], 0, keepdims=True)
            return inner

        lax.fori_loop(0, tile, pair, 0, unroll=2)
        return carry

    lax.fori_loop(0, 64 // tile, load_group, 0)

    total = jnp.zeros((n_b, n_f), F32)
    for k in range(n_k):
        total = total + inter_ref[k * n_b : (k + 1) * n_b, :]
    center = jnp.sum(total, 1, keepdims=True) / width
    total = jnp.zeros((n_b, n_f), F32)
    for k in range(n_k):
        shifted = inter_ref[k * n_b : (k + 1) * n_b, :] - center
        total = total + shifted * shifted
    rstd = lax.rsqrt(jnp.sum(total, 1, keepdims=True) / width + EPS)
    for k in range(n_k):
        normed = (inter_ref[k * n_b : (k + 1) * n_b, :] - center) * rstd
        inter_ref[k * n_b : (k + 1) * n_b, :] = normed
        nb_ref[:, k * n_f : (k + 1) * n_f] = normed.astype(BF)
    pre_act = mm(nb_ref[...], winp_ref[...])
    sigma = 1.0 / (1.0 + jnp.exp(-pre_act))
    hidden = (pre_act * sigma).astype(BF)
    factor = mm(hidden, wout_ref[...])
    head = head_ref[...]
    lin = ld_ref[...]
    lin1 = jnp.sum(jnp.where(row_lane1, lin, 0.0), 1, keepdims=True)
    lin2 = jnp.sum(jnp.where(row_lane1, 0.0, lin), 1, keepdims=True)
    logit = jnp.sum(factor * head, 1, keepdims=True) + jnp.concatenate([lin1, lin2], 0)
    target = label_ref[...]
    terms = jnp.maximum(logit, 0.0) + jnp.log1p(jnp.exp(-jnp.abs(logit))) - target * logit
    loss_ref[...] = jnp.broadcast_to(
        jnp.sum(jnp.broadcast_to(terms, (n_b, 128)), 0, keepdims=True), loss_ref.shape
    )
    slope = scale * (1.0 / (1.0 + jnp.exp(-logit)) - target)
    slope_ref[...] = jnp.broadcast_to(slope, (n_b, 128))
    den_ref[AT_HEAD:, :] = jnp.zeros((den_ref.shape[0] - AT_HEAD, 128), F32)
    ghead = jnp.sum(slope * factor, 0, keepdims=True)
    for i in range(ghead.shape[1] // 128):
        den_ref[AT_HEAD + i : AT_HEAD + i + 1, :] = ghead[:, i * 128 : (i + 1) * 128]
    gfactor = (slope * head).astype(BF)
    for i in range(gfactor.shape[1] // 128):
        den_ref[AT_WOUT + i * 256 : AT_WOUT + (i + 1) * 256, :] = mm(
            hidden, gfactor[:, i * 128 : (i + 1) * 128], TN
        )
    ghidden = mm(gfactor, wout_ref[...], NT)
    gpre = (ghidden * sigma * (1.0 + pre_act * (1.0 - sigma))).astype(BF)
    first = jnp.zeros((n_b, n_f), F32)
    second = jnp.zeros((n_b, n_f), F32)
    for k in range(n_k):
        feats = slice(k * n_f, (k + 1) * n_f)
        gwin = mm(nb_ref[:, feats], gpre, TN)
        den_ref[feats, :] = gwin[:, :128]
        den_ref[width + k * n_f : width + (k + 1) * n_f, :] = gwin[:, 128:]
        gnormed = mm(gpre, winp_ref[feats, :], NT)
        first = first + gnormed
        second = second + gnormed * inter_ref[k * n_b : (k + 1) * n_b, :]
    mean1 = jnp.sum(first, 1, keepdims=True) / width
    mean2 = jnp.sum(second, 1, keepdims=True) / width
    for k in range(n_k):
        feats = slice(k * n_f, (k + 1) * n_f)
        span = slice(k * n_b, (k + 1) * n_b)
        gnormed = mm(gpre, winp_ref[feats, :], NT)
        inter_ref[span, :] = rstd * (gnormed - mean1 - inter_ref[span, :] * mean2)

    for q in range(4):
        for d in range(1, n_p):
            link(y_ref, x_ref, ysend, xrecv, q, (p + d) % n_p).wait_send()
    gw_ref[...] = jnp.zeros_like(gw_ref)
    ghl_ref[...] = jnp.zeros_like(ghl_ref)

    def back_group(q, carry):
        def pair(j, inner):
            p = q * tile + j
            x3 = xp_ref[p]
            gi = jnp.concatenate(
                [
                    inter_ref[pl.ds(p, n_k, stride=n_b), :],
                    inter_ref[pl.ds(64 + p, n_k, stride=n_b), :],
                ],
                0,
            ).astype(BF)
            gc = mm(gi, x3)
            gc = jnp.where(lane1, gc[:n_k], gc[n_k:]).astype(BF)
            s1 = slope_ref[pl.ds(p, 1), :]
            s2 = slope_ref[pl.ds(64 + p, 1), :]
            srow = jnp.where(
                row_lane1,
                jnp.concatenate([s1, s1, s1], 1),
                jnp.concatenate([s2, s2, s2], 1),
            )
            gl = (srow * hpair_ref[...]).astype(BF)
            mixed = mix_ref[p]
            ghl_ref[...] += srow * mixed[n_k:]
            compact = mixed[:n_k]
            tail = jnp.concatenate([gc, gl], 0)
            right = jnp.concatenate(
                [
                    jnp.where(lane1, compact, 0.0).astype(BF),
                    jnp.where(lane1, 0.0, compact).astype(BF),
                    tail,
                ],
                0,
            )
            left = jnp.concatenate([gi, wt], 0)
            gp = mm(left, right, TN)
            gw_ref[...] += mm(tail, x3, NT)
            for part, at in ((0, 0), (2, 128), (1, 256)):
                split_ref[part, pl.ds(j, n_f, stride=tile), :] = gp[:, at : at + 128]
            return inner

        lax.fori_loop(0, tile, pair, 0, unroll=2)
        for part in range(3):
            y_ref[q, :, :, :, part * tile : (part + 1) * tile, :] = (
                split_ref[part].reshape(4, n_p, 2, tile, 128).astype(BF)
            )
        for d in range(1, n_p):
            link(y_ref, bk_ref, gsend, brecv, q, (p + d) % n_p).start()
        bk_ref[q, :, p] = y_ref[q, :, p]
        return carry

    lax.fori_loop(0, 64 // tile, back_group, 0)
    den_ref[AT_GW : AT_GW + 48, :] = gw_ref[...]
    ghl = ghl_ref[...]
    second = ghl[:, 128:256]
    lane = lax.broadcasted_iota(jnp.int32, second.shape, 1)
    den_ref[AT_LIN : AT_LIN + 32, :] = ghl[:, :128] + ghl[:, 256:]
    den_ref[AT_LIN + 32 : AT_LIN + 64, :] = jnp.where(
        lane < 64, second + pltpu.roll(second, 64, 1), 0.0
    )

    acc_ref[...] = jnp.zeros_like(acc_ref)

    def scatter(q, carry):
        for d in range(1, n_p):
            src = (p + n_p - d) % n_p
            arrived(bk_ref.at[q, :, src], brecv.at[q, src])
        for f in range(8):
            hots, mains = [], []
            rest = bk_ref[q, f // 2, :, f % 2, 2 * tile :, :].reshape(256, 128)
            turned = pltpu.roll(rest.astype(F32), 64, 1).astype(BF)
            for h, tail in ((0, rest), (1, turned)):
                first = pl.multiple_of((q * 2 + h) * 256, 256)
                row = lax.broadcasted_iota(jnp.int32, (rows, 256), 0)
                at = 2 * (f % 2)
                id0 = idz_ref[f // 2, at : at + 1, pl.ds(first, 256)]
                id1 = idz_ref[f // 2, at + 1 : at + 2, pl.ds(first, 256)]
                hot = jnp.where(row == id0, 1.0, 0.0) + jnp.where(row == id1, 1.0, 0.0)
                hots.append(hot.astype(BF))
                main = bk_ref[q, f // 2, :, f % 2, h * tile : (h + 1) * tile, :]
                mains.append(jnp.concatenate([main.reshape(256, 128), tail], 1))
            acc_ref[f] += mm(jnp.concatenate(hots, 1), jnp.concatenate(mains, 0))
        return carry

    lax.fori_loop(0, 4, scatter, 0)

    def pack(f, carry):
        part_ref[f, :rows, :] = acc_ref[f, :, :128]
        low = acc_ref[f, : rows // 2, 128:]
        high = pltpu.roll(acc_ref[f, rows // 2 :, 128:], 64, 1)
        lane = lax.broadcasted_iota(jnp.int32, low.shape, 1)
        part_ref[f, rows:, :] = jnp.where(lane < 64, low, high)
        return carry

    lax.fori_loop(0, 8, pack, 0)
    for copy in sends:
        copy.wait_send()
    for q in range(4):
        for d in range(1, n_p):
            link(y_ref, bk_ref, gsend, brecv, q, (p + d) % n_p).wait_send()


def whole(n):
    return [pl.BlockSpec(memory_space=pltpu.VMEM)] * n


def run_main(scale, ids, tab, wt, win, wout, head, hpair, label):
    rows = tab.shape[1] * 2 // 3
    blocks = (4, 4, 16, 2, 48, 128)
    dma = pltpu.SemaphoreType.DMA
    return pl.pallas_call(
        functools.partial(main_kernel, scale),
        out_shape=[
            jax.ShapeDtypeStruct((8, rows * 3 // 2, 128), F32),
            jax.ShapeDtypeStruct((DEN_ROWS, 128), F32),
            jax.ShapeDtypeStruct((8, 128), F32),
        ],
        in_specs=whole(8),
        out_specs=whole(3),
        scratch_shapes=[
            pltpu.VMEM((8, rows * 3 // 2, 128), BF),
            pltpu.VMEM(ids.shape, jnp.int32),
            pltpu.VMEM((2048, 32), jnp.int32),
            pltpu.VMEM((8, rows, 256), BF),
            pltpu.VMEM((8, rows, 256), BF),
            pltpu.VMEM(blocks, BF),
            pltpu.VMEM(blocks, BF),
            pltpu.VMEM(blocks, BF),
            pltpu.VMEM(win.shape, BF),
            pltpu.VMEM((8, rows, 256), F32),
            pltpu.VMEM((48, 128), F32),
            pltpu.VMEM((32, 384), F32),
            pltpu.VMEM((3, 128 * 16, 128), F32),
            pltpu.VMEM((64, 128, 384), BF),
            pltpu.VMEM((64, 48, 384), F32),
            pltpu.VMEM((16 * 128, 128), F32),
            pltpu.VMEM((128, 16 * 128), BF),
            pltpu.VMEM((64, 384), F32),
            pltpu.VMEM((128, 128), F32),
            dma((9,)),
            dma((4,)),
            dma((4,)),
            dma((4,)),
            dma((4, 16)),
            dma((4, 16)),
            dma((4, 16)),
            dma((4, 16)),
        ],
        compiler_params=pltpu.CompilerParams(
            vmem_limit_bytes=VMEM_LIMIT, collective_id=1, has_side_effects=True
        ),
        name="main",
    )(ids, tab, wt, win, wout, head, hpair, label)


def reduce_kernel(
    tab_ref,
    den_ref,
    loss_ref,
    out_tab_ref,
    gwin_ref,
    gwout_ref,
    gproj_ref,
    gcomp_ref,
    ghead_ref,
    glin_ref,
    out_loss_ref,
    ta_ref,
    tb_ref,
    tc_ref,
    td_ref,
    te_ref,
    da_ref,
    db_ref,
    dc_ref,
    dd_ref,
    de_ref,
    df_ref,
    la_ref,
    lb_ref,
    lc_ref,
    ls_ref,
    send_ref,
    core_sem,
    tz_sem,
    tr_sem,
    dp_sem,
    dz_sem,
    dg_sem,
    dh_sem,
    lc_sem,
    lp_sem,
    lz_sem,
):
    zh, x, y, zl, c = [lax.axis_index(name) for name in ("zh", "x", "y", "zl", "c")]
    n_y, n_z, n_p = 4, 8, 16
    z = zh * 2 + zl
    p = x * n_y + y
    other = 1 - c

    def at_plane(q):
        return (zh, q // n_y, q % n_y, zl, c)

    def at_z(v):
        return (v // 2, x, y, v % 2, c)

    sibling = (zh, x, y, zl, other)
    replicas = [sibling, (zh, x, y, 1 - zl, c), (zh, x, y, 1 - zl, other)]
    barrier = pltpu.get_barrier_semaphore()
    for d in range(1, n_p):
        pl.semaphore_signal(barrier, inc=1, device_id=at_plane((p + d) % n_p), device_id_type=MESH)
    for d in range(1, n_z):
        pl.semaphore_signal(barrier, inc=1, device_id=at_z((z + d) % n_z), device_id_type=MESH)
    for device in (replicas[0], replicas[2]):
        pl.semaphore_signal(barrier, inc=1, device_id=device, device_id_type=MESH)
    pl.semaphore_wait(barrier, n_p - 1 + n_z - 1 + 2)

    sends = []

    def send(src, dst, sem, device):
        k = len(sends)
        copy = pltpu.make_async_remote_copy(
            src_ref=src,
            dst_ref=dst,
            send_sem=send_ref.at[k],
            recv_sem=sem,
            device_id=device,
            device_id_type=MESH,
        )
        copy.start()
        sends.append(copy)

    half = DEN_ROWS // 2
    for v in range(4):
        ta_ref[v] = tab_ref[2 * v + other].astype(BF)
    send(ta_ref, tb_ref, core_sem.at[0], sibling)
    da_ref[...] = den_ref[pl.ds(pl.multiple_of(other * half, half), half), :].astype(BF)
    send(da_ref, db_ref, core_sem.at[1], sibling)
    send(loss_ref, lc_ref, lc_sem, sibling)

    arrived(tb_ref, core_sem.at[0])
    for v in range(4):
        mine = tab_ref[2 * v + c] + tb_ref[v].astype(F32)
        tc_ref[2 * v] = mine[:384].astype(BF)
        tc_ref[2 * v + 1] = mine[384:].astype(BF)
    for d in range(1, n_z):
        to = (z + d) % n_z
        send(tc_ref.at[to], td_ref.at[z], tz_sem.at[z], at_z(to))

    chunk = half // n_p
    arrived(db_ref, core_sem.at[1])
    for i in range(n_p):
        rows = pl.ds(pl.multiple_of(c * half + i * chunk, chunk), chunk)
        dc_ref[i] = (
            den_ref[rows, :] + db_ref[i * chunk : (i + 1) * chunk, :].astype(F32)
        ).astype(BF)
    for d in range(1, n_p):
        to = (p + d) % n_p
        send(dc_ref.at[to], dd_ref.at[p], dp_sem.at[p], at_plane(to))
    arrived(lc_ref, lc_sem)
    loss = loss_ref[...] + lc_ref[...]
    ls_ref[0] = loss
    for d in range(1, n_p):
        to = (p + d) % n_p
        send(ls_ref.at[0], la_ref.at[p], lp_sem.at[p], at_plane(to))
    la_ref[p] = loss

    own = dc_ref[p].astype(F32)
    for d in range(1, n_p):
        q = (p + d) % n_p
        arrived(dd_ref.at[q], dp_sem.at[q])
        own = own + dd_ref[q].astype(F32)
    de_ref[z] = own.astype(BF)
    for d in range(1, n_z):
        send(de_ref.at[z], de_ref.at[z], dz_sem.at[z], at_z((z + d) % n_z))
    for d in range(1, n_p):
        q = (p + d) % n_p
        arrived(la_ref.at[q], lp_sem.at[q])
    loss = la_ref[0]
    for q in range(1, n_p):
        loss = loss + la_ref[q]
    ls_ref[1] = loss
    for d in range(1, n_z):
        send(ls_ref.at[1], lb_ref.at[z], lz_sem.at[z], at_z((z + d) % n_z))
    lb_ref[z] = loss

    own = tc_ref[z].astype(F32)
    for d in range(1, n_z):
        v = (z + d) % n_z
        arrived(td_ref.at[v], tz_sem.at[v])
        own = own + td_ref[v].astype(F32)
    te_ref[2 * c + zl] = own.astype(BF)
    for device in replicas:
        send(te_ref.at[2 * c + zl], te_ref.at[2 * c + zl], tr_sem.at[2 * c + zl], device)

    for d in range(1, n_z):
        v = (z + d) % n_z
        arrived(de_ref.at[v], dz_sem.at[v])
    own = de_ref[0].astype(F32)
    for v in range(1, n_z):
        own = own + de_ref[v].astype(F32)
    mine = c * n_p + p
    df_ref[mine] = own.astype(BF)
    for d in range(1, n_p):
        send(df_ref.at[mine], df_ref.at[mine], dg_sem.at[p], at_plane((p + d) % n_p))
    send(df_ref.at[mine], df_ref.at[mine], dh_sem.at[p], sibling)

    for d in range(1, 4):
        k = (2 * c + zl + d) % 4
        arrived(te_ref.at[k], tr_sem.at[k])
    n_rows = out_tab_ref.shape[1]
    for j in range(2):
        low, high = te_ref[2 * j].astype(F32), te_ref[2 * j + 1].astype(F32)
        out_tab_ref[j, :384, :128] = low
        out_tab_ref[j, 384:n_rows, :128] = high[: n_rows - 384]
        rest = high[n_rows - 384 :]
        out_tab_ref[j, : n_rows // 2, 128:192] = rest[:, :64]
        out_tab_ref[j, n_rows // 2 :, 128:192] = pltpu.roll(rest, 64, 1)[:, :64]

    for d in range(1, n_z):
        v = (z + d) % n_z
        arrived(lb_ref.at[v], lz_sem.at[v])
    loss = lb_ref[0]
    for v in range(1, n_z):
        loss = loss + lb_ref[v]
    out_loss_ref[...] = loss

    for d in range(1, n_p):
        q = (p + d) % n_p
        arrived(df_ref.at[c * n_p + q], dg_sem.at[q])
        send(df_ref.at[c * n_p + q], df_ref.at[c * n_p + q], dh_sem.at[q], sibling)
    for q in range(n_p):
        arrived(df_ref.at[other * n_p + q], dh_sem.at[q])

    def final(first, count):
        pieces = []
        at = first
        while at < first + count:
            i, r = at // chunk, at % chunk
            n = min(chunk - r, first + count - at)
            pieces.append(df_ref[i, r : r + n, :].astype(F32))
            at += n
        return pieces[0] if len(pieces) == 1 else jnp.concatenate(pieces, 0)

    for side in range(2):
        for k in range(16):
            gwin_ref[side, pl.ds(k, 128, stride=16), :] = final(side * 2048 + k * 128, 128)
    for i in range(6):
        gwout_ref[:, i * 128 : (i + 1) * 128] = final(AT_WOUT + i * 256, 256)
    gproj_ref[...] = final(AT_GW, 16).T
    gcomp_ref[...] = final(AT_GW + 16, 32)
    glin_ref[:, :128] = final(AT_LIN, 32)
    glin_ref[:, 128:192] = final(AT_LIN + 32, 32)[:, :64]
    ghead_ref[...] = final(AT_HEAD, 16)
    for copy in sends:
        copy.wait_send()


def reduce_all(tab, den, loss, rows):
    half = DEN_ROWS // 2
    chunk = half // 16
    dma = pltpu.SemaphoreType.DMA
    return pl.pallas_call(
        reduce_kernel,
        out_shape=[
            jax.ShapeDtypeStruct((2, rows, 192), F32),
            jax.ShapeDtypeStruct((2, 2048, 128), F32),
            jax.ShapeDtypeStruct((256, 768), F32),
            jax.ShapeDtypeStruct((128, 16), F32),
            jax.ShapeDtypeStruct((32, 128), F32),
            jax.ShapeDtypeStruct((16, 128), F32),
            jax.ShapeDtypeStruct((32, 192), F32),
            jax.ShapeDtypeStruct(loss.shape, F32),
        ],
        in_specs=whole(3),
        out_specs=whole(8),
        scratch_shapes=[
            pltpu.VMEM((4, 768, 128), BF),
            pltpu.VMEM((4, 768, 128), BF),
            pltpu.VMEM((8, 384, 128), BF),
            pltpu.VMEM((8, 384, 128), BF),
            pltpu.VMEM((4, 384, 128), BF),
            pltpu.VMEM((half, 128), BF),
            pltpu.VMEM((half, 128), BF),
            pltpu.VMEM((16, chunk, 128), BF),
            pltpu.VMEM((16, chunk, 128), BF),
            pltpu.VMEM((8, chunk, 128), BF),
            pltpu.VMEM((32, chunk, 128), BF),
            pltpu.VMEM((16, 8, 128), F32),
            pltpu.VMEM((8, 8, 128), F32),
            pltpu.VMEM((8, 128), F32),
            pltpu.VMEM((2, 8, 128), F32),
            dma((96,)),
            dma((2,)),
            dma((8,)),
            dma((4,)),
            dma((16,)),
            dma((8,)),
            dma((16,)),
            dma((16,)),
            dma,
            dma((16,)),
            dma((8,)),
        ],
        compiler_params=pltpu.CompilerParams(
            vmem_limit_bytes=VMEM_LIMIT, collective_id=0, has_side_effects=True
        ),
        name="reduce",
    )(tab, den, loss)


def pack_tables(t):
    half = t.shape[1] // 2
    rest = jnp.concatenate([t[:, :half, 128:], t[:, half:, 128:]], 2)
    return jnp.concatenate([t[:, :, :128], rest], 1)


def order_ids(feature_ids, bag_lengths, rows):
    ids = feature_ids[:, 0].transpose(1, 2, 0)
    lens = bag_lengths[:, 0].T
    slots = jnp.arange(ids.shape[1], dtype=jnp.int32)[None, :, None]
    ids = jnp.where(lens[:, None, :] > slots, ids, rows)
    ids = ids.reshape(4, 4, 16, 2, 4, 16).transpose(1, 0, 4, 3, 2, 5).reshape(4, 4, 2048)
    return jnp.pad(ids, ((0, 0), (0, 4), (0, 0)))


def pair_head(w_head, n_out):
    lin = w_head[n_out:].astype(F32).reshape(-1, 192)
    return jnp.concatenate([lin, lin[:, 128:], lin[:, :128]], 1)


def per_device(
    feature_ids, bag_lengths, click_labels, tables, projection, compress, w_in, w_out, w_head
):
    rows = tables.shape[1]
    n_out = w_out.shape[1]
    total = feature_ids.shape[0] * lax.axis_size("zl") * lax.axis_size("c")
    scale = 1.0 / math.sqrt(total)
    ids = order_ids(feature_ids, bag_lengths, rows)
    wt = jnp.concatenate([projection.T, compress], 0)
    head = w_head[:n_out].astype(F32)[None, :]
    hpair = pair_head(w_head, n_out)
    label = click_labels.astype(F32)
    partial, den, loss = run_main(
        scale, ids, pack_tables(tables), wt, w_in, w_out, head, hpair, label
    )
    table_grad, gwin, gwout, gproj, gcomp, ghead, glin, loss = reduce_all(
        partial, den, loss, rows
    )
    gwin = jnp.concatenate([gwin[0], gwin[1]], 1)
    ghead = jnp.concatenate([ghead[: n_out // 128].reshape(-1), glin.reshape(-1)])
    return (loss[0, 0] / total, gproj, gcomp, gwin, gwout, ghead, table_grad)


def solution(mesh):
    fine = Mesh(mesh.devices.reshape(4, 4, 4, 2, 2), ("zh", "x", "y", "zl", "c"))
    emb = ("zh", "x", "y")
    rep = ("zl", "c")
    placed = (
        P(None, rep, emb, None),
        P(None, rep, emb),
        P(emb, rep),
        P(emb, None, None),
        P(),
        P(),
        P(),
        P(),
        P(),
    )
    return jax.shard_map(
        per_device,
        mesh=fine,
        in_specs=placed,
        out_specs=(P(), P(), P(), P(), P(), P(), P(emb, None, None)),
        check_vma=False,
    )
```

```python
import functools
import math

import jax
import jax.numpy as jnp
import numpy as np
from jax import lax
from jax.experimental import pallas as pl
from jax.experimental.pallas import tpu as pltpu
from jax.sharding import Mesh, PartitionSpec as P

EPS = 1e-05
BF = jnp.bfloat16
F32 = jnp.float32
NT = (((1,), (1,)), ((), ()))
TN = (((0,), (0,)), ((), ()))
VMEM_LIMIT = 60 * 1024 * 1024
MESH = pl.DeviceIdType.MESH
AT_WOUT = 4096
AT_GW = AT_WOUT + 1536
AT_LIN = AT_GW + 48
AT_HEAD = AT_LIN + 64
DEN_ROWS = 6144


def mm(a, b, dims=None):
    if dims is None:
        return jnp.dot(a, b, preferred_element_type=F32)
    return lax.dot_general(a, b, dims, preferred_element_type=F32)


def arrived(dst, sem):
    pltpu.make_async_copy(dst, dst, sem).wait()


def step_kernel(
    scale,
    ids_ref,
    tab_ref,
    perm_ref,
    wtn_ref,
    win_ref,
    wout_ref,
    head_ref,
    hpair_ref,
    label_ref,
    out_tab_ref,
    gwin_ref,
    gwout_ref,
    gproj_ref,
    gcomp_ref,
    ghead_ref,
    glin_ref,
    out_loss_ref,
    tz_ref,
    idt_ref,
    col_ref,
    y_ref,
    x_ref,
    winp_ref,
    den_ref,
    gw_ref,
    split_ref,
    xp_ref,
    mix_ref,
    inter_ref,
    nb_ref,
    ld_ref,
    slope_ref,
    da_ref,
    db_ref,
    dc_ref,
    dd_ref,
    de_ref,
    df_ref,
    te_ref,
    tf_ref,
    tr_ref,
    sa_ref,
    sb_ref,
    sp_ref,
    sz_ref,
    asend,
    arecv,
    irecv,
    ysend,
    xrecv,
    gsend,
    grecv,
    free_sem,
    core_sem,
    dsend,
    dp_sem,
    dz_sem,
    dg_sem,
    dh_sem,
    t1send,
    t1recv,
    t2send,
    t2recv,
    t3send,
    t3recv,
    t4send,
    t4recv,
    ssend,
    sc_sem,
    sp_sem,
    sz_sem,
):
    zh, px, py, zl, c = [lax.axis_index(name) for name in ("zh", "x", "y", "zl", "c")]
    n_p, n_z = 16, 8
    z = zh * 2 + zl
    p = px * 4 + py
    other = 1 - c
    sibling = (zh, px, py, zl, other)
    n_f, n_b, n_k, tile = 128, 128, 16, 16
    rows = 512
    low, high, rest_rows = slice(0, 256), slice(256, 512), slice(512, 768)
    width = n_k * n_f
    half = DEN_ROWS // 2
    chunk = half // n_p
    o = py * other + px * c
    o_other = px * other + py * c

    def at_plane(q):
        return (zh, q // 4, q % 4, zl, c)

    def at_z(v):
        return (v // 2, px, py, v % 2, c)

    def along(d):
        return (zh, (px + d * c) % 4, (py + d * other) % 4, zl, c)

    def in_row(s, d):
        if s == 0:
            return (px + d) % 4, (zh, (px + d) % 4, py, zl, c)
        return (py + d) % 4, (zh, px, (py + d) % 4, zl, c)

    def remote(src, dst, send_sem, recv_sem, device):
        return pltpu.make_async_remote_copy(
            src_ref=src,
            dst_ref=dst,
            send_sem=send_sem,
            recv_sem=recv_sem,
            device_id=device,
            device_id_type=MESH,
        )

    barrier = pltpu.get_barrier_semaphore()
    partners = [sibling, (zh, px, py, 1 - zl, other)]
    partners += [at_plane((p + d) % n_p) for d in range(1, n_p)]
    partners += [at_z((z + d) % n_z) for d in range(1, n_z)]
    for dz in range(1, 4):
        for d in range(1, 4):
            partners.append(((zh + dz) % 4, px, (py + d) % 4, zl, c))
            partners.append(((zh + dz) % 4, (px + d) % 4, py, zl, c))
    for device in partners:
        pl.semaphore_signal(barrier, inc=1, device_id=device, device_id_type=MESH)
    pl.semaphore_wait(barrier, len(partners))

    sends = []

    def send(src, dst, sem, device):
        copy = remote(src, dst, asend.at[len(sends)], sem, device)
        copy.start()
        sends.append(copy)

    def send_table(at, device):
        send(tz_ref.at[at], tz_ref.at[at], arecv.at[at], device)

    mine = c * 16 + zh * 4 + o
    tz_ref[mine] = tab_ref[c]
    tz_ref[other * 16 + zh * 4 + o_other] = tab_ref[other]
    near = (zh + 3 + 2 * zl) % 4
    for to, lo in ((near, 0), (near, 1), ((zh + 2) % 4, 1 - zl)):
        send_table(mine, (to, px, py, lo, c))
    for d in range(1, 4):
        send_table(mine, along(d))
    for dz in range(4):
        for d in range(4):
            if dz == 0 and d == 0:
                continue
            to = (zh + dz) % 4
            ty, tx = (py + d) % 4, (px + d) % 4
            send(
                ids_ref.at[0, to * 4 + ty],
                idt_ref.at[0, zh * 4 + py],
                irecv.at[0, zh * 4 + py],
                (to, px, ty, zl, c),
            )
            send(
                ids_ref.at[1, to * 4 + tx],
                idt_ref.at[1, zh * 4 + px],
                irecv.at[1, zh * 4 + px],
                (to, tx, py, zl, c),
            )
    idt_ref[0, zh * 4 + py] = ids_ref[0, zh * 4 + py]
    idt_ref[1, zh * 4 + px] = ids_ref[1, zh * 4 + px]
    for dz in (1, 3, 2):
        at = c * 16 + (zh + dz) % 4 * 4 + o
        arrived(tz_ref.at[at], arecv.at[at])
        for d in range(1, 4):
            send_table(at, along(d))
        send_table(at, sibling)

    perm = perm_ref[...]
    wt = mm(wtn_ref[...], perm).astype(BF)
    for side in range(2):
        cols = slice(side * 128, (side + 1) * 128)
        split_ref[side] = win_ref[:, cols].astype(F32)
        for k in range(n_k):
            block = split_ref[side, pl.ds(k, n_f, stride=n_k), :].astype(BF)
            winp_ref[k * n_f : (k + 1) * n_f, cols] = mm(perm, block, TN).astype(BF)

    for dz in (0, 1, 3, 2):
        for d in (1, 3, 2):
            at = c * 16 + (zh + dz) % 4 * 4 + (o + d) % 4
            arrived(tz_ref.at[at], arecv.at[at])
            send_table(at, sibling)
    for dz in range(4):
        for d in range(4):
            if dz == 0 and d == 0:
                continue
            v = (zh + dz) % 4 * 4
            for s, own in ((0, py), (1, px)):
                at = v + (own + d) % 4
                arrived(idt_ref.at[s, at], irecv.at[s, at])
    for s in range(2):
        col_ref[s] = idt_ref[s].reshape(128, 128).T
    for dz in (0, 1, 3, 2):
        for d in range(4):
            if dz == 0 and d == 0:
                continue
            at = other * 16 + (zh + dz) % 4 * 4 + (o_other + d) % 4
            arrived(tz_ref.at[at], arecv.at[at])

    def row_copy(q, s, d, send_sems, recv_sems):
        to, device = in_row(s, d)
        here = py if s else px
        return remote(
            y_ref.at[q, s, to],
            x_ref.at[q, s, here],
            send_sems.at[q, s, to],
            recv_sems.at[q, s, here],
            device,
        )

    def keep_own(q):
        x_ref[q, 0, px] = y_ref[q, 0, px]
        x_ref[q, 1, py] = y_ref[q, 1, py]

    def row_arrived(q, recv_sems):
        for s in range(2):
            for d in (1, 3, 2):
                src = in_row(s, d)[0]
                arrived(x_ref.at[q, s, src], recv_sems.at[q, s, src])

    def lookup(q, carry):
        def one_set(s, inner):
            cols = col_ref[s, pl.ds(pl.multiple_of(q * 32, 32), 32), :]
            lane = lax.broadcasted_iota(jnp.int32, (128, rows), 1)
            first = lax.broadcasted_iota(jnp.int32, (4, tile, 128), 2) < 64
            for i in range(16):
                hot = jnp.zeros((128, rows), F32)
                for slot in range(2):
                    at = i * 8 + slot * 4
                    ids = jnp.concatenate([cols[:, at + k : at + k + 1] for k in range(4)], 0)
                    hot = hot + jnp.where(lane == ids, 1.0, 0.0)
                hot = hot.astype(BF)
                f = s * 16 + i
                rest = tz_ref[f, rest_rows, :]
                one = mm(hot[:, low], jnp.concatenate([tz_ref[f, low, :], rest], 1))
                two = mm(hot[:, high], jnp.concatenate([tz_ref[f, high, :], rest], 1))
                main = one[:, :128] + two[:, :128]
                y_ref[q, s, :, i, : 2 * tile, :] = main.astype(BF).reshape(4, 2 * tile, 128)
                one, two = [v[:, 128:].reshape(4, 2, tile, 128) for v in (one, two)]

                def turn(v):
                    return pltpu.roll(v.reshape(64, 128), 64, 1).reshape(4, tile, 128)

                tail = jnp.where(
                    first, one[:, 0] + turn(two[:, 0]), turn(one[:, 1]) + two[:, 1]
                )
                y_ref[q, s, :, i, 2 * tile :, :] = tail.astype(BF)
            return inner

        lax.fori_loop(0, 2, one_set, 0)
        for d in (1, 3, 2):
            for s in range(2):
                row_copy(q, s, d, ysend, xrecv).start()
        keep_own(q)
        return carry

    lax.fori_loop(0, 4, lookup, 0)
    for copy in sends:
        copy.wait_send()

    lane1 = lax.broadcasted_iota(jnp.int32, (n_k, 384), 1) < 192
    row_lane1 = lax.broadcasted_iota(jnp.int32, (1, 384), 1) < 192

    def load_group(q, carry):
        row_arrived(q, xrecv)
        for part in range(3):
            block = x_ref[q, :, :, :, part * tile : (part + 1) * tile, :]
            split_ref[part] = block.astype(F32).reshape(n_f * tile, 128)

        def pair(j, inner):
            p = q * tile + j
            pieces = [
                split_ref[part, pl.ds(j, n_f, stride=tile), :].astype(BF) for part in (0, 2, 1)
            ]
            x3 = jnp.concatenate(pieces, 1)
            for part in range(3):
                first = pl.multiple_of(p % 2 * 384 + part * 128, 128)
                xp_ref[p // 2, pl.ds(first, 128), :] = pieces[part]
            mixed = mm(wt, x3)
            mix_ref[p] = mixed
            compact = mixed[:n_k]
            stacked = jnp.concatenate(
                [jnp.where(lane1, compact, 0.0), jnp.where(lane1, 0.0, compact)], 0
            ).astype(BF)
            inter = mm(stacked, x3, NT)
            inter_ref[pl.ds(p, n_k, stride=n_b), :] = inter[:n_k]
            inter_ref[pl.ds(64 + p, n_k, stride=n_b), :] = inter[n_k:]
            ld_ref[pl.ds(p, 1), :] = jnp.sum(mixed[n_k:] * hpair_ref[...], 0, keepdims=True)
            return inner

        lax.fori_loop(0, tile, pair, 0, unroll=2)
        return carry

    lax.fori_loop(0, 64 // tile, load_group, 0)

    for s in range(2):
        for d in range(1, 4):
            pl.semaphore_signal(
                free_sem, inc=1, device_id=in_row(s, d)[1], device_id_type=MESH
            )

    total = jnp.zeros((n_b, n_f), F32)
    for k in range(n_k):
        total = total + inter_ref[k * n_b : (k + 1) * n_b, :]
    center = jnp.sum(total, 1, keepdims=True) / width
    total = jnp.zeros((n_b, n_f), F32)
    for k in range(n_k):
        shifted = inter_ref[k * n_b : (k + 1) * n_b, :] - center
        total = total + shifted * shifted
    rstd = lax.rsqrt(jnp.sum(total, 1, keepdims=True) / width + EPS)
    for k in range(n_k):
        normed = (inter_ref[k * n_b : (k + 1) * n_b, :] - center) * rstd
        inter_ref[k * n_b : (k + 1) * n_b, :] = normed
        nb_ref[:, k * n_f : (k + 1) * n_f] = normed.astype(BF)
    pre_act = mm(nb_ref[...], winp_ref[...])
    sigma = 1.0 / (1.0 + jnp.exp(-pre_act))
    hidden = (pre_act * sigma).astype(BF)
    factor = mm(hidden, wout_ref[...])
    head = head_ref[...]
    lin = ld_ref[...]
    lin1 = jnp.sum(jnp.where(row_lane1, lin, 0.0), 1, keepdims=True)
    lin2 = jnp.sum(jnp.where(row_lane1, 0.0, lin), 1, keepdims=True)
    logit = jnp.sum(factor * head, 1, keepdims=True) + jnp.concatenate([lin1, lin2], 0)
    target = label_ref[...]
    terms = jnp.maximum(logit, 0.0) + jnp.log1p(jnp.exp(-jnp.abs(logit))) - target * logit
    sa_ref[48:, :] = jnp.broadcast_to(
        jnp.sum(jnp.broadcast_to(terms, (n_b, 128)), 0, keepdims=True), (8, 128)
    )
    slope = scale * (1.0 / (1.0 + jnp.exp(-logit)) - target)
    slope_ref[...] = jnp.broadcast_to(slope, (n_b, 128))
    den_ref[AT_HEAD:, :] = jnp.zeros((den_ref.shape[0] - AT_HEAD, 128), F32)
    ghead = jnp.sum(slope * factor, 0, keepdims=True)
    for i in range(ghead.shape[1] // 128):
        den_ref[AT_HEAD + i : AT_HEAD + i + 1, :] = ghead[:, i * 128 : (i + 1) * 128]
    gfactor = (slope * head).astype(BF)
    for i in range(gfactor.shape[1] // 128):
        den_ref[AT_WOUT + i * 256 : AT_WOUT + (i + 1) * 256, :] = mm(
            hidden, gfactor[:, i * 128 : (i + 1) * 128], TN
        )
    ghidden = mm(gfactor, wout_ref[...], NT)
    gpre = (ghidden * sigma * (1.0 + pre_act * (1.0 - sigma))).astype(BF)
    first = jnp.zeros((n_b, n_f), F32)
    second = jnp.zeros((n_b, n_f), F32)
    for k in range(n_k):
        feats = slice(k * n_f, (k + 1) * n_f)
        gwin = mm(nb_ref[:, feats], gpre, TN)
        den_ref[feats, :] = gwin[:, :128]
        den_ref[width + k * n_f : width + (k + 1) * n_f, :] = gwin[:, 128:]
        gnormed = mm(gpre, winp_ref[feats, :], NT)
        first = first + gnormed
        second = second + gnormed * inter_ref[k * n_b : (k + 1) * n_b, :]
    mean1 = jnp.sum(first, 1, keepdims=True) / width
    mean2 = jnp.sum(second, 1, keepdims=True) / width
    for k in range(n_k):
        feats = slice(k * n_f, (k + 1) * n_f)
        span = slice(k * n_b, (k + 1) * n_b)
        gnormed = mm(gpre, winp_ref[feats, :], NT)
        inter_ref[span, :] = rstd * (gnormed - mean1 - inter_ref[span, :] * mean2)

    def slope_row(p):
        s1 = slope_ref[pl.ds(p, 1), :]
        s2 = slope_ref[pl.ds(64 + p, 1), :]
        return jnp.where(
            row_lane1,
            jnp.concatenate([s1, s1, s1], 1),
            jnp.concatenate([s2, s2, s2], 1),
        )

    ghl = lax.fori_loop(
        0,
        64,
        lambda p, sum: sum + slope_row(p) * mix_ref[p, n_k:, :],
        jnp.zeros((32, 384), F32),
        unroll=4,
    )
    second = ghl[:, 128:256]
    lane = lax.broadcasted_iota(jnp.int32, second.shape, 1)
    den_ref[AT_LIN : AT_LIN + 32, :] = ghl[:, :128] + ghl[:, 256:]
    den_ref[AT_LIN + 32 : AT_LIN + 64, :] = jnp.where(
        lane < 64, second + pltpu.roll(second, 64, 1), 0.0
    )
    den_ref[AT_GW:AT_LIN, :] = jnp.zeros((AT_LIN - AT_GW, 128), F32)
    gw_ref[...] = jnp.zeros_like(gw_ref)

    def dense_core():
        return remote(da_ref, db_ref, dsend.at[0], core_sem, sibling)

    def dense_plane(d):
        to = (p + d) % n_p
        return remote(
            dc_ref.at[to], dd_ref.at[p], dsend.at[d], dp_sem.at[p], at_plane(to)
        )

    def dense_z(d):
        return remote(
            de_ref.at[z], de_ref.at[z], dsend.at[15 + d], dz_sem.at[z], at_z((z + d) % n_z)
        )

    def dense_gather(d):
        at = c * n_p + p
        return remote(
            df_ref.at[at],
            df_ref.at[at],
            dsend.at[22 + d],
            dg_sem.at[p],
            at_plane((p + d) % n_p),
        )

    def dense_last(d):
        q = (p + d) % n_p
        at = c * n_p + q
        return remote(df_ref.at[at], df_ref.at[at], dsend.at[38 + d], dh_sem.at[q], sibling)

    def dense_step1():
        arrived(db_ref, core_sem)

        def add(i, carry):
            at = pl.multiple_of(i * chunk, chunk)
            mine = den_ref[pl.ds(pl.multiple_of(c * half + i * chunk, chunk), chunk), :]
            dc_ref[i] = (mine + db_ref[pl.ds(at, chunk), :].astype(F32)).astype(BF)
            return carry

        lax.fori_loop(0, n_p, add, 0)
        for d in range(1, n_p):
            dense_plane(d).start()

    def dense_step2():
        own = dc_ref[p].astype(F32)
        for d in range(1, n_p):
            q = (p + d) % n_p
            arrived(dd_ref.at[q], dp_sem.at[q])
            own = own + dd_ref[q].astype(F32)
        de_ref[z] = own.astype(BF)
        for d in range(1, n_z):
            dense_z(d).start()

    def dense_step3():
        for d in range(1, n_z):
            v = (z + d) % n_z
            arrived(de_ref.at[v], dz_sem.at[v])
        own = de_ref[0].astype(F32)
        for v in range(1, n_z):
            own = own + de_ref[v].astype(F32)
        df_ref[c * n_p + p] = own.astype(BF)
        for d in range(1, n_p):
            dense_gather(d).start()
        dense_last(0).start()

    da_ref[...] = den_ref[pl.ds(pl.multiple_of(other * half, half), half), :].astype(BF)
    dense_core().start()
    for q in range(4):
        for s in range(2):
            for d in range(1, 4):
                row_copy(q, s, d, ysend, xrecv).wait_send()
    pl.semaphore_wait(free_sem, 6)

    def back_group(q, carry):
        pl.when(q == 1)(dense_step1)
        pl.when(q == 2)(dense_step2)
        pl.when(q == 3)(dense_step3)

        def pair(j, inner):
            p = q * tile + j
            x3 = jnp.concatenate(
                [
                    xp_ref[p // 2, pl.ds(pl.multiple_of(p % 2 * 384 + part * 128, 128), 128), :]
                    for part in range(3)
                ],
                1,
            )
            gi = jnp.concatenate(
                [
                    inter_ref[pl.ds(p, n_k, stride=n_b), :],
                    inter_ref[pl.ds(64 + p, n_k, stride=n_b), :],
                ],
                0,
            ).astype(BF)
            gc = mm(gi, x3)
            gc = jnp.where(lane1, gc[:n_k], gc[n_k:]).astype(BF)
            srow = slope_row(p)
            gl = (srow * hpair_ref[...]).astype(BF)
            compact = mix_ref[p, :n_k, :]
            tail = jnp.concatenate([gc, gl], 0)
            right = jnp.concatenate(
                [
                    jnp.where(lane1, compact, 0.0).astype(BF),
                    jnp.where(lane1, 0.0, compact).astype(BF),
                    tail,
                ],
                0,
            )
            left = jnp.concatenate([gi, wt], 0)
            gp = mm(left, right, TN)
            gw_ref[...] += mm(tail, x3, NT)
            for part, at in ((0, 0), (2, 128), (1, 256)):
                split_ref[part, pl.ds(j, n_f, stride=tile), :] = gp[:, at : at + 128]
            return inner

        lax.fori_loop(0, tile, pair, 0, unroll=2)
        for part in range(3):
            y_ref[q, :, :, :, part * tile : (part + 1) * tile, :] = (
                split_ref[part].reshape(2, 4, 16, tile, 128).astype(BF)
            )
        for d in (1, 3, 2):
            for s in range(2):
                row_copy(q, s, d, gsend, grecv).start()
        keep_own(q)
        return carry

    lax.fori_loop(0, 64 // tile, back_group, 0)

    def small_core():
        return remote(sa_ref, sb_ref, ssend.at[0], sc_sem, sibling)

    def small_plane(d):
        return remote(
            sp_ref.at[p], sp_ref.at[p], ssend.at[d], sp_sem.at[p], at_plane((p + d) % n_p)
        )

    def small_z(d):
        return remote(
            sz_ref.at[z], sz_ref.at[z], ssend.at[15 + d], sz_sem.at[z], at_z((z + d) % n_z)
        )

    sa_ref[:48, :] = gw_ref[...]
    small_core().start()

    def table_grad(s, i):
        hots, mains, rests = [], [], []
        row = lax.broadcasted_iota(jnp.int32, (rows, 128), 0)
        for src in range(4):
            hot = jnp.zeros((rows, 128), F32)
            for slot in range(2):
                ids = idt_ref[s, i, slot * 4 + src : slot * 4 + src + 1, :]
                hot = hot + jnp.where(row == ids, 1.0, 0.0)
            hots.append(hot.astype(BF))
            for q in range(4):
                mains.append(x_ref[q, s, src, i, : 2 * tile, :])
                rests.append(x_ref[q, s, src, i, 2 * tile :, :])
        turned = pltpu.roll(jnp.concatenate(rests, 0).astype(F32), 64, 1).astype(BF)
        tails = []
        for k, rest in enumerate(rests):
            tails += [rest, turned[k * tile : (k + 1) * tile]]
        right = jnp.concatenate([jnp.concatenate(mains, 0), jnp.concatenate(tails, 0)], 1)
        sums = mm(jnp.concatenate(hots, 1), right)
        lane = lax.broadcasted_iota(jnp.int32, (256, 128), 1)
        tail = jnp.where(lane < 64, sums[low, 128:], pltpu.roll(sums[high, 128:], 64, 1))
        return sums[:, :128], tail

    def table_core(i):
        return remote(
            tz_ref.at[16 + i], tz_ref.at[i], t1send.at[i], t1recv.at[i], sibling
        )

    def table_along(d, v):
        return remote(
            xp_ref.at[v * 4 + (o + d) % 4],
            xp_ref.at[16 + o * 4 + v],
            t2send.at[d * 4 + v],
            t2recv.at[o * 4 + v],
            along(d),
        )

    def table_z(d):
        to = (z + d) % n_z
        return remote(te_ref.at[to], tf_ref.at[z], t3send.at[d], t3recv.at[z], at_z(to))

    own_slot = 2 * c + zl

    def table_replica(k):
        device = (sibling, (zh, px, py, 1 - zl, c), (zh, px, py, 1 - zl, other))[k]
        return remote(
            tr_ref.at[own_slot], tr_ref.at[own_slot], t4send.at[k], t4recv.at[own_slot], device
        )

    for q in range(4):
        row_arrived(q, grecv)

    def for_sibling(n, carry):
        i = (n % 4) * 4 + (o_other + 1 + n // 4) % 4
        main, tail = table_grad(other, i)
        tz_ref[16 + i, :rows, :] = main.astype(BF)
        tz_ref[16 + i, rest_rows, :] = tail.astype(BF)
        table_core(i).start()
        return carry

    lax.fori_loop(0, 16, for_sibling, 0)

    arrived(sb_ref, sc_sem)
    sp_ref[p] = sa_ref[...] + sb_ref[...]
    for d in range(1, n_p):
        small_plane(d).start()

    def for_chip(n, carry):
        d, v = n // 4 + 1, n % 4
        i = v * 4 + (o + d) % 4
        main, tail = table_grad(c, i)
        arrived(tz_ref.at[i], t1recv.at[i])
        xp_ref[i, :rows, :] = (main + tz_ref[i, :rows, :].astype(F32)).astype(BF)
        xp_ref[i, rest_rows, :] = (tail + tz_ref[i, rest_rows, :].astype(F32)).astype(BF)

        @pl.when(d < 4)
        def _():
            table_along(d, v).start()

        return carry

    lax.fori_loop(0, 16, for_chip, 0)

    for d in range(1, n_p):
        q = (p + d) % n_p
        arrived(df_ref.at[c * n_p + q], dg_sem.at[q])
        dense_last(d).start()
    for d in range(1, n_p):
        q = (p + d) % n_p
        arrived(sp_ref.at[q], sp_sem.at[q])
    small = sp_ref[0]
    for q in range(1, n_p):
        small = small + sp_ref[q]
    sz_ref[z] = small
    for d in range(1, n_z):
        small_z(d).start()

    for d in range(1, 4):
        for v in range(4):
            at = (o + d) % 4 * 4 + v
            arrived(xp_ref.at[16 + at], t2recv.at[at])
    own = None
    for d in (1, 7, 2, 6, 3, 5, 4, 0):
        to = (z + d) % n_z
        span = pl.ds(pl.multiple_of(to % 2 * 384, 384), 384)
        own = xp_ref[to // 2 * 4 + o, span, :].astype(F32)
        for k in range(1, 4):
            own = own + xp_ref[16 + (o + k) % 4 * 4 + to // 2, span, :].astype(F32)
        if d > 0:
            te_ref[to] = own.astype(BF)
            table_z(d).start()

    for q in range(n_p):
        arrived(df_ref.at[other * n_p + q], dh_sem.at[q])

    def final(first, count):
        pieces = []
        at = first
        while at < first + count:
            i, r = at // chunk, at % chunk
            n = min(chunk - r, first + count - at)
            pieces.append(df_ref[i, r : r + n, :])
            at += n
        return pieces[0] if len(pieces) == 1 else jnp.concatenate(pieces, 0)

    for side in range(2):
        for k in range(n_k):
            block = final(side * 2048 + k * 128, 128)
            gwin_ref[side, pl.ds(k, n_f, stride=n_k), :] = mm(perm, block)
    for i in range(6):
        gwout_ref[:, i * 128 : (i + 1) * 128] = final(AT_WOUT + i * 256, 256).astype(F32)
    glin_ref[:, :128] = final(AT_LIN, 32).astype(F32)
    glin_ref[:, 128:192] = final(AT_LIN + 32, 32).astype(F32)[:, :64]
    ghead_ref[...] = final(AT_HEAD, 16).astype(F32)

    for d in range(1, n_z):
        v = (z + d) % n_z
        arrived(tf_ref.at[v], t3recv.at[v])
        own = own + tf_ref[v].astype(F32)
    tr_ref[own_slot] = own.astype(BF)
    for k in range(3):
        table_replica(k).start()

    for d in range(1, n_z):
        v = (z + d) % n_z
        arrived(sz_ref.at[v], sz_sem.at[v])
    small = sz_ref[0]
    for v in range(1, n_z):
        small = small + sz_ref[v]
    out_loss_ref[...] = small[48:]
    natural = lax.dot_general(
        small[:48],
        perm.astype(F32),
        NT,
        precision=lax.Precision.HIGHEST,
        preferred_element_type=F32,
    )
    gproj_ref[...] = natural[:n_k].T
    gcomp_ref[...] = natural[n_k:]

    for d in range(1, 4):
        k = (own_slot + d) % 4
        arrived(tr_ref.at[k], t4recv.at[k])
    for j in range(2):
        first, second = tr_ref[2 * j].astype(F32), tr_ref[2 * j + 1].astype(F32)
        out_tab_ref[j, :384, :128] = first
        out_tab_ref[j, 384:rows, :128] = second[: rows - 384]
        rest = second[rows - 384 :]
        out_tab_ref[j, : rows // 2, 128:192] = rest[:, :64]
        out_tab_ref[j, rows // 2 :, 128:192] = pltpu.roll(rest, 64, 1)[:, :64]

    for q in range(4):
        for s in range(2):
            for d in range(1, 4):
                row_copy(q, s, d, gsend, grecv).wait_send()
    dense_core().wait_send()
    small_core().wait_send()
    for d in range(1, n_p):
        dense_plane(d).wait_send()
        dense_gather(d).wait_send()
        small_plane(d).wait_send()
    for d in range(n_p):
        dense_last(d).wait_send()
        table_core(d).wait_send()
    for d in range(1, n_z):
        dense_z(d).wait_send()
        small_z(d).wait_send()
        table_z(d).wait_send()
    for d in range(1, 4):
        for v in range(4):
            table_along(d, v).wait_send()
    for k in range(3):
        table_replica(k).wait_send()


def whole(n):
    return [pl.BlockSpec(memory_space=pltpu.VMEM)] * n


def run_step(scale, *args):
    half = DEN_ROWS // 2
    chunk = half // 16
    blocks = (4, 2, 4, 16, 48, 128)
    dma = pltpu.SemaphoreType.DMA
    vmem = pltpu.VMEM
    return pl.pallas_call(
        functools.partial(step_kernel, scale),
        out_shape=[
            jax.ShapeDtypeStruct((2, 512, 192), F32),
            jax.ShapeDtypeStruct((2, 2048, 128), F32),
            jax.ShapeDtypeStruct((256, 768), F32),
            jax.ShapeDtypeStruct((128, 16), F32),
            jax.ShapeDtypeStruct((32, 128), F32),
            jax.ShapeDtypeStruct((16, 128), F32),
            jax.ShapeDtypeStruct((32, 192), F32),
            jax.ShapeDtypeStruct((8, 128), F32),
        ],
        in_specs=whole(9),
        out_specs=whole(8),
        scratch_shapes=[
            vmem((32, 768, 128), BF),
            vmem((2, 16, 8, 128), jnp.int32),
            vmem((2, 128, 128), jnp.int32),
            vmem(blocks, BF),
            vmem(blocks, BF),
            vmem((2048, 256), BF),
            vmem((DEN_ROWS, 128), F32),
            vmem((48, 128), F32),
            vmem((3, 2048, 128), F32),
            vmem((32, 768, 128), BF),
            vmem((64, 48, 384), F32),
            vmem((2048, 128), F32),
            vmem((128, 2048), BF),
            vmem((64, 384), F32),
            vmem((128, 128), F32),
            vmem((half, 128), BF),
            vmem((half, 128), BF),
            vmem((16, chunk, 128), BF),
            vmem((16, chunk, 128), BF),
            vmem((8, chunk, 128), BF),
            vmem((32, chunk, 128), BF),
            vmem((8, 384, 128), BF),
            vmem((8, 384, 128), BF),
            vmem((4, 384, 128), BF),
            vmem((56, 128), F32),
            vmem((56, 128), F32),
            vmem((16, 56, 128), F32),
            vmem((8, 56, 128), F32),
            dma((64,)),
            dma((32,)),
            dma((2, 16)),
            dma((4, 2, 4)),
            dma((4, 2, 4)),
            dma((4, 2, 4)),
            dma((4, 2, 4)),
            pltpu.SemaphoreType.REGULAR,
            dma,
            dma((56,)),
            dma((16,)),
            dma((8,)),
            dma((16,)),
            dma((16,)),
            dma((16,)),
            dma((16,)),
            dma((20,)),
            dma((16,)),
            dma((8,)),
            dma((8,)),
            dma((3,)),
            dma((4,)),
            dma((24,)),
            dma,
            dma((16,)),
            dma((8,)),
        ],
        compiler_params=pltpu.CompilerParams(
            vmem_limit_bytes=VMEM_LIMIT, collective_id=0, has_side_effects=True
        ),
        name="step",
    )(*args)


def pack_tables(t):
    half = t.shape[1] // 2
    rest = jnp.concatenate([t[:, :half, 128:], t[:, half:, 128:]], 2)
    return jnp.concatenate([t[:, :, :128], rest], 1)


def order_ids(feature_ids, bag_lengths, rows):
    ids = feature_ids[:, 0].transpose(1, 2, 0)
    lens = bag_lengths[:, 0].T
    slots = jnp.arange(ids.shape[1], dtype=jnp.int32)[None, :, None]
    ids = jnp.where(lens[:, None, :] > slots, ids, rows)
    ids = ids.reshape(2, 2, 4, 4, 4, 2, 4, 16).swapaxes(5, 6).reshape(2, 2, 4, 4, 4, 128)
    even = ids[0].transpose(1, 3, 0, 2, 4)
    odd = ids[1].transpose(1, 2, 0, 3, 4)
    return jnp.stack([even, odd]).reshape(2, 16, 8, 128)


def feature_order():
    at = np.arange(128)
    j, a, zh, b = at // 64, at // 16 % 4, at // 4 % 4, at % 4
    x, y = np.where(j == 0, a, b), np.where(j == 0, b, a)
    perm = np.zeros((128, 128), np.float32)
    perm[zh * 32 + x * 8 + y * 2 + j, at] = 1.0
    return perm


def pair_head(w_head, n_out):
    lin = w_head[n_out:].astype(F32).reshape(-1, 192)
    return jnp.concatenate([lin, lin[:, 128:], lin[:, :128]], 1)


def per_device(
    feature_ids, bag_lengths, click_labels, tables, projection, compress, w_in, w_out, w_head
):
    n_out = w_out.shape[1]
    total = feature_ids.shape[0] * lax.axis_size("zl") * lax.axis_size("c")
    scale = 1.0 / math.sqrt(total)
    table_grad, gwin, gwout, gproj, gcomp, ghead, glin, loss = run_step(
        scale,
        order_ids(feature_ids, bag_lengths, tables.shape[1]),
        pack_tables(tables),
        jnp.asarray(feature_order(), BF),
        jnp.concatenate([projection.T, compress], 0),
        w_in,
        w_out,
        w_head[:n_out].astype(F32)[None, :],
        pair_head(w_head, n_out),
        click_labels.astype(F32),
    )
    gwin = jnp.concatenate([gwin[0], gwin[1]], 1)
    ghead = jnp.concatenate([ghead[: n_out // 128].reshape(-1), glin.reshape(-1)])
    return (loss[0, 0] / total, gproj, gcomp, gwin, gwout, ghead, table_grad)


def solution(mesh):
    fine = Mesh(mesh.devices.reshape(4, 4, 4, 2, 2), ("zh", "x", "y", "zl", "c"))
    emb = ("zh", "x", "y")
    rep = ("zl", "c")
    placed = (
        P(None, rep, emb, None),
        P(None, rep, emb),
        P(emb, rep),
        P(emb, None, None),
        P(),
        P(),
        P(),
        P(),
        P(),
    )
    return jax.shard_map(
        per_device,
        mesh=fine,
        in_specs=placed,
        out_specs=(P(), P(), P(), P(), P(), P(), P(emb, None, None)),
        check_vma=False,
    )
```

```python
import functools
import math

import jax
import jax.numpy as jnp
import numpy as np
from jax import lax
from jax.experimental import pallas as pl
from jax.experimental.pallas import tpu as pltpu
from jax.sharding import Mesh, PartitionSpec as P

EPS = 1e-05
BF = jnp.bfloat16
F32 = jnp.float32
NT = (((1,), (1,)), ((), ()))
TN = (((0,), (0,)), ((), ()))
VMEM_LIMIT = 60 * 1024 * 1024
MESH = pl.DeviceIdType.MESH
AT_WOUT = 4096
AT_GW = AT_WOUT + 1536
AT_LIN = AT_GW + 48
AT_HEAD = AT_LIN + 64
DEN_ROWS = 6144


def mm(a, b, dims=None):
    if dims is None:
        return jnp.dot(a, b, preferred_element_type=F32)
    return lax.dot_general(a, b, dims, preferred_element_type=F32)


def arrived(dst, sem):
    pltpu.make_async_copy(dst, dst, sem).wait()


def step_kernel(
    scale,
    raw_ref,
    lens_ref,
    tabt_ref,
    perm_ref,
    proj_ref,
    comp_ref,
    win_hbm,
    wout_hbm,
    whead_ref,
    label_ref,
    out_tab_ref,
    gwin_hbm,
    gwout_hbm,
    gproj_ref,
    gcomp_ref,
    ghead_ref,
    out_loss_ref,
    win_ref,
    wout_ref,
    win_sem,
    wout_sem,
    gwin_sem,
    gwout_sem,
    ids_ref,
    hp_ref,
    tz_ref,
    idt_ref,
    col_ref,
    y_ref,
    x_ref,
    winp_ref,
    den_ref,
    gw_ref,
    split_ref,
    xp_ref,
    mix_ref,
    inter_ref,
    nb_ref,
    ld_ref,
    slope_ref,
    da_ref,
    db_ref,
    dc_ref,
    dd_ref,
    de_ref,
    df_ref,
    te_ref,
    tf_ref,
    tr_ref,
    sa_ref,
    sb_ref,
    sp_ref,
    sz_ref,
    asend,
    arecv,
    irecv,
    ysend,
    xrecv,
    gsend,
    grecv,
    free_sem,
    core_sem,
    dsend,
    dp_sem,
    dz_sem,
    dg_sem,
    dh_sem,
    t1send,
    t1recv,
    t2send,
    t2recv,
    t3send,
    t3recv,
    t4send,
    t4recv,
    ssend,
    sc_sem,
    sp_sem,
    sz_sem,
):
    zh, px, py, zl, c = [lax.axis_index(name) for name in ("zh", "x", "y", "zl", "c")]
    n_p, n_z = 16, 8
    z = zh * 2 + zl
    p = px * 4 + py
    other = 1 - c
    sibling = (zh, px, py, zl, other)
    n_f, n_b, n_k, tile = 128, 128, 16, 16
    rows = 512
    low, high, rest_rows = slice(0, 256), slice(256, 512), slice(512, 768)
    width = n_k * n_f
    half = DEN_ROWS // 2
    chunk = half // n_p
    o = py * other + px * c
    o_other = px * other + py * c

    def at_plane(q):
        return (zh, q // 4, q % 4, zl, c)

    def at_z(v):
        return (v // 2, px, py, v % 2, c)

    def along(d):
        return (zh, (px + d * c) % 4, (py + d * other) % 4, zl, c)

    def in_row(s, d):
        if s == 0:
            return (px + d) % 4, (zh, (px + d) % 4, py, zl, c)
        return (py + d) % 4, (zh, px, (py + d) % 4, zl, c)

    def remote(src, dst, send_sem, recv_sem, device):
        return pltpu.make_async_remote_copy(
            src_ref=src,
            dst_ref=dst,
            send_sem=send_sem,
            recv_sem=recv_sem,
            device_id=device,
            device_id_type=MESH,
        )

    load_win = pltpu.make_async_copy(win_hbm, win_ref, win_sem)
    load_wout = pltpu.make_async_copy(wout_hbm, wout_ref, wout_sem)
    load_win.start()
    load_wout.start()
    barrier = pltpu.get_barrier_semaphore()
    partners = [sibling, (zh, px, py, 1 - zl, other)]
    partners += [at_plane((p + d) % n_p) for d in range(1, n_p)]
    partners += [at_z((z + d) % n_z) for d in range(1, n_z)]
    for dz in range(1, 4):
        for d in range(1, 4):
            partners.append(((zh + dz) % 4, px, (py + d) % 4, zl, c))
            partners.append(((zh + dz) % 4, (px + d) % 4, py, zl, c))
    for device in partners:
        pl.semaphore_signal(barrier, inc=1, device_id=device, device_id_type=MESH)
    eye = (
        lax.broadcasted_iota(jnp.int32, (128, 128), 0)
        == lax.broadcasted_iota(jnp.int32, (128, 128), 1)
    ).astype(F32).astype(BF)
    mine = c * 16 + zh * 4 + o
    for j, at in ((c, mine), (other, other * 16 + zh * 4 + o_other)):
        tz_ref[at, :rows, :] = mm(tabt_ref[j, :128, :], eye, TN).astype(BF)
        tz_ref[at, rest_rows, :] = (
            mm(tabt_ref[j, 128:, low], eye[:64], TN) + mm(tabt_ref[j, 128:, high], eye[64:], TN)
        ).astype(BF)
    for slot in range(2):
        for j in range(2):
            ids = jnp.where(
                lens_ref[j : j + 1, :] > slot, raw_ref[j, slot : slot + 1, :], rows
            )
            for e in range(64):
                ez, ex, ey = e // 16, e // 4 % 4, e % 4
                to, at = (ez * 4 + ey, ex) if j == 0 else (ez * 4 + ex, ey)
                ids_ref[j, to, slot * 4 + at : slot * 4 + at + 1, :] = ids[
                    :, e * 128 : (e + 1) * 128
                ]
    pl.semaphore_wait(barrier, len(partners))

    sends = []

    def send(src, dst, sem, device):
        copy = remote(src, dst, asend.at[len(sends)], sem, device)
        copy.start()
        sends.append(copy)

    def send_table(at, device):
        send(tz_ref.at[at], tz_ref.at[at], arecv.at[at], device)

    near = (zh + 3 + 2 * zl) % 4
    for to, lo in ((near, 0), (near, 1), ((zh + 2) % 4, 1 - zl)):
        send_table(mine, (to, px, py, lo, c))
    for d in range(1, 4):
        send_table(mine, along(d))
    for dz in range(4):
        for d in range(4):
            if dz == 0 and d == 0:
                continue
            to = (zh + dz) % 4
            ty, tx = (py + d) % 4, (px + d) % 4
            send(
                ids_ref.at[0, to * 4 + ty],
                idt_ref.at[0, zh * 4 + py],
                irecv.at[0, zh * 4 + py],
                (to, px, ty, zl, c),
            )
            send(
                ids_ref.at[1, to * 4 + tx],
                idt_ref.at[1, zh * 4 + px],
                irecv.at[1, zh * 4 + px],
                (to, tx, py, zl, c),
            )
    idt_ref[0, zh * 4 + py] = ids_ref[0, zh * 4 + py]
    idt_ref[1, zh * 4 + px] = ids_ref[1, zh * 4 + px]
    for dz in (1, 3, 2):
        at = c * 16 + (zh + dz) % 4 * 4 + o
        arrived(tz_ref.at[at], arecv.at[at])
        for d in range(1, 4):
            send_table(at, along(d))
        send_table(at, sibling)

    perm = perm_ref[...]
    wt = jnp.concatenate([mm(proj_ref[...], perm), mm(comp_ref[...], perm)], 0).astype(BF)
    n_head = wout_ref.shape[1] // 128
    heads = whead_ref[...].astype(F32)
    head = jnp.concatenate([heads[i : i + 1] for i in range(n_head)], 1)
    split_ref[2, :48, :] = heads[n_head:]
    r0, r1, r2 = [split_ref[2, pl.ds(i, 16, stride=3), :] for i in range(3)]
    left64 = lax.broadcasted_iota(jnp.int32, (16, 128), 1) < 64
    turn1, turn2 = pltpu.roll(r1, 64, 1), pltpu.roll(r2, 64, 1)
    hp_ref[0, pl.ds(0, 16, stride=2), :] = r0
    hp_ref[0, pl.ds(1, 16, stride=2), :] = jnp.where(left64, turn1, turn2)
    hp_ref[1, pl.ds(0, 16, stride=2), :] = jnp.where(left64, r1, turn1)
    hp_ref[1, pl.ds(1, 16, stride=2), :] = jnp.where(left64, turn2, r2)
    hpair = jnp.concatenate([hp_ref[0], hp_ref[1], hp_ref[0]], 1)
    load_win.wait()
    load_wout.wait()
    for side in range(2):
        cols = slice(side * 128, (side + 1) * 128)
        split_ref[side] = win_ref[:, cols].astype(F32)
        for k in range(n_k):
            block = split_ref[side, pl.ds(k, n_f, stride=n_k), :].astype(BF)
            winp_ref[k * n_f : (k + 1) * n_f, cols] = mm(perm, block, TN).astype(BF)

    for dz in (0, 1, 3, 2):
        for d in (1, 3, 2):
            at = c * 16 + (zh + dz) % 4 * 4 + (o + d) % 4
            arrived(tz_ref.at[at], arecv.at[at])
            send_table(at, sibling)
    for dz in range(4):
        for d in range(4):
            if dz == 0 and d == 0:
                continue
            v = (zh + dz) % 4 * 4
            for s, own in ((0, py), (1, px)):
                at = v + (own + d) % 4
                arrived(idt_ref.at[s, at], irecv.at[s, at])
    for s in range(2):
        col_ref[s] = idt_ref[s].reshape(128, 128).T
    for dz in (0, 1, 3, 2):
        for d in range(4):
            if dz == 0 and d == 0:
                continue
            at = other * 16 + (zh + dz) % 4 * 4 + (o_other + d) % 4
            arrived(tz_ref.at[at], arecv.at[at])

    def row_copy(q, s, d, send_sems, recv_sems):
        to, device = in_row(s, d)
        here = py if s else px
        return remote(
            y_ref.at[q, s, to],
            x_ref.at[q, s, here],
            send_sems.at[q, s, to],
            recv_sems.at[q, s, here],
            device,
        )

    def keep_own(q):
        x_ref[q, 0, px] = y_ref[q, 0, px]
        x_ref[q, 1, py] = y_ref[q, 1, py]

    def row_arrived(q, recv_sems):
        for s in range(2):
            for d in (1, 3, 2):
                src = in_row(s, d)[0]
                arrived(x_ref.at[q, s, src], recv_sems.at[q, s, src])

    def lookup(q, carry):
        def one_set(s, inner):
            cols = jnp.concatenate(
                [
                    col_ref[s, pl.ds(pl.multiple_of(h * 64 + q * tile, tile), tile), :]
                    for h in range(2)
                ],
                0,
            )
            lane = lax.broadcasted_iota(jnp.int32, (128, rows), 1)
            first = lax.broadcasted_iota(jnp.int32, (4, tile, 128), 2) < 64
            for i in range(16):
                hot = jnp.zeros((128, rows), F32)
                for slot in range(2):
                    at = i * 8 + slot * 4
                    ids = jnp.concatenate([cols[:, at + k : at + k + 1] for k in range(4)], 0)
                    hot = hot + jnp.where(lane == ids, 1.0, 0.0)
                hot = hot.astype(BF)
                f = s * 16 + i
                rest = tz_ref[f, rest_rows, :]
                one = mm(hot[:, low], jnp.concatenate([tz_ref[f, low, :], rest], 1))
                two = mm(hot[:, high], jnp.concatenate([tz_ref[f, high, :], rest], 1))
                main = one[:, :128] + two[:, :128]
                y_ref[q, s, :, i, : 2 * tile, :] = main.astype(BF).reshape(4, 2 * tile, 128)
                one, two = [v[:, 128:].reshape(4, 2, tile, 128) for v in (one, two)]

                def turn(v):
                    return pltpu.roll(v.reshape(64, 128), 64, 1).reshape(4, tile, 128)

                tail = jnp.where(
                    first, one[:, 0] + turn(two[:, 0]), turn(one[:, 1]) + two[:, 1]
                )
                y_ref[q, s, :, i, 2 * tile :, :] = tail.astype(BF)
            return inner

        lax.fori_loop(0, 2, one_set, 0)
        for d in (1, 3, 2):
            for s in range(2):
                row_copy(q, s, d, ysend, xrecv).start()
        keep_own(q)
        return carry

    lax.fori_loop(0, 4, lookup, 0)
    for copy in sends:
        copy.wait_send()

    lane1 = lax.broadcasted_iota(jnp.int32, (n_k, 384), 1) < 192
    row_lane1 = lax.broadcasted_iota(jnp.int32, (1, 384), 1) < 192

    def load_group(q, carry):
        row_arrived(q, xrecv)
        for part in range(3):
            block = x_ref[q, :, :, :, part * tile : (part + 1) * tile, :]
            split_ref[part] = block.astype(F32).reshape(n_f * tile, 128)

        def pair(j, inner):
            p = q * tile + j
            pieces = [
                split_ref[part, pl.ds(j, n_f, stride=tile), :].astype(BF) for part in (0, 2, 1)
            ]
            x3 = jnp.concatenate(pieces, 1)
            for part in range(3):
                first = pl.multiple_of(p % 2 * 384 + part * 128, 128)
                xp_ref[p // 2, pl.ds(first, 128), :] = pieces[part]
            mixed = mm(wt, x3)
            mix_ref[p] = mixed
            compact = mixed[:n_k]
            stacked = jnp.concatenate(
                [jnp.where(lane1, compact, 0.0), jnp.where(lane1, 0.0, compact)], 0
            ).astype(BF)
            inter = mm(stacked, x3, NT)
            inter_ref[pl.ds(p, n_k, stride=n_b), :] = inter[:n_k]
            inter_ref[pl.ds(64 + p, n_k, stride=n_b), :] = inter[n_k:]
            ld_ref[pl.ds(p, 1), :] = jnp.sum(mixed[n_k:] * hpair, 0, keepdims=True)
            return inner

        lax.fori_loop(0, tile, pair, 0, unroll=2)
        return carry

    lax.fori_loop(0, 64 // tile, load_group, 0)

    for s in range(2):
        for d in range(1, 4):
            pl.semaphore_signal(
                free_sem, inc=1, device_id=in_row(s, d)[1], device_id_type=MESH
            )

    total = jnp.zeros((n_b, n_f), F32)
    for k in range(n_k):
        total = total + inter_ref[k * n_b : (k + 1) * n_b, :]
    center = jnp.sum(total, 1, keepdims=True) / width
    total = jnp.zeros((n_b, n_f), F32)
    for k in range(n_k):
        shifted = inter_ref[k * n_b : (k + 1) * n_b, :] - center
        total = total + shifted * shifted
    rstd = lax.rsqrt(jnp.sum(total, 1, keepdims=True) / width + EPS)
    for k in range(n_k):
        normed = (inter_ref[k * n_b : (k + 1) * n_b, :] - center) * rstd
        inter_ref[k * n_b : (k + 1) * n_b, :] = normed
        nb_ref[:, k * n_f : (k + 1) * n_f] = normed.astype(BF)
    pre_act = mm(nb_ref[...], winp_ref[...])
    sigma = 1.0 / (1.0 + jnp.exp(-pre_act))
    hidden = (pre_act * sigma).astype(BF)
    factor = mm(hidden, wout_ref[...])
    lin = ld_ref[...]
    lin1 = jnp.sum(jnp.where(row_lane1, lin, 0.0), 1, keepdims=True)
    lin2 = jnp.sum(jnp.where(row_lane1, 0.0, lin), 1, keepdims=True)
    logit = jnp.sum(factor * head, 1, keepdims=True) + jnp.concatenate([lin1, lin2], 0)
    target = jnp.broadcast_to(label_ref[...].astype(F32), (8, 128)).T[:, :1]
    terms = jnp.maximum(logit, 0.0) + jnp.log1p(jnp.exp(-jnp.abs(logit))) - target * logit
    sa_ref[48:, :] = jnp.broadcast_to(
        jnp.sum(jnp.broadcast_to(terms, (n_b, 128)), 0, keepdims=True), (8, 128)
    )
    slope = scale * (1.0 / (1.0 + jnp.exp(-logit)) - target)
    slope_ref[...] = jnp.broadcast_to(slope, (n_b, 128))
    den_ref[AT_HEAD:, :] = jnp.zeros((den_ref.shape[0] - AT_HEAD, 128), F32)
    ghead = jnp.sum(slope * factor, 0, keepdims=True)
    for i in range(ghead.shape[1] // 128):
        den_ref[AT_HEAD + i : AT_HEAD + i + 1, :] = ghead[:, i * 128 : (i + 1) * 128]
    gfactor = (slope * head).astype(BF)
    for i in range(gfactor.shape[1] // 128):
        den_ref[AT_WOUT + i * 256 : AT_WOUT + (i + 1) * 256, :] = mm(
            hidden, gfactor[:, i * 128 : (i + 1) * 128], TN
        )
    ghidden = mm(gfactor, wout_ref[...], NT)
    gpre = (ghidden * sigma * (1.0 + pre_act * (1.0 - sigma))).astype(BF)
    first = jnp.zeros((n_b, n_f), F32)
    second = jnp.zeros((n_b, n_f), F32)
    for k in range(n_k):
        feats = slice(k * n_f, (k + 1) * n_f)
        gwin = mm(nb_ref[:, feats], gpre, TN)
        den_ref[feats, :] = gwin[:, :128]
        den_ref[width + k * n_f : width + (k + 1) * n_f, :] = gwin[:, 128:]
        gnormed = mm(gpre, winp_ref[feats, :], NT)
        first = first + gnormed
        second = second + gnormed * inter_ref[k * n_b : (k + 1) * n_b, :]
    mean1 = jnp.sum(first, 1, keepdims=True) / width
    mean2 = jnp.sum(second, 1, keepdims=True) / width
    for k in range(n_k):
        feats = slice(k * n_f, (k + 1) * n_f)
        span = slice(k * n_b, (k + 1) * n_b)
        gnormed = mm(gpre, winp_ref[feats, :], NT)
        inter_ref[span, :] = rstd * (gnormed - mean1 - inter_ref[span, :] * mean2)

    def slope_row(p):
        s1 = slope_ref[pl.ds(p, 1), :]
        s2 = slope_ref[pl.ds(64 + p, 1), :]
        return jnp.where(
            row_lane1,
            jnp.concatenate([s1, s1, s1], 1),
            jnp.concatenate([s2, s2, s2], 1),
        )

    ghl = lax.fori_loop(
        0,
        64,
        lambda p, sum: sum + slope_row(p) * mix_ref[p, n_k:, :],
        jnp.zeros((32, 384), F32),
        unroll=4,
    )
    second = ghl[:, 128:256]
    lane = lax.broadcasted_iota(jnp.int32, second.shape, 1)
    den_ref[AT_LIN : AT_LIN + 32, :] = ghl[:, :128] + ghl[:, 256:]
    den_ref[AT_LIN + 32 : AT_LIN + 64, :] = jnp.where(
        lane < 64, second + pltpu.roll(second, 64, 1), 0.0
    )
    den_ref[AT_GW:AT_LIN, :] = jnp.zeros((AT_LIN - AT_GW, 128), F32)
    gw_ref[...] = jnp.zeros_like(gw_ref)

    def dense_core():
        return remote(da_ref, db_ref, dsend.at[0], core_sem, sibling)

    def dense_plane(d):
        to = (p + d) % n_p
        return remote(
            dc_ref.at[to], dd_ref.at[p], dsend.at[d], dp_sem.at[p], at_plane(to)
        )

    def dense_z(d):
        return remote(
            de_ref.at[z], de_ref.at[z], dsend.at[15 + d], dz_sem.at[z], at_z((z + d) % n_z)
        )

    def dense_gather(d):
        at = c * n_p + p
        return remote(
            df_ref.at[at],
            df_ref.at[at],
            dsend.at[22 + d],
            dg_sem.at[p],
            at_plane((p + d) % n_p),
        )

    def dense_last(d):
        q = (p + d) % n_p
        at = c * n_p + q
        return remote(df_ref.at[at], df_ref.at[at], dsend.at[38 + d], dh_sem.at[q], sibling)

    def dense_step1():
        arrived(db_ref, core_sem)

        def add(i, carry):
            at = pl.multiple_of(i * chunk, chunk)
            mine = den_ref[pl.ds(pl.multiple_of(c * half + i * chunk, chunk), chunk), :]
            dc_ref[i] = (mine + db_ref[pl.ds(at, chunk), :].astype(F32)).astype(BF)
            return carry

        lax.fori_loop(0, n_p, add, 0)
        for d in range(1, n_p):
            dense_plane(d).start()

    def dense_step2():
        own = dc_ref[p].astype(F32)
        for d in range(1, n_p):
            q = (p + d) % n_p
            arrived(dd_ref.at[q], dp_sem.at[q])
            own = own + dd_ref[q].astype(F32)
        de_ref[z] = own.astype(BF)
        for d in range(1, n_z):
            dense_z(d).start()

    def dense_step3():
        for d in range(1, n_z):
            v = (z + d) % n_z
            arrived(de_ref.at[v], dz_sem.at[v])
        own = de_ref[0].astype(F32)
        for v in range(1, n_z):
            own = own + de_ref[v].astype(F32)
        df_ref[c * n_p + p] = own.astype(BF)
        for d in range(1, n_p):
            dense_gather(d).start()
        dense_last(0).start()

    da_ref[...] = den_ref[pl.ds(pl.multiple_of(other * half, half), half), :].astype(BF)
    dense_core().start()
    for q in range(4):
        for s in range(2):
            for d in range(1, 4):
                row_copy(q, s, d, ysend, xrecv).wait_send()
    pl.semaphore_wait(free_sem, 6)

    def back_group(q, carry):
        pl.when(q == 3)(dense_step2)

        def pair(j, inner):
            p = q * tile + j
            x3 = jnp.concatenate(
                [
                    xp_ref[p // 2, pl.ds(pl.multiple_of(p % 2 * 384 + part * 128, 128), 128), :]
                    for part in range(3)
                ],
                1,
            )
            gi = jnp.concatenate(
                [
                    inter_ref[pl.ds(p, n_k, stride=n_b), :],
                    inter_ref[pl.ds(64 + p, n_k, stride=n_b), :],
                ],
                0,
            ).astype(BF)
            gc = mm(gi, x3)
            gc = jnp.where(lane1, gc[:n_k], gc[n_k:]).astype(BF)
            srow = slope_row(p)
            gl = (srow * hpair).astype(BF)
            compact = mix_ref[p, :n_k, :]
            tail = jnp.concatenate([gc, gl], 0)
            right = jnp.concatenate(
                [
                    jnp.where(lane1, compact, 0.0).astype(BF),
                    jnp.where(lane1, 0.0, compact).astype(BF),
                    tail,
                ],
                0,
            )
            left = jnp.concatenate([gi, wt], 0)
            gp = mm(left, right, TN)
            gw_ref[...] += mm(tail, x3, NT)
            for part, at in ((0, 0), (2, 128), (1, 256)):
                split_ref[part, pl.ds(j, n_f, stride=tile), :] = gp[:, at : at + 128]
            return inner

        lax.fori_loop(0, tile, pair, 0, unroll=2)
        for part in range(3):
            y_ref[q, :, :, :, part * tile : (part + 1) * tile, :] = (
                split_ref[part].reshape(2, 4, 16, tile, 128).astype(BF)
            )
        pl.when(q == 0)(dense_step1)
        for d in (1, 3, 2):
            for s in range(2):
                row_copy(q, s, d, gsend, grecv).start()
        keep_own(q)
        return carry

    lax.fori_loop(0, 64 // tile, back_group, 0)

    def small_core():
        return remote(sa_ref, sb_ref, ssend.at[0], sc_sem, sibling)

    def small_plane(d):
        return remote(
            sp_ref.at[p], sp_ref.at[p], ssend.at[d], sp_sem.at[p], at_plane((p + d) % n_p)
        )

    def small_z(d):
        return remote(
            sz_ref.at[z], sz_ref.at[z], ssend.at[15 + d], sz_sem.at[z], at_z((z + d) % n_z)
        )

    sa_ref[:48, :] = gw_ref[...]
    small_core().start()

    def table_grad(s, i):
        hots, mains, rests = [], [], []
        row = lax.broadcasted_iota(jnp.int32, (rows, 128), 0)
        for src in range(4):
            hot = jnp.zeros((rows, 128), F32)
            for slot in range(2):
                ids = idt_ref[s, i, slot * 4 + src : slot * 4 + src + 1, :]
                hot = hot + jnp.where(row == ids, 1.0, 0.0)
            hots.append(hot.astype(BF))
            for k in range(8):
                mains.append(x_ref[k % 4, s, src, i, k // 4 * tile : (k // 4 + 1) * tile, :])
            for q in range(4):
                rests.append(x_ref[q, s, src, i, 2 * tile :, :])
        turned = pltpu.roll(jnp.concatenate(rests, 0).astype(F32), 64, 1).astype(BF)
        tails = []
        for src in range(4):
            tails += rests[src * 4 : src * 4 + 4]
            tails.append(turned[src * 64 : (src + 1) * 64])
        right = jnp.concatenate([jnp.concatenate(mains, 0), jnp.concatenate(tails, 0)], 1)
        sums = mm(jnp.concatenate(hots, 1), right)
        lane = lax.broadcasted_iota(jnp.int32, (256, 128), 1)
        tail = jnp.where(lane < 64, sums[low, 128:], pltpu.roll(sums[high, 128:], 64, 1))
        return sums[:, :128], tail

    def table_core(i):
        return remote(
            tz_ref.at[16 + i], tz_ref.at[i], t1send.at[i], t1recv.at[i], sibling
        )

    def table_along(d, v):
        return remote(
            xp_ref.at[v * 4 + (o + d) % 4],
            xp_ref.at[16 + o * 4 + v],
            t2send.at[d * 4 + v],
            t2recv.at[o * 4 + v],
            along(d),
        )

    def table_z(to):
        return remote(te_ref.at[to], tf_ref.at[z], t3send.at[to], t3recv.at[z], at_z(to))

    own_slot = 2 * c + zl

    def table_replica(k):
        device = (sibling, (zh, px, py, 1 - zl, c), (zh, px, py, 1 - zl, other))[k]
        return remote(
            tr_ref.at[own_slot], tr_ref.at[own_slot], t4send.at[k], t4recv.at[own_slot], device
        )

    for q in range(4):
        row_arrived(q, grecv)
    dense_step3()

    def for_sibling(n, carry):
        i = (zh + 1 + n // 4) % 4 * 4 + (o_other + 1 + n % 4) % 4
        main, tail = table_grad(other, i)
        tz_ref[16 + i, :rows, :] = main.astype(BF)
        tz_ref[16 + i, rest_rows, :] = tail.astype(BF)
        table_core(i).start()
        return carry

    lax.fori_loop(0, 16, for_sibling, 0)

    arrived(sb_ref, sc_sem)
    sp_ref[p] = sa_ref[...] + sb_ref[...]
    for d in range(1, n_p):
        small_plane(d).start()

    def for_chip(n, carry):
        d, v = n % 4 + 1, (zh + 1 + n // 4) % 4
        i = v * 4 + (o + d) % 4
        main, tail = table_grad(c, i)
        arrived(tz_ref.at[i], t1recv.at[i])
        xp_ref[i, :rows, :] = (main + tz_ref[i, :rows, :].astype(F32)).astype(BF)
        xp_ref[i, rest_rows, :] = (tail + tz_ref[i, rest_rows, :].astype(F32)).astype(BF)

        @pl.when(d < 4)
        def _():
            table_along(d, v).start()

        return carry

    lax.fori_loop(0, 16, for_chip, 0)

    own = None
    for dv in (1, 2, 3, 0):
        v = (zh + dv) % 4
        for k in range(1, 4):
            at = (o + k) % 4 * 4 + v
            arrived(xp_ref.at[16 + at], t2recv.at[at])
        for flip in (1, 0):
            lo = (zl + flip) % 2
            span = pl.ds(pl.multiple_of(lo * 384, 384), 384)
            own = xp_ref[v * 4 + o, span, :].astype(F32)
            for k in range(1, 4):
                own = own + xp_ref[16 + (o + k) % 4 * 4 + v, span, :].astype(F32)
            if dv > 0 or flip > 0:
                te_ref[v * 2 + lo] = own.astype(BF)
                table_z(v * 2 + lo).start()

    for d in range(1, n_p):
        q = (p + d) % n_p
        arrived(df_ref.at[c * n_p + q], dg_sem.at[q])
        dense_last(d).start()
    for d in range(1, n_p):
        q = (p + d) % n_p
        arrived(sp_ref.at[q], sp_sem.at[q])
    small = sp_ref[0]
    for q in range(1, n_p):
        small = small + sp_ref[q]
    sz_ref[z] = small
    for d in range(1, n_z):
        small_z(d).start()

    for q in range(n_p):
        arrived(df_ref.at[other * n_p + q], dh_sem.at[q])

    def final(first, count):
        pieces = []
        at = first
        while at < first + count:
            i, r = at // chunk, at % chunk
            n = min(chunk - r, first + count - at)
            pieces.append(df_ref[i, r : r + n, :])
            at += n
        return pieces[0] if len(pieces) == 1 else jnp.concatenate(pieces, 0)

    stores = []

    def store(src, dst, sem):
        copy = pltpu.make_async_copy(src, dst, sem)
        copy.start()
        stores.append(copy)

    for side in range(2):
        for k in range(n_k):
            block = final(side * 2048 + k * 128, 128)
            split_ref[side, pl.ds(k, n_f, stride=n_k), :] = mm(perm, block)
        store(
            split_ref.at[side],
            gwin_hbm.at[:, side * 128 : (side + 1) * 128],
            gwin_sem.at[side],
        )
    for i in range(n_head):
        span = slice(i * 256, (i + 1) * 256)
        split_ref[2, span, :] = final(AT_WOUT + i * 256, 256).astype(F32)
        store(
            split_ref.at[2, span],
            gwout_hbm.at[:, i * 128 : (i + 1) * 128],
            gwout_sem.at[i],
        )
    ghead_ref[:n_head, :] = final(AT_HEAD, 16).astype(F32)[:n_head]
    hp_ref[0] = final(AT_LIN, 32).astype(F32)
    hp_ref[1] = final(AT_LIN + 32, 32).astype(F32)
    even, odd = [hp_ref[0, pl.ds(i, 16, stride=2), :] for i in range(2)]
    even_rest, odd_rest = [hp_ref[1, pl.ds(i, 16, stride=2), :] for i in range(2)]
    turned = pltpu.roll(odd, 64, 1)
    lin_ref = split_ref.at[2, 1536:]
    lin_ref[pl.ds(0, 16, stride=3), :] = even
    lin_ref[pl.ds(1, 16, stride=3), :] = jnp.where(left64, even_rest, turned)
    lin_ref[pl.ds(2, 16, stride=3), :] = jnp.where(
        left64, turned, pltpu.roll(odd_rest, 64, 1)
    )
    ghead_ref[n_head:, :] = lin_ref[:48, :]

    for d in range(1, n_z):
        v = (z + d) % n_z
        arrived(tf_ref.at[v], t3recv.at[v])
        own = own + tf_ref[v].astype(F32)
    tr_ref[own_slot] = own.astype(BF)
    for k in range(3):
        table_replica(k).start()

    for d in range(1, n_z):
        v = (z + d) % n_z
        arrived(sz_ref.at[v], sz_sem.at[v])
    small = sz_ref[0]
    for v in range(1, n_z):
        small = small + sz_ref[v]
    out_loss_ref[...] = small[48:49, :1] * (scale * scale)
    natural = lax.dot_general(
        small[:48],
        perm.astype(F32),
        NT,
        precision=lax.Precision.HIGHEST,
        preferred_element_type=F32,
    )
    gproj_ref[...] = natural[:n_k]
    gcomp_ref[...] = natural[n_k:]

    for d in range(1, 4):
        k = (own_slot + d) % 4
        arrived(tr_ref.at[k], t4recv.at[k])
    for j in range(2):
        first, second = tr_ref[2 * j], tr_ref[2 * j + 1]
        main = jnp.concatenate([first, second[: rows - 384]], 0)
        rest = second[rows - 384 :]
        out_tab_ref[j, :128, :] = mm(eye, main, NT)
        out_tab_ref[j, 128:, low] = mm(eye[:64], rest, NT)
        out_tab_ref[j, 128:, high] = mm(eye[64:], rest, NT)
    for copy in stores:
        copy.wait()

    for q in range(4):
        for s in range(2):
            for d in range(1, 4):
                row_copy(q, s, d, gsend, grecv).wait_send()
    dense_core().wait_send()
    small_core().wait_send()
    for d in range(1, n_p):
        dense_plane(d).wait_send()
        dense_gather(d).wait_send()
        small_plane(d).wait_send()
    for d in range(n_p):
        dense_last(d).wait_send()
        table_core(d).wait_send()
    for d in range(1, n_z):
        dense_z(d).wait_send()
        small_z(d).wait_send()
        table_z((z + d) % n_z).wait_send()
    for d in range(1, 4):
        for v in range(4):
            table_along(d, v).wait_send()
    for k in range(3):
        table_replica(k).wait_send()


def whole(n):
    return [pl.BlockSpec(memory_space=pltpu.VMEM)] * n


def run_step(scale, *args):
    half = DEN_ROWS // 2
    chunk = half // 16
    blocks = (4, 2, 4, 16, 48, 128)
    dma = pltpu.SemaphoreType.DMA
    vmem = pltpu.VMEM
    anywhere = [pl.BlockSpec(memory_space=pl.ANY)]
    return pl.pallas_call(
        functools.partial(step_kernel, scale),
        out_shape=[
            jax.ShapeDtypeStruct((2, 192, 512), F32),
            jax.ShapeDtypeStruct((2048, 256), F32),
            jax.ShapeDtypeStruct((256, 768), F32),
            jax.ShapeDtypeStruct((16, 128), F32),
            jax.ShapeDtypeStruct((32, 128), F32),
            jax.ShapeDtypeStruct((54, 128), F32),
            jax.ShapeDtypeStruct((1, 1), F32),
        ],
        in_specs=whole(6) + anywhere * 2 + whole(2),
        out_specs=whole(1) + anywhere * 2 + whole(4),
        scratch_shapes=[
            vmem((2048, 256), BF),
            vmem((256, 768), BF),
            dma,
            dma,
            dma((2,)),
            dma((6,)),
            vmem((2, 16, 8, 128), jnp.int32),
            vmem((2, 32, 128), F32),
            vmem((32, 768, 128), BF),
            vmem((2, 16, 8, 128), jnp.int32),
            vmem((2, 128, 128), jnp.int32),
            vmem(blocks, BF),
            vmem(blocks, BF),
            vmem((2048, 256), BF),
            vmem((DEN_ROWS, 128), F32),
            vmem((48, 128), F32),
            vmem((3, 2048, 128), F32),
            vmem((32, 768, 128), BF),
            vmem((64, 48, 384), F32),
            vmem((2048, 128), F32),
            vmem((128, 2048), BF),
            vmem((64, 384), F32),
            vmem((128, 128), F32),
            vmem((half, 128), BF),
            vmem((half, 128), BF),
            vmem((16, chunk, 128), BF),
            vmem((16, chunk, 128), BF),
            vmem((8, chunk, 128), BF),
            vmem((32, chunk, 128), BF),
            vmem((8, 384, 128), BF),
            vmem((8, 384, 128), BF),
            vmem((4, 384, 128), BF),
            vmem((56, 128), F32),
            vmem((56, 128), F32),
            vmem((16, 56, 128), F32),
            vmem((8, 56, 128), F32),
            dma((64,)),
            dma((32,)),
            dma((2, 16)),
            dma((4, 2, 4)),
            dma((4, 2, 4)),
            dma((4, 2, 4)),
            dma((4, 2, 4)),
            pltpu.SemaphoreType.REGULAR,
            dma,
            dma((56,)),
            dma((16,)),
            dma((8,)),
            dma((16,)),
            dma((16,)),
            dma((16,)),
            dma((16,)),
            dma((20,)),
            dma((16,)),
            dma((8,)),
            dma((8,)),
            dma((3,)),
            dma((4,)),
            dma((24,)),
            dma,
            dma((16,)),
            dma((8,)),
        ],
        compiler_params=pltpu.CompilerParams(
            vmem_limit_bytes=VMEM_LIMIT, collective_id=0, has_side_effects=True
        ),
        name="step",
    )(*args)


def feature_order():
    at = np.arange(128)
    j, a, zh, b = at // 64, at // 16 % 4, at // 4 % 4, at % 4
    x, y = np.where(j == 0, a, b), np.where(j == 0, b, a)
    perm = np.zeros((128, 128), np.float32)
    perm[zh * 32 + x * 8 + y * 2 + j, at] = 1.0
    return perm


def per_device(
    feature_ids, bag_lengths, click_labels, tables, projection, compress, w_in, w_out, w_head
):
    total = feature_ids.shape[0] * lax.axis_size("zl") * lax.axis_size("c")
    table_grad, gwin, gwout, gproj, gcomp, ghead, loss = run_step(
        1.0 / math.sqrt(total),
        feature_ids[:, 0].transpose(1, 2, 0),
        bag_lengths[:, 0].T,
        tables.transpose(0, 2, 1),
        jnp.asarray(feature_order(), BF),
        projection.T,
        compress,
        w_in,
        w_out,
        w_head.reshape(-1, 128),
        click_labels.T,
    )
    return (
        loss[0, 0],
        gproj.T,
        gcomp,
        gwin,
        gwout,
        ghead.reshape(-1),
        table_grad.transpose(0, 2, 1),
    )


def solution(mesh):
    fine = Mesh(mesh.devices.reshape(4, 4, 4, 2, 2), ("zh", "x", "y", "zl", "c"))
    emb = ("zh", "x", "y")
    rep = ("zl", "c")
    placed = (
        P(None, rep, emb, None),
        P(None, rep, emb),
        P(emb, rep),
        P(emb, None, None),
        P(),
        P(),
        P(),
        P(),
        P(),
    )
    return jax.shard_map(
        per_device,
        mesh=fine,
        in_specs=placed,
        out_specs=(P(), P(), P(), P(), P(), P(), P(emb, None, None)),
        check_vma=False,
    )
```

```python
import functools
import math

import jax
import jax.numpy as jnp
import numpy as np
from jax import lax
from jax.experimental import pallas as pl
from jax.experimental.pallas import tpu as pltpu
from jax.sharding import Mesh, PartitionSpec as P

EPS = 1e-05
BF = jnp.bfloat16
F32 = jnp.float32
NT = (((1,), (1,)), ((), ()))
TN = (((0,), (0,)), ((), ()))
VMEM_LIMIT = 60 * 1024 * 1024
MESH = pl.DeviceIdType.MESH
AT_WOUT = 4096
AT_GW = AT_WOUT + 1536
AT_LIN = AT_GW + 48
AT_HEAD = AT_LIN + 64
DEN_ROWS = 6144


def mm(a, b, dims=None):
    if dims is None:
        return jnp.dot(a, b, preferred_element_type=F32)
    return lax.dot_general(a, b, dims, preferred_element_type=F32)


def arrived(dst, sem):
    pltpu.make_async_copy(dst, dst, sem).wait()


def step_kernel(
    scale,
    raw_ref,
    lens_ref,
    tabt_ref,
    perm_ref,
    proj_ref,
    comp_ref,
    win_hbm,
    wout_hbm,
    whead_ref,
    label_ref,
    out_tab_ref,
    gwin_hbm,
    gwout_hbm,
    gproj_ref,
    gcomp_ref,
    ghead_ref,
    out_loss_ref,
    win_ref,
    wout_ref,
    win_sem,
    wout_sem,
    gwin_sem,
    gwout_sem,
    ids_ref,
    hp_ref,
    tz_ref,
    idt_ref,
    col_ref,
    y_ref,
    x_ref,
    winp_ref,
    den_ref,
    gw_ref,
    split_ref,
    xp_ref,
    mix_ref,
    inter_ref,
    nb_ref,
    ld_ref,
    slope_ref,
    da_ref,
    db_ref,
    dc_ref,
    dd_ref,
    de_ref,
    df_ref,
    te_ref,
    tf_ref,
    tr_ref,
    sa_ref,
    sb_ref,
    sp_ref,
    sz_ref,
    asend,
    arecv,
    irecv,
    ysend,
    xrecv,
    gsend,
    grecv,
    free_sem,
    core_sem,
    dsend,
    dp_sem,
    dz_sem,
    dg_sem,
    dx_sem,
    dh_sem,
    t1send,
    t1recv,
    t2send,
    t2recv,
    t3send,
    t3recv,
    t4send,
    t4recv,
    ssend,
    sc_sem,
    sp_sem,
    sz_sem,
):
    zh, px, py, zl, c = [lax.axis_index(name) for name in ("zh", "x", "y", "zl", "c")]
    n_p, n_z = 16, 8
    z = zh * 2 + zl
    p = px * 4 + py
    other = 1 - c
    sibling = (zh, px, py, zl, other)
    n_f, n_b, n_k, tile = 128, 128, 16, 16
    rows = 512
    low, high, rest_rows = slice(0, 256), slice(256, 512), slice(512, 768)
    width = n_k * n_f
    half = DEN_ROWS // 2
    chunk = half // n_p
    o = py * other + px * c
    o_other = px * other + py * c

    def at_plane(q):
        return (zh, q // 4, q % 4, zl, c)

    m = o_other * 4 + o

    def at_m(k):
        a, b = k // 4, k % 4
        return (zh, a * other + b * c, b * other + a * c, zl, c)

    def cross(d):
        return (zh, (px + d * other) % 4, (py + d * c) % 4, zl, c)

    def at_z(v):
        return (v // 2, px, py, v % 2, c)

    def along(d):
        return (zh, (px + d * c) % 4, (py + d * other) % 4, zl, c)

    def in_row(s, d):
        if s == 0:
            return (px + d) % 4, (zh, (px + d) % 4, py, zl, c)
        return (py + d) % 4, (zh, px, (py + d) % 4, zl, c)

    def remote(src, dst, send_sem, recv_sem, device):
        return pltpu.make_async_remote_copy(
            src_ref=src,
            dst_ref=dst,
            send_sem=send_sem,
            recv_sem=recv_sem,
            device_id=device,
            device_id_type=MESH,
        )

    load_win = pltpu.make_async_copy(win_hbm, win_ref, win_sem)
    load_wout = pltpu.make_async_copy(wout_hbm, wout_ref, wout_sem)
    load_win.start()
    load_wout.start()
    barrier = pltpu.get_barrier_semaphore()
    partners = [sibling, (zh, px, py, 1 - zl, other)]
    partners += [at_plane((p + d) % n_p) for d in range(1, n_p)]
    partners += [at_z((z + d) % n_z) for d in range(1, n_z)]
    for dz in range(1, 4):
        for d in range(1, 4):
            partners.append(((zh + dz) % 4, px, (py + d) % 4, zl, c))
            partners.append(((zh + dz) % 4, (px + d) % 4, py, zl, c))
    for device in partners:
        pl.semaphore_signal(barrier, inc=1, device_id=device, device_id_type=MESH)
    eye = (
        lax.broadcasted_iota(jnp.int32, (128, 128), 0)
        == lax.broadcasted_iota(jnp.int32, (128, 128), 1)
    ).astype(F32).astype(BF)
    mine = c * 16 + zh * 4 + o
    for j, at in ((c, mine), (other, other * 16 + zh * 4 + o_other)):
        tz_ref[at, :rows, :] = mm(tabt_ref[j, :128, :], eye, TN).astype(BF)
        tz_ref[at, rest_rows, :] = (
            mm(tabt_ref[j, 128:, low], eye[:64], TN) + mm(tabt_ref[j, 128:, high], eye[64:], TN)
        ).astype(BF)
    for slot in range(2):
        for j in range(2):
            ids = jnp.where(
                lens_ref[j : j + 1, :] > slot, raw_ref[j, slot : slot + 1, :], rows
            )
            for e in range(64):
                ez, ex, ey = e // 16, e // 4 % 4, e % 4
                to, at = (ez * 4 + ey, ex) if j == 0 else (ez * 4 + ex, ey)
                ids_ref[j, to, slot * 4 + at : slot * 4 + at + 1, :] = ids[
                    :, e * 128 : (e + 1) * 128
                ]
    pl.semaphore_wait(barrier, len(partners))

    sends = []

    def send(src, dst, sem, device):
        copy = remote(src, dst, asend.at[len(sends)], sem, device)
        copy.start()
        sends.append(copy)

    def send_table(at, device):
        send(tz_ref.at[at], tz_ref.at[at], arecv.at[at], device)

    near = (zh + 3 + 2 * zl) % 4
    for to, lo in ((near, 0), (near, 1), ((zh + 2) % 4, 1 - zl)):
        send_table(mine, (to, px, py, lo, c))
    for d in range(1, 4):
        send_table(mine, along(d))
    for dz in range(4):
        for d in range(4):
            if dz == 0 and d == 0:
                continue
            to = (zh + dz) % 4
            ty, tx = (py + d) % 4, (px + d) % 4
            send(
                ids_ref.at[0, to * 4 + ty],
                idt_ref.at[0, zh * 4 + py],
                irecv.at[0, zh * 4 + py],
                (to, px, ty, zl, c),
            )
            send(
                ids_ref.at[1, to * 4 + tx],
                idt_ref.at[1, zh * 4 + px],
                irecv.at[1, zh * 4 + px],
                (to, tx, py, zl, c),
            )
    idt_ref[0, zh * 4 + py] = ids_ref[0, zh * 4 + py]
    idt_ref[1, zh * 4 + px] = ids_ref[1, zh * 4 + px]
    for dz in (1, 3, 2):
        at = c * 16 + (zh + dz) % 4 * 4 + o
        arrived(tz_ref.at[at], arecv.at[at])
        for d in range(1, 4):
            send_table(at, along(d))
        send_table(at, sibling)

    perm = perm_ref[...]
    wt = jnp.concatenate([mm(proj_ref[...], perm), mm(comp_ref[...], perm)], 0).astype(BF)
    n_head = wout_ref.shape[1] // 128
    heads = whead_ref[...].astype(F32)
    head = jnp.concatenate([heads[i : i + 1] for i in range(n_head)], 1)
    split_ref[2, :48, :] = heads[n_head:]
    r0, r1, r2 = [split_ref[2, pl.ds(i, 16, stride=3), :] for i in range(3)]
    left64 = lax.broadcasted_iota(jnp.int32, (16, 128), 1) < 64
    turn1, turn2 = pltpu.roll(r1, 64, 1), pltpu.roll(r2, 64, 1)
    hp_ref[0, pl.ds(0, 16, stride=2), :] = r0
    hp_ref[0, pl.ds(1, 16, stride=2), :] = jnp.where(left64, turn1, turn2)
    hp_ref[1, pl.ds(0, 16, stride=2), :] = jnp.where(left64, r1, turn1)
    hp_ref[1, pl.ds(1, 16, stride=2), :] = jnp.where(left64, turn2, r2)
    hpair = jnp.concatenate([hp_ref[0], hp_ref[1], hp_ref[0]], 1)
    load_win.wait()
    load_wout.wait()
    for side in range(2):
        cols = slice(side * 128, (side + 1) * 128)
        split_ref[side] = win_ref[:, cols].astype(F32)
        for k in range(n_k):
            block = split_ref[side, pl.ds(k, n_f, stride=n_k), :].astype(BF)
            winp_ref[k * n_f : (k + 1) * n_f, cols] = mm(perm, block, TN).astype(BF)

    for dz in (0, 1, 3, 2):
        for d in (1, 3, 2):
            at = c * 16 + (zh + dz) % 4 * 4 + (o + d) % 4
            arrived(tz_ref.at[at], arecv.at[at])
            send_table(at, sibling)
    for dz in range(4):
        for d in range(4):
            if dz == 0 and d == 0:
                continue
            v = (zh + dz) % 4 * 4
            for s, own in ((0, py), (1, px)):
                at = v + (own + d) % 4
                arrived(idt_ref.at[s, at], irecv.at[s, at])
    for s in range(2):
        col_ref[s] = idt_ref[s].reshape(128, 128).T
    for dz in (0, 1, 3, 2):
        for d in range(4):
            if dz == 0 and d == 0:
                continue
            at = other * 16 + (zh + dz) % 4 * 4 + (o_other + d) % 4
            arrived(tz_ref.at[at], arecv.at[at])

    def row_copy(q, s, d, send_sems, recv_sems):
        to, device = in_row(s, d)
        here = py if s else px
        return remote(
            y_ref.at[q, s, to],
            x_ref.at[q, s, here],
            send_sems.at[q, s, to],
            recv_sems.at[q, s, here],
            device,
        )

    def keep_own(q):
        x_ref[q, 0, px] = y_ref[q, 0, px]
        x_ref[q, 1, py] = y_ref[q, 1, py]

    def row_arrived(q, recv_sems):
        for s in range(2):
            for d in (1, 3, 2):
                src = in_row(s, d)[0]
                arrived(x_ref.at[q, s, src], recv_sems.at[q, s, src])

    def lookup(q, carry):
        def one_set(s, inner):
            cols = jnp.concatenate(
                [
                    col_ref[s, pl.ds(pl.multiple_of(h * 64 + q * tile, tile), tile), :]
                    for h in range(2)
                ],
                0,
            )
            lane = lax.broadcasted_iota(jnp.int32, (128, rows), 1)
            first = lax.broadcasted_iota(jnp.int32, (4, tile, 128), 2) < 64
            for i in range(16):
                hot = jnp.zeros((128, rows), F32)
                for slot in range(2):
                    at = i * 8 + slot * 4
                    ids = jnp.concatenate([cols[:, at + k : at + k + 1] for k in range(4)], 0)
                    hot = hot + jnp.where(lane == ids, 1.0, 0.0)
                hot = hot.astype(BF)
                f = s * 16 + i
                rest = tz_ref[f, rest_rows, :]
                one = mm(hot[:, low], jnp.concatenate([tz_ref[f, low, :], rest], 1))
                two = mm(hot[:, high], jnp.concatenate([tz_ref[f, high, :], rest], 1))
                main = one[:, :128] + two[:, :128]
                y_ref[q, s, :, i, : 2 * tile, :] = main.astype(BF).reshape(4, 2 * tile, 128)
                one, two = [v[:, 128:].reshape(4, 2, tile, 128) for v in (one, two)]

                def turn(v):
                    return pltpu.roll(v.reshape(64, 128), 64, 1).reshape(4, tile, 128)

                tail = jnp.where(
                    first, one[:, 0] + turn(two[:, 0]), turn(one[:, 1]) + two[:, 1]
                )
                y_ref[q, s, :, i, 2 * tile :, :] = tail.astype(BF)
            return inner

        lax.fori_loop(0, 2, one_set, 0)
        for d in (1, 3, 2):
            for s in range(2):
                row_copy(q, s, d, ysend, xrecv).start()
        keep_own(q)
        return carry

    lax.fori_loop(0, 4, lookup, 0)
    for copy in sends:
        copy.wait_send()

    lane1 = lax.broadcasted_iota(jnp.int32, (n_k, 384), 1) < 192
    row_lane1 = lax.broadcasted_iota(jnp.int32, (1, 384), 1) < 192

    def load_group(q, carry):
        row_arrived(q, xrecv)
        for part in range(3):
            block = x_ref[q, :, :, :, part * tile : (part + 1) * tile, :]
            split_ref[part] = block.astype(F32).reshape(n_f * tile, 128)

        def pair(j, inner):
            p = q * tile + j
            pieces = [
                split_ref[part, pl.ds(j, n_f, stride=tile), :].astype(BF) for part in (0, 2, 1)
            ]
            x3 = jnp.concatenate(pieces, 1)
            for part in range(3):
                first = pl.multiple_of(p % 2 * 384 + part * 128, 128)
                xp_ref[p // 2, pl.ds(first, 128), :] = pieces[part]
            mixed = mm(wt, x3)
            mix_ref[p] = mixed
            compact = mixed[:n_k]
            stacked = jnp.concatenate(
                [jnp.where(lane1, compact, 0.0), jnp.where(lane1, 0.0, compact)], 0
            ).astype(BF)
            inter = mm(stacked, x3, NT)
            inter_ref[pl.ds(p, n_k, stride=n_b), :] = inter[:n_k]
            inter_ref[pl.ds(64 + p, n_k, stride=n_b), :] = inter[n_k:]
            ld_ref[pl.ds(p, 1), :] = jnp.sum(mixed[n_k:] * hpair, 0, keepdims=True)
            return inner

        lax.fori_loop(0, tile, pair, 0, unroll=2)
        return carry

    lax.fori_loop(0, 64 // tile, load_group, 0)

    for s in range(2):
        for d in range(1, 4):
            pl.semaphore_signal(
                free_sem, inc=1, device_id=in_row(s, d)[1], device_id_type=MESH
            )

    total = jnp.zeros((n_b, n_f), F32)
    for k in range(n_k):
        total = total + inter_ref[k * n_b : (k + 1) * n_b, :]
    center = jnp.sum(total, 1, keepdims=True) / width
    total = jnp.zeros((n_b, n_f), F32)
    for k in range(n_k):
        shifted = inter_ref[k * n_b : (k + 1) * n_b, :] - center
        total = total + shifted * shifted
    rstd = lax.rsqrt(jnp.sum(total, 1, keepdims=True) / width + EPS)
    for k in range(n_k):
        normed = (inter_ref[k * n_b : (k + 1) * n_b, :] - center) * rstd
        inter_ref[k * n_b : (k + 1) * n_b, :] = normed
        nb_ref[:, k * n_f : (k + 1) * n_f] = normed.astype(BF)
    pre_act = mm(nb_ref[...], winp_ref[...])
    sigma = 1.0 / (1.0 + jnp.exp(-pre_act))
    hidden = (pre_act * sigma).astype(BF)
    factor = mm(hidden, wout_ref[...])
    lin = ld_ref[...]
    lin1 = jnp.sum(jnp.where(row_lane1, lin, 0.0), 1, keepdims=True)
    lin2 = jnp.sum(jnp.where(row_lane1, 0.0, lin), 1, keepdims=True)
    logit = jnp.sum(factor * head, 1, keepdims=True) + jnp.concatenate([lin1, lin2], 0)
    target = jnp.broadcast_to(label_ref[...].astype(F32), (8, 128)).T[:, :1]
    terms = jnp.maximum(logit, 0.0) + jnp.log1p(jnp.exp(-jnp.abs(logit))) - target * logit
    sa_ref[48:, :] = jnp.broadcast_to(
        jnp.sum(jnp.broadcast_to(terms, (n_b, 128)), 0, keepdims=True), (8, 128)
    )
    slope = scale * (1.0 / (1.0 + jnp.exp(-logit)) - target)
    slope_ref[...] = jnp.broadcast_to(slope, (n_b, 128))
    den_ref[AT_HEAD:, :] = jnp.zeros((den_ref.shape[0] - AT_HEAD, 128), F32)
    ghead = jnp.sum(slope * factor, 0, keepdims=True)
    for i in range(ghead.shape[1] // 128):
        den_ref[AT_HEAD + i : AT_HEAD + i + 1, :] = ghead[:, i * 128 : (i + 1) * 128]
    gfactor = (slope * head).astype(BF)
    for i in range(gfactor.shape[1] // 128):
        den_ref[AT_WOUT + i * 256 : AT_WOUT + (i + 1) * 256, :] = mm(
            hidden, gfactor[:, i * 128 : (i + 1) * 128], TN
        )
    ghidden = mm(gfactor, wout_ref[...], NT)
    gpre = (ghidden * sigma * (1.0 + pre_act * (1.0 - sigma))).astype(BF)
    first = jnp.zeros((n_b, n_f), F32)
    second = jnp.zeros((n_b, n_f), F32)
    for k in range(n_k):
        feats = slice(k * n_f, (k + 1) * n_f)
        gwin = mm(nb_ref[:, feats], gpre, TN)
        den_ref[feats, :] = gwin[:, :128]
        den_ref[width + k * n_f : width + (k + 1) * n_f, :] = gwin[:, 128:]
        gnormed = mm(gpre, winp_ref[feats, :], NT)
        first = first + gnormed
        second = second + gnormed * inter_ref[k * n_b : (k + 1) * n_b, :]
    def slope_row(p):
        s1 = slope_ref[pl.ds(p, 1), :]
        s2 = slope_ref[pl.ds(64 + p, 1), :]
        return jnp.where(
            row_lane1,
            jnp.concatenate([s1, s1, s1], 1),
            jnp.concatenate([s2, s2, s2], 1),
        )

    ghl = lax.fori_loop(
        0,
        64,
        lambda p, sum: sum + slope_row(p) * mix_ref[p, n_k:, :],
        jnp.zeros((32, 384), F32),
        unroll=4,
    )
    middle = ghl[:, 128:256]
    lane = lax.broadcasted_iota(jnp.int32, middle.shape, 1)
    den_ref[AT_LIN : AT_LIN + 32, :] = ghl[:, :128] + ghl[:, 256:]
    den_ref[AT_LIN + 32 : AT_LIN + 64, :] = jnp.where(
        lane < 64, middle + pltpu.roll(middle, 64, 1), 0.0
    )
    den_ref[AT_GW:AT_LIN, :] = jnp.zeros((AT_LIN - AT_GW, 128), F32)

    def dense_core():
        return remote(da_ref, db_ref, dsend.at[0], core_sem, sibling)

    def dense_plane(d):
        to = (m + d) % n_p
        return remote(
            dc_ref.at[to], dd_ref.at[m], dsend.at[d], dp_sem.at[m], at_m(to)
        )

    def dense_z(d):
        return remote(
            de_ref.at[z], de_ref.at[z], dsend.at[15 + d], dz_sem.at[z], at_z((z + d) % n_z)
        )

    def dense_gather(d):
        at = c * n_p + m
        return remote(df_ref.at[at], df_ref.at[at], dsend.at[22 + d], dg_sem.at[o], along(d))

    def four(core, a):
        return df_ref.at[pl.ds(core * n_p + a * 4, 4)]

    def dense_spread(d):
        part = four(c, o_other)
        return remote(part, part, dsend.at[25 + d], dx_sem.at[o_other], cross(d))

    def dense_last(d):
        a = (o_other + d) % 4
        return remote(four(c, a), four(c, a), dsend.at[29 + d], dh_sem.at[a], sibling)

    def dense_step1():
        arrived(db_ref, core_sem)

        def add(i, carry):
            at = pl.multiple_of(i * chunk, chunk)
            mine = den_ref[pl.ds(pl.multiple_of(c * half + i * chunk, chunk), chunk), :]
            dc_ref[i] = (mine + db_ref[pl.ds(at, chunk), :].astype(F32)).astype(BF)
            return carry

        lax.fori_loop(0, n_p, add, 0)
        for d in range(1, n_p):
            dense_plane(d).start()

    def dense_step2():
        own = dc_ref[m].astype(F32)
        for d in range(1, n_p):
            q = (m + d) % n_p
            arrived(dd_ref.at[q], dp_sem.at[q])
            own = own + dd_ref[q].astype(F32)
        de_ref[z] = own.astype(BF)
        for d in range(1, n_z):
            dense_z(d).start()

    def dense_step3():
        for d in range(1, n_z):
            v = (z + d) % n_z
            arrived(de_ref.at[v], dz_sem.at[v])
        own = de_ref[0].astype(F32)
        for v in range(1, n_z):
            own = own + de_ref[v].astype(F32)
        df_ref[c * n_p + m] = own.astype(BF)
        for d in range(1, 4):
            dense_gather(d).start()

    def dense_step4():
        for d in range(1, 4):
            k = (o + d) % 4
            arrived(df_ref.at[c * n_p + o_other * 4 + k], dg_sem.at[k])
        for d in range(1, 4):
            dense_spread(d).start()
        dense_last(0).start()

    def dense_step5():
        for d in range(1, 4):
            a = (o_other + d) % 4
            arrived(four(c, a), dx_sem.at[a])
            dense_last(d).start()

    da_ref[...] = den_ref[pl.ds(pl.multiple_of(other * half, half), half), :].astype(BF)
    dense_core().start()
    mean1 = jnp.sum(first, 1, keepdims=True) / width
    mean2 = jnp.sum(second, 1, keepdims=True) / width
    for k in range(n_k):
        feats = slice(k * n_f, (k + 1) * n_f)
        span = slice(k * n_b, (k + 1) * n_b)
        gnormed = mm(gpre, winp_ref[feats, :], NT)
        inter_ref[span, :] = rstd * (gnormed - mean1 - inter_ref[span, :] * mean2)

    for q in range(4):
        for s in range(2):
            for d in range(1, 4):
                row_copy(q, s, d, ysend, xrecv).wait_send()
    pl.semaphore_wait(free_sem, 6)
    gw_ref[...] = jnp.zeros_like(gw_ref)
    dense_step1()

    def back_group(q, carry):
        pl.when(q == 2)(dense_step2)
        pl.when(q == 3)(dense_step3)

        def pair(j, inner):
            p = q * tile + j
            x3 = jnp.concatenate(
                [
                    xp_ref[p // 2, pl.ds(pl.multiple_of(p % 2 * 384 + part * 128, 128), 128), :]
                    for part in range(3)
                ],
                1,
            )
            gi = jnp.concatenate(
                [
                    inter_ref[pl.ds(p, n_k, stride=n_b), :],
                    inter_ref[pl.ds(64 + p, n_k, stride=n_b), :],
                ],
                0,
            ).astype(BF)
            gc = mm(gi, x3)
            gc = jnp.where(lane1, gc[:n_k], gc[n_k:]).astype(BF)
            srow = slope_row(p)
            gl = (srow * hpair).astype(BF)
            compact = mix_ref[p, :n_k, :]
            tail = jnp.concatenate([gc, gl], 0)
            right = jnp.concatenate(
                [
                    jnp.where(lane1, compact, 0.0).astype(BF),
                    jnp.where(lane1, 0.0, compact).astype(BF),
                    tail,
                ],
                0,
            )
            left = jnp.concatenate([gi, wt], 0)
            gp = mm(left, right, TN)
            gw_ref[...] += mm(tail, x3, NT)
            for part, at in ((0, 0), (2, 128), (1, 256)):
                split_ref[part, pl.ds(j, n_f, stride=tile), :] = gp[:, at : at + 128]
            return inner

        lax.fori_loop(0, tile, pair, 0, unroll=2)
        for part in range(3):
            y_ref[q, :, :, :, part * tile : (part + 1) * tile, :] = (
                split_ref[part].reshape(2, 4, 16, tile, 128).astype(BF)
            )
        for d in (1, 3, 2):
            for s in range(2):
                row_copy(q, s, d, gsend, grecv).start()
        keep_own(q)
        return carry

    lax.fori_loop(0, 64 // tile, back_group, 0)

    def small_core():
        return remote(sa_ref, sb_ref, ssend.at[0], sc_sem, sibling)

    def small_row(s, d):
        here = py if s else px
        return remote(
            sp_ref.at[s, here],
            sp_ref.at[s, here],
            ssend.at[s * 4 + d],
            sp_sem.at[s, here],
            in_row(s, d)[1],
        )

    def small_start(s):
        if s == 0:
            arrived(sb_ref, sc_sem)
            sp_ref[0, px] = sa_ref[...] + sb_ref[...]
        else:
            sp_ref[1, py] = small_sum(0)
        for d in range(1, 4):
            small_row(s, d).start()

    def small_sum(s):
        for d in range(1, 4):
            src = in_row(s, d)[0]
            arrived(sp_ref.at[s, src], sp_sem.at[s, src])
        return sp_ref[s, 0] + sp_ref[s, 1] + sp_ref[s, 2] + sp_ref[s, 3]

    def small_z(d):
        return remote(
            sz_ref.at[z], sz_ref.at[z], ssend.at[15 + d], sz_sem.at[z], at_z((z + d) % n_z)
        )

    sa_ref[:48, :] = gw_ref[...]
    small_core().start()
    dense_step4()

    def table_grad(s, i):
        hots, mains, rests = [], [], []
        row = lax.broadcasted_iota(jnp.int32, (rows, 128), 0)
        for src in range(4):
            hot = jnp.zeros((rows, 128), F32)
            for slot in range(2):
                ids = idt_ref[s, i, slot * 4 + src : slot * 4 + src + 1, :]
                hot = hot + jnp.where(row == ids, 1.0, 0.0)
            hots.append(hot.astype(BF))
            for k in range(8):
                mains.append(x_ref[k % 4, s, src, i, k // 4 * tile : (k // 4 + 1) * tile, :])
            for q in range(4):
                rests.append(x_ref[q, s, src, i, 2 * tile :, :])
        turned = pltpu.roll(jnp.concatenate(rests, 0).astype(F32), 64, 1).astype(BF)
        tails = []
        for src in range(4):
            tails += rests[src * 4 : src * 4 + 4]
            tails.append(turned[src * 64 : (src + 1) * 64])
        right = jnp.concatenate([jnp.concatenate(mains, 0), jnp.concatenate(tails, 0)], 1)
        sums = mm(jnp.concatenate(hots, 1), right)
        lane = lax.broadcasted_iota(jnp.int32, (256, 128), 1)
        tail = jnp.where(lane < 64, sums[low, 128:], pltpu.roll(sums[high, 128:], 64, 1))
        return sums[:, :128], tail

    def table_core(i):
        return remote(
            tz_ref.at[16 + i], tz_ref.at[i], t1send.at[i], t1recv.at[i], sibling
        )

    def table_along(d, v):
        return remote(
            xp_ref.at[v * 4 + (o + d) % 4],
            xp_ref.at[16 + o * 4 + v],
            t2send.at[d * 4 + v],
            t2recv.at[o * 4 + v],
            along(d),
        )

    def table_z(to):
        return remote(te_ref.at[to], tf_ref.at[z], t3send.at[to], t3recv.at[z], at_z(to))

    own_slot = 2 * c + zl

    def table_replica(k):
        device = (sibling, (zh, px, py, 1 - zl, c), (zh, px, py, 1 - zl, other))[k]
        return remote(
            tr_ref.at[own_slot], tr_ref.at[own_slot], t4send.at[k], t4recv.at[own_slot], device
        )

    for q in range(4):
        row_arrived(q, grecv)

    def for_sibling(n, carry):
        i = (zh + 1 + n // 4) % 4 * 4 + (o_other + 1 + n % 4) % 4
        main, tail = table_grad(other, i)
        tz_ref[16 + i, :rows, :] = main.astype(BF)
        tz_ref[16 + i, rest_rows, :] = tail.astype(BF)
        table_core(i).start()
        return carry

    def for_chip(n, carry):
        d, v = n % 4 + 1, (zh + 1 + n // 4) % 4
        i = v * 4 + (o + d) % 4
        main, tail = table_grad(c, i)
        arrived(tz_ref.at[i], t1recv.at[i])
        xp_ref[i, :rows, :] = (main + tz_ref[i, :rows, :].astype(F32)).astype(BF)
        xp_ref[i, rest_rows, :] = (tail + tz_ref[i, rest_rows, :].astype(F32)).astype(BF)

        @pl.when(d < 4)
        def _():
            table_along(d, v).start()

        return carry

    def by_owner(t, carry):
        pl.when(t == 1)(functools.partial(small_start, 0))
        pl.when(t == 3)(functools.partial(small_start, 1))

        @pl.when(t < 4)
        def _():
            lax.fori_loop(t * 4, t * 4 + 4, for_sibling, 0)

        @pl.when(t > 0)
        def _():
            lax.fori_loop(t * 4 - 4, t * 4, for_chip, 0)

        return carry

    lax.fori_loop(0, 5, by_owner, 0)
    dense_step5()
    sz_ref[z] = small_sum(1)
    for d in range(1, n_z):
        small_z(d).start()

    own = None
    for dv in (1, 2, 3, 0):
        v = (zh + dv) % 4
        for k in range(1, 4):
            at = (o + k) % 4 * 4 + v
            arrived(xp_ref.at[16 + at], t2recv.at[at])
        for flip in (1, 0):
            lo = (zl + flip) % 2
            span = pl.ds(pl.multiple_of(lo * 384, 384), 384)
            own = xp_ref[v * 4 + o, span, :].astype(F32)
            for k in range(1, 4):
                own = own + xp_ref[16 + (o + k) % 4 * 4 + v, span, :].astype(F32)
            if dv > 0 or flip > 0:
                te_ref[v * 2 + lo] = own.astype(BF)
                table_z(v * 2 + lo).start()

    for a in range(4):
        arrived(four(other, a), dh_sem.at[a])

    def final(first, count):
        pieces = []
        at = first
        while at < first + count:
            i, r = at // chunk, at % chunk
            n = min(chunk - r, first + count - at)
            pieces.append(df_ref[i, r : r + n, :])
            at += n
        return pieces[0] if len(pieces) == 1 else jnp.concatenate(pieces, 0)

    stores = []

    def store(src, dst, sem):
        copy = pltpu.make_async_copy(src, dst, sem)
        copy.start()
        stores.append(copy)

    for side in range(2):
        for k in range(n_k):
            block = final(side * 2048 + k * 128, 128)
            split_ref[side, pl.ds(k, n_f, stride=n_k), :] = mm(perm, block)
        store(
            split_ref.at[side],
            gwin_hbm.at[:, side * 128 : (side + 1) * 128],
            gwin_sem.at[side],
        )
    for i in range(n_head):
        span = slice(i * 256, (i + 1) * 256)
        split_ref[2, span, :] = final(AT_WOUT + i * 256, 256).astype(F32)
        store(
            split_ref.at[2, span],
            gwout_hbm.at[:, i * 128 : (i + 1) * 128],
            gwout_sem.at[i],
        )
    ghead_ref[:n_head, :] = final(AT_HEAD, 16).astype(F32)[:n_head]
    hp_ref[0] = final(AT_LIN, 32).astype(F32)
    hp_ref[1] = final(AT_LIN + 32, 32).astype(F32)
    even, odd = [hp_ref[0, pl.ds(i, 16, stride=2), :] for i in range(2)]
    even_rest, odd_rest = [hp_ref[1, pl.ds(i, 16, stride=2), :] for i in range(2)]
    turned = pltpu.roll(odd, 64, 1)
    lin_ref = split_ref.at[2, 1536:]
    lin_ref[pl.ds(0, 16, stride=3), :] = even
    lin_ref[pl.ds(1, 16, stride=3), :] = jnp.where(left64, even_rest, turned)
    lin_ref[pl.ds(2, 16, stride=3), :] = jnp.where(
        left64, turned, pltpu.roll(odd_rest, 64, 1)
    )
    ghead_ref[n_head:, :] = lin_ref[:48, :]

    for d in range(1, n_z):
        v = (z + d) % n_z
        arrived(tf_ref.at[v], t3recv.at[v])
        own = own + tf_ref[v].astype(F32)
    tr_ref[own_slot] = own.astype(BF)
    for k in range(3):
        table_replica(k).start()

    for d in range(1, n_z):
        v = (z + d) % n_z
        arrived(sz_ref.at[v], sz_sem.at[v])
    small = sz_ref[0]
    for v in range(1, n_z):
        small = small + sz_ref[v]
    out_loss_ref[...] = small[48:49, :1] * (scale * scale)
    natural = lax.dot_general(
        small[:48],
        perm.astype(F32),
        NT,
        precision=lax.Precision.HIGHEST,
        preferred_element_type=F32,
    )
    gproj_ref[...] = natural[:n_k]
    gcomp_ref[...] = natural[n_k:]

    for d in range(1, 4):
        k = (own_slot + d) % 4
        arrived(tr_ref.at[k], t4recv.at[k])
    for j in range(2):
        first, second = tr_ref[2 * j], tr_ref[2 * j + 1]
        main = jnp.concatenate([first, second[: rows - 384]], 0)
        rest = second[rows - 384 :]
        out_tab_ref[j, :128, :] = mm(eye, main, NT)
        out_tab_ref[j, 128:, low] = mm(eye[:64], rest, NT)
        out_tab_ref[j, 128:, high] = mm(eye[64:], rest, NT)
    for copy in stores:
        copy.wait()

    for q in range(4):
        for s in range(2):
            for d in range(1, 4):
                row_copy(q, s, d, gsend, grecv).wait_send()
    dense_core().wait_send()
    small_core().wait_send()
    for d in range(1, n_p):
        dense_plane(d).wait_send()
    for d in range(n_p):
        table_core(d).wait_send()
    for d in range(4):
        dense_last(d).wait_send()
    for d in range(1, 4):
        dense_gather(d).wait_send()
        dense_spread(d).wait_send()
        small_row(0, d).wait_send()
        small_row(1, d).wait_send()
    for d in range(1, n_z):
        dense_z(d).wait_send()
        small_z(d).wait_send()
        table_z((z + d) % n_z).wait_send()
    for d in range(1, 4):
        for v in range(4):
            table_along(d, v).wait_send()
    for k in range(3):
        table_replica(k).wait_send()


def whole(n):
    return [pl.BlockSpec(memory_space=pltpu.VMEM)] * n


def run_step(scale, *args):
    half = DEN_ROWS // 2
    chunk = half // 16
    blocks = (4, 2, 4, 16, 48, 128)
    dma = pltpu.SemaphoreType.DMA
    vmem = pltpu.VMEM
    anywhere = [pl.BlockSpec(memory_space=pl.ANY)]
    return pl.pallas_call(
        functools.partial(step_kernel, scale),
        out_shape=[
            jax.ShapeDtypeStruct((2, 192, 512), F32),
            jax.ShapeDtypeStruct((2048, 256), F32),
            jax.ShapeDtypeStruct((256, 768), F32),
            jax.ShapeDtypeStruct((16, 128), F32),
            jax.ShapeDtypeStruct((32, 128), F32),
            jax.ShapeDtypeStruct((54, 128), F32),
            jax.ShapeDtypeStruct((1, 1), F32),
        ],
        in_specs=whole(6) + anywhere * 2 + whole(2),
        out_specs=whole(1) + anywhere * 2 + whole(4),
        scratch_shapes=[
            vmem((2048, 256), BF),
            vmem((256, 768), BF),
            dma,
            dma,
            dma((2,)),
            dma((6,)),
            vmem((2, 16, 8, 128), jnp.int32),
            vmem((2, 32, 128), F32),
            vmem((32, 768, 128), BF),
            vmem((2, 16, 8, 128), jnp.int32),
            vmem((2, 128, 128), jnp.int32),
            vmem(blocks, BF),
            vmem(blocks, BF),
            vmem((2048, 256), BF),
            vmem((DEN_ROWS, 128), F32),
            vmem((48, 128), F32),
            vmem((3, 2048, 128), F32),
            vmem((32, 768, 128), BF),
            vmem((64, 48, 384), F32),
            vmem((2048, 128), F32),
            vmem((128, 2048), BF),
            vmem((64, 384), F32),
            vmem((128, 128), F32),
            vmem((half, 128), BF),
            vmem((half, 128), BF),
            vmem((16, chunk, 128), BF),
            vmem((16, chunk, 128), BF),
            vmem((8, chunk, 128), BF),
            vmem((32, chunk, 128), BF),
            vmem((8, 384, 128), BF),
            vmem((8, 384, 128), BF),
            vmem((4, 384, 128), BF),
            vmem((56, 128), F32),
            vmem((56, 128), F32),
            vmem((2, 4, 56, 128), F32),
            vmem((8, 56, 128), F32),
            dma((64,)),
            dma((32,)),
            dma((2, 16)),
            dma((4, 2, 4)),
            dma((4, 2, 4)),
            dma((4, 2, 4)),
            dma((4, 2, 4)),
            pltpu.SemaphoreType.REGULAR,
            dma,
            dma((36,)),
            dma((16,)),
            dma((8,)),
            dma((4,)),
            dma((4,)),
            dma((4,)),
            dma((16,)),
            dma((16,)),
            dma((20,)),
            dma((16,)),
            dma((8,)),
            dma((8,)),
            dma((3,)),
            dma((4,)),
            dma((24,)),
            dma,
            dma((2, 4)),
            dma((8,)),
        ],
        compiler_params=pltpu.CompilerParams(
            vmem_limit_bytes=VMEM_LIMIT, collective_id=0, has_side_effects=True
        ),
        name="step",
    )(*args)


def feature_order():
    at = np.arange(128)
    j, a, zh, b = at // 64, at // 16 % 4, at // 4 % 4, at % 4
    x, y = np.where(j == 0, a, b), np.where(j == 0, b, a)
    perm = np.zeros((128, 128), np.float32)
    perm[zh * 32 + x * 8 + y * 2 + j, at] = 1.0
    return perm


def finish_kernel(*refs):
    n = len(refs) // 2
    for src, dst in zip(refs[:n], refs[n:]):
        dst[...] = src[...]


def finish(*args):
    return pl.pallas_call(
        finish_kernel,
        out_shape=[jax.ShapeDtypeStruct(a.shape, a.dtype) for a in args],
        in_specs=whole(len(args)),
        out_specs=whole(len(args)),
        compiler_params=pltpu.CompilerParams(vmem_limit_bytes=VMEM_LIMIT),
        name="finish",
    )(*args)


def per_device(
    feature_ids, bag_lengths, click_labels, tables, projection, compress, w_in, w_out, w_head
):
    total = feature_ids.shape[0] * lax.axis_size("zl") * lax.axis_size("c")
    results = run_step(
        1.0 / math.sqrt(total),
        feature_ids[:, 0].transpose(1, 2, 0),
        bag_lengths[:, 0].T,
        tables.transpose(0, 2, 1),
        jnp.asarray(feature_order(), BF),
        projection.T,
        compress,
        w_in,
        w_out,
        w_head.reshape(-1, 128),
        click_labels.T,
    )
    table_grad, gwin, gwout, gproj, gcomp, ghead, loss = finish(*results)
    return (
        loss[0, 0],
        gproj.T,
        gcomp,
        gwin,
        gwout,
        ghead.reshape(-1),
        table_grad.transpose(0, 2, 1),
    )


def solution(mesh):
    fine = Mesh(mesh.devices.reshape(4, 4, 4, 2, 2), ("zh", "x", "y", "zl", "c"))
    emb = ("zh", "x", "y")
    rep = ("zl", "c")
    placed = (
        P(None, rep, emb, None),
        P(None, rep, emb),
        P(emb, rep),
        P(emb, None, None),
        P(),
        P(),
        P(),
        P(),
        P(),
    )
    return jax.shard_map(
        per_device,
        mesh=fine,
        in_specs=placed,
        out_specs=(P(), P(), P(), P(), P(), P(), P(emb, None, None)),
        check_vma=False,
    )
```

```python
import functools
import math

import jax
import jax.numpy as jnp
import numpy as np
from jax import lax
from jax.experimental import pallas as pl
from jax.experimental.pallas import tpu as pltpu
from jax.sharding import Mesh, PartitionSpec as P

EPS = 1e-05
BF = jnp.bfloat16
F32 = jnp.float32
NT = (((1,), (1,)), ((), ()))
TN = (((0,), (0,)), ((), ()))
VMEM_LIMIT = 60 * 1024 * 1024
MESH = pl.DeviceIdType.MESH
AT_WOUT = 4096
AT_GW = AT_WOUT + 1536
AT_LIN = AT_GW + 48
AT_HEAD = AT_LIN + 64
DEN_ROWS = 6144


def mm(a, b, dims=None):
    if dims is None:
        return jnp.dot(a, b, preferred_element_type=F32)
    return lax.dot_general(a, b, dims, preferred_element_type=F32)


def arrived(dst, sem):
    pltpu.make_async_copy(dst, dst, sem).wait()


def step_kernel(
    scale,
    raw_ref,
    lens_ref,
    tabt_ref,
    perm_ref,
    proj_ref,
    comp_ref,
    win_hbm,
    wout_hbm,
    whead_ref,
    label_ref,
    out_tab_ref,
    gwin_hbm,
    gwout_hbm,
    gproj_ref,
    gcomp_ref,
    ghead_ref,
    out_loss_ref,
    win_ref,
    wout_ref,
    win_sem,
    wout_sem,
    gwin_sem,
    gwout_sem,
    ids_ref,
    mid_ref,
    msem,
    hp_ref,
    tz_ref,
    idt_ref,
    col_ref,
    y_ref,
    x_ref,
    winp_ref,
    den_ref,
    gw_ref,
    split_ref,
    xp_ref,
    mix_ref,
    inter_ref,
    nb_ref,
    ld_ref,
    slope_ref,
    da_ref,
    db_ref,
    dc_ref,
    dd_ref,
    de_ref,
    df_ref,
    te_ref,
    tf_ref,
    tr_ref,
    sa_ref,
    sb_ref,
    sp_ref,
    sz_ref,
    asend,
    arecv,
    irecv,
    ysend,
    xrecv,
    gsend,
    grecv,
    free_sem,
    core_sem,
    dsend,
    dp_sem,
    dz_sem,
    dg_sem,
    dx_sem,
    dh_sem,
    t1send,
    t1recv,
    t2send,
    t2recv,
    t3send,
    t3recv,
    t4send,
    t4recv,
    ssend,
    sc_sem,
    sp_sem,
    sz_sem,
):
    zh, px, py, zl, c = [lax.axis_index(name) for name in ("zh", "x", "y", "zl", "c")]
    n_p, n_z = 16, 8
    z = zh * 2 + zl
    p = px * 4 + py
    other = 1 - c
    sibling = (zh, px, py, zl, other)
    n_f, n_b, n_k, tile = 128, 128, 16, 16
    rows = 512
    low, high, rest_rows = slice(0, 256), slice(256, 512), slice(512, 768)
    width = n_k * n_f
    half = DEN_ROWS // 2
    chunk = half // n_p
    o = py * other + px * c
    o_other = px * other + py * c

    def at_plane(q):
        return (zh, q // 4, q % 4, zl, c)

    m = o_other * 4 + o

    def at_m(k):
        a, b = k // 4, k % 4
        return (zh, a * other + b * c, b * other + a * c, zl, c)

    def cross(d):
        return (zh, (px + d * other) % 4, (py + d * c) % 4, zl, c)

    def at_z(v):
        return (v // 2, px, py, v % 2, c)

    def along(d):
        return (zh, (px + d * c) % 4, (py + d * other) % 4, zl, c)

    def in_row(s, d):
        if s == 0:
            return (px + d) % 4, (zh, (px + d) % 4, py, zl, c)
        return (py + d) % 4, (zh, px, (py + d) % 4, zl, c)

    def remote(src, dst, send_sem, recv_sem, device):
        return pltpu.make_async_remote_copy(
            src_ref=src,
            dst_ref=dst,
            send_sem=send_sem,
            recv_sem=recv_sem,
            device_id=device,
            device_id_type=MESH,
        )

    load_win = pltpu.make_async_copy(win_hbm, win_ref, win_sem)
    load_wout = pltpu.make_async_copy(wout_hbm, wout_ref, wout_sem)
    load_win.start()
    load_wout.start()
    barrier = pltpu.get_barrier_semaphore()
    partners = [sibling, (zh, px, py, 1 - zl, other)]
    partners += [at_plane((p + d) % n_p) for d in range(1, n_p)]
    partners += [at_z((z + d) % n_z) for d in range(1, n_z)]
    for device in partners:
        pl.semaphore_signal(barrier, inc=1, device_id=device, device_id_type=MESH)
    eye = (
        lax.broadcasted_iota(jnp.int32, (128, 128), 0)
        == lax.broadcasted_iota(jnp.int32, (128, 128), 1)
    ).astype(F32).astype(BF)
    mine = c * 16 + zh * 4 + o
    for j, at in ((c, mine), (other, other * 16 + zh * 4 + o_other)):
        tz_ref[at, :rows, :] = mm(tabt_ref[j, :128, :], eye, TN).astype(BF)
        tz_ref[at, rest_rows, :] = (
            mm(tabt_ref[j, 128:, low], eye[:64], TN) + mm(tabt_ref[j, 128:, high], eye[64:], TN)
        ).astype(BF)
    for slot in range(2):
        for j in range(2):
            ids = jnp.where(
                lens_ref[j : j + 1, :] > slot, raw_ref[j, slot : slot + 1, :], rows
            )
            for e in range(64):
                ez, ex, ey = e // 16, e // 4 % 4, e % 4
                to, at = (ez * 4 + ey, ex) if j == 0 else (ez * 4 + ex, ey)
                ids_ref[j, to // 4, to % 4, slot * 4 + at : slot * 4 + at + 1, :] = ids[
                    :, e * 128 : (e + 1) * 128
                ]
    pl.semaphore_wait(barrier, len(partners))

    sends = []

    def send(src, dst, sem, device):
        copy = remote(src, dst, asend.at[len(sends)], sem, device)
        copy.start()
        sends.append(copy)

    def send_table(at, device):
        send(tz_ref.at[at], tz_ref.at[at], arecv.at[at], device)

    near = (zh + 3 + 2 * zl) % 4
    for to, lo in ((near, 0), (near, 1), ((zh + 2) % 4, 1 - zl)):
        send_table(mine, (to, px, py, lo, c))
    for d in range(1, 4):
        send_table(mine, along(d))
    for dz in range(1, 4):
        to = (zh + dz) % 4
        for s in range(2):
            send(
                ids_ref.at[s, to], mid_ref.at[s, :, zh], msem.at[s, zh], (to, px, py, zl, c)
            )
    for s in range(2):
        mid_ref[s, :, zh] = ids_ref[s, zh]
    for dz in (1, 3, 2):
        at = c * 16 + (zh + dz) % 4 * 4 + o
        arrived(tz_ref.at[at], arecv.at[at])
        for d in range(1, 4):
            send_table(at, along(d))
        send_table(at, sibling)

    for s, own in ((0, py), (1, px)):
        for dz in range(1, 4):
            v = (zh + dz) % 4
            arrived(mid_ref.at[s, :, v], msem.at[s, v])
        for d in range(1, 4):
            to = (own + d) % 4
            device = (zh, px, to, zl, c) if s == 0 else (zh, to, py, zl, c)
            send(mid_ref.at[s, to], idt_ref.at[s, :, own], irecv.at[s, own], device)
        idt_ref[s, :, own] = mid_ref[s, own]

    perm = perm_ref[...]
    wt = jnp.concatenate([mm(proj_ref[...], perm), mm(comp_ref[...], perm)], 0).astype(BF)
    n_head = wout_ref.shape[1] // 128
    heads = whead_ref[...].astype(F32)
    head = jnp.concatenate([heads[i : i + 1] for i in range(n_head)], 1)
    split_ref[2, :48, :] = heads[n_head:]
    r0, r1, r2 = [split_ref[2, pl.ds(i, 16, stride=3), :] for i in range(3)]
    left64 = lax.broadcasted_iota(jnp.int32, (16, 128), 1) < 64
    turn1, turn2 = pltpu.roll(r1, 64, 1), pltpu.roll(r2, 64, 1)
    hp_ref[0, pl.ds(0, 16, stride=2), :] = r0
    hp_ref[0, pl.ds(1, 16, stride=2), :] = jnp.where(left64, turn1, turn2)
    hp_ref[1, pl.ds(0, 16, stride=2), :] = jnp.where(left64, r1, turn1)
    hp_ref[1, pl.ds(1, 16, stride=2), :] = jnp.where(left64, turn2, r2)
    hpair = jnp.concatenate([hp_ref[0], hp_ref[1], hp_ref[0]], 1)
    load_win.wait()
    load_wout.wait()
    for side in range(2):
        cols = slice(side * 128, (side + 1) * 128)
        split_ref[side] = win_ref[:, cols].astype(F32)
        for k in range(n_k):
            block = split_ref[side, pl.ds(k, n_f, stride=n_k), :].astype(BF)
            winp_ref[k * n_f : (k + 1) * n_f, cols] = mm(perm, block, TN).astype(BF)

    for dz in (0, 1, 3, 2):
        for d in (1, 3, 2):
            at = c * 16 + (zh + dz) % 4 * 4 + (o + d) % 4
            arrived(tz_ref.at[at], arecv.at[at])
            send_table(at, sibling)
    for s, own in ((0, py), (1, px)):
        for d in range(1, 4):
            src = (own + d) % 4
            arrived(idt_ref.at[s, :, src], irecv.at[s, src])
    for s in range(2):
        col_ref[s] = idt_ref[s].reshape(128, 128).T
    for dz in (0, 1, 3, 2):
        for d in range(4):
            if dz == 0 and d == 0:
                continue
            at = other * 16 + (zh + dz) % 4 * 4 + (o_other + d) % 4
            arrived(tz_ref.at[at], arecv.at[at])

    def row_copy(q, s, d, send_sems, recv_sems):
        to, device = in_row(s, d)
        here = py if s else px
        return remote(
            y_ref.at[q, s, to],
            x_ref.at[q, s, here],
            send_sems.at[q, s, to],
            recv_sems.at[q, s, here],
            device,
        )

    def keep_own(q):
        x_ref[q, 0, px] = y_ref[q, 0, px]
        x_ref[q, 1, py] = y_ref[q, 1, py]

    def row_arrived(q, recv_sems):
        for s in range(2):
            for d in (1, 3, 2):
                src = in_row(s, d)[0]
                arrived(x_ref.at[q, s, src], recv_sems.at[q, s, src])

    def lookup(q, carry):
        def one_set(s, inner):
            cols = jnp.concatenate(
                [
                    col_ref[s, pl.ds(pl.multiple_of(h * 64 + q * tile, tile), tile), :]
                    for h in range(2)
                ],
                0,
            )
            lane = lax.broadcasted_iota(jnp.int32, (128, rows), 1)
            first = lax.broadcasted_iota(jnp.int32, (4, tile, 128), 2) < 64
            for i in range(16):
                hot = jnp.zeros((128, rows), F32)
                for slot in range(2):
                    at = i * 8 + slot * 4
                    ids = jnp.concatenate([cols[:, at + k : at + k + 1] for k in range(4)], 0)
                    hot = hot + jnp.where(lane == ids, 1.0, 0.0)
                hot = hot.astype(BF)
                f = s * 16 + i
                rest = tz_ref[f, rest_rows, :]
                one = mm(hot[:, low], jnp.concatenate([tz_ref[f, low, :], rest], 1))
                two = mm(hot[:, high], jnp.concatenate([tz_ref[f, high, :], rest], 1))
                main = one[:, :128] + two[:, :128]
                y_ref[q, s, :, i, : 2 * tile, :] = main.astype(BF).reshape(4, 2 * tile, 128)
                one, two = [v[:, 128:].reshape(4, 2, tile, 128) for v in (one, two)]

                def turn(v):
                    return pltpu.roll(v.reshape(64, 128), 64, 1).reshape(4, tile, 128)

                tail = jnp.where(
                    first, one[:, 0] + turn(two[:, 0]), turn(one[:, 1]) + two[:, 1]
                )
                y_ref[q, s, :, i, 2 * tile :, :] = tail.astype(BF)
            return inner

        lax.fori_loop(0, 2, one_set, 0)
        for d in (1, 3, 2):
            for s in range(2):
                row_copy(q, s, d, ysend, xrecv).start()
        keep_own(q)
        return carry

    lax.fori_loop(0, 4, lookup, 0)
    for copy in sends:
        copy.wait_send()

    lane1 = lax.broadcasted_iota(jnp.int32, (n_k, 384), 1) < 192
    row_lane1 = lax.broadcasted_iota(jnp.int32, (1, 384), 1) < 192

    def load_group(q, carry):
        row_arrived(q, xrecv)
        for part in range(3):
            block = x_ref[q, :, :, :, part * tile : (part + 1) * tile, :]
            split_ref[part] = block.astype(F32).reshape(n_f * tile, 128)

        def pair(j, inner):
            p = q * tile + j
            pieces = [
                split_ref[part, pl.ds(j, n_f, stride=tile), :].astype(BF) for part in (0, 2, 1)
            ]
            x3 = jnp.concatenate(pieces, 1)
            for part in range(3):
                first = pl.multiple_of(p % 2 * 384 + part * 128, 128)
                xp_ref[p // 2, pl.ds(first, 128), :] = pieces[part]
            mixed = mm(wt, x3)
            mix_ref[p] = mixed
            compact = mixed[:n_k]
            stacked = jnp.concatenate(
                [jnp.where(lane1, compact, 0.0), jnp.where(lane1, 0.0, compact)], 0
            ).astype(BF)
            inter = mm(stacked, x3, NT)
            inter_ref[pl.ds(p, n_k, stride=n_b), :] = inter[:n_k]
            inter_ref[pl.ds(64 + p, n_k, stride=n_b), :] = inter[n_k:]
            ld_ref[pl.ds(p, 1), :] = jnp.sum(mixed[n_k:] * hpair, 0, keepdims=True)
            return inner

        lax.fori_loop(0, tile, pair, 0, unroll=2)
        return carry

    lax.fori_loop(0, 64 // tile, load_group, 0)

    for s in range(2):
        for d in range(1, 4):
            pl.semaphore_signal(
                free_sem, inc=1, device_id=in_row(s, d)[1], device_id_type=MESH
            )

    total = jnp.zeros((n_b, n_f), F32)
    for k in range(n_k):
        total = total + inter_ref[k * n_b : (k + 1) * n_b, :]
    center = jnp.sum(total, 1, keepdims=True) / width
    total = jnp.zeros((n_b, n_f), F32)
    for k in range(n_k):
        shifted = inter_ref[k * n_b : (k + 1) * n_b, :] - center
        total = total + shifted * shifted
    rstd = lax.rsqrt(jnp.sum(total, 1, keepdims=True) / width + EPS)
    for k in range(n_k):
        normed = (inter_ref[k * n_b : (k + 1) * n_b, :] - center) * rstd
        inter_ref[k * n_b : (k + 1) * n_b, :] = normed
        nb_ref[:, k * n_f : (k + 1) * n_f] = normed.astype(BF)
    pre_act = mm(nb_ref[...], winp_ref[...])
    sigma = 1.0 / (1.0 + jnp.exp(-pre_act))
    hidden = (pre_act * sigma).astype(BF)
    factor = mm(hidden, wout_ref[...])
    lin = ld_ref[...]
    lin1 = jnp.sum(jnp.where(row_lane1, lin, 0.0), 1, keepdims=True)
    lin2 = jnp.sum(jnp.where(row_lane1, 0.0, lin), 1, keepdims=True)
    logit = jnp.sum(factor * head, 1, keepdims=True) + jnp.concatenate([lin1, lin2], 0)
    target = jnp.broadcast_to(label_ref[...].astype(F32), (8, 128)).T[:, :1]
    terms = jnp.maximum(logit, 0.0) + jnp.log1p(jnp.exp(-jnp.abs(logit))) - target * logit
    sa_ref[48:, :] = jnp.broadcast_to(
        jnp.sum(jnp.broadcast_to(terms, (n_b, 128)), 0, keepdims=True), (8, 128)
    )
    slope = scale * (1.0 / (1.0 + jnp.exp(-logit)) - target)
    slope_ref[...] = jnp.broadcast_to(slope, (n_b, 128))
    den_ref[AT_HEAD:, :] = jnp.zeros((den_ref.shape[0] - AT_HEAD, 128), F32)
    ghead = jnp.sum(slope * factor, 0, keepdims=True)
    for i in range(ghead.shape[1] // 128):
        den_ref[AT_HEAD + i : AT_HEAD + i + 1, :] = ghead[:, i * 128 : (i + 1) * 128]
    gfactor = (slope * head).astype(BF)
    for i in range(gfactor.shape[1] // 128):
        den_ref[AT_WOUT + i * 256 : AT_WOUT + (i + 1) * 256, :] = mm(
            hidden, gfactor[:, i * 128 : (i + 1) * 128], TN
        )
    ghidden = mm(gfactor, wout_ref[...], NT)
    gpre = (ghidden * sigma * (1.0 + pre_act * (1.0 - sigma))).astype(BF)
    first = jnp.zeros((n_b, n_f), F32)
    second = jnp.zeros((n_b, n_f), F32)
    for k in range(n_k):
        feats = slice(k * n_f, (k + 1) * n_f)
        gwin = mm(nb_ref[:, feats], gpre, TN)
        den_ref[feats, :] = gwin[:, :128]
        den_ref[width + k * n_f : width + (k + 1) * n_f, :] = gwin[:, 128:]
        gnormed = mm(gpre, winp_ref[feats, :], NT)
        first = first + gnormed
        second = second + gnormed * inter_ref[k * n_b : (k + 1) * n_b, :]
    def slope_row(p):
        s1 = slope_ref[pl.ds(p, 1), :]
        s2 = slope_ref[pl.ds(64 + p, 1), :]
        return jnp.where(
            row_lane1,
            jnp.concatenate([s1, s1, s1], 1),
            jnp.concatenate([s2, s2, s2], 1),
        )

    ghl = lax.fori_loop(
        0,
        64,
        lambda p, sum: sum + slope_row(p) * mix_ref[p, n_k:, :],
        jnp.zeros((32, 384), F32),
        unroll=4,
    )
    middle = ghl[:, 128:256]
    lane = lax.broadcasted_iota(jnp.int32, middle.shape, 1)
    den_ref[AT_LIN : AT_LIN + 32, :] = ghl[:, :128] + ghl[:, 256:]
    den_ref[AT_LIN + 32 : AT_LIN + 64, :] = jnp.where(
        lane < 64, middle + pltpu.roll(middle, 64, 1), 0.0
    )
    den_ref[AT_GW:AT_LIN, :] = jnp.zeros((AT_LIN - AT_GW, 128), F32)

    def dense_core():
        return remote(da_ref, db_ref, dsend.at[0], core_sem, sibling)

    def dense_plane(d):
        to = (m + d) % n_p
        return remote(
            dc_ref.at[to], dd_ref.at[m], dsend.at[d], dp_sem.at[m], at_m(to)
        )

    def dense_z(d):
        return remote(
            de_ref.at[z], de_ref.at[z], dsend.at[15 + d], dz_sem.at[z], at_z((z + d) % n_z)
        )

    def dense_gather(d):
        at = c * n_p + m
        return remote(df_ref.at[at], df_ref.at[at], dsend.at[22 + d], dg_sem.at[o], along(d))

    def four(core, a):
        return df_ref.at[pl.ds(core * n_p + a * 4, 4)]

    def dense_spread(d):
        part = four(c, o_other)
        return remote(part, part, dsend.at[25 + d], dx_sem.at[o_other], cross(d))

    def dense_last(d):
        a = (o_other + d) % 4
        return remote(four(c, a), four(c, a), dsend.at[29 + d], dh_sem.at[a], sibling)

    def dense_step1():
        arrived(db_ref, core_sem)

        def add(i, carry):
            at = pl.multiple_of(i * chunk, chunk)
            mine = den_ref[pl.ds(pl.multiple_of(c * half + i * chunk, chunk), chunk), :]
            dc_ref[i] = (mine + db_ref[pl.ds(at, chunk), :].astype(F32)).astype(BF)
            return carry

        lax.fori_loop(0, n_p, add, 0)
        for d in range(1, n_p):
            dense_plane(d).start()

    def dense_step2():
        own = dc_ref[m].astype(F32)
        for d in range(1, n_p):
            q = (m + d) % n_p
            arrived(dd_ref.at[q], dp_sem.at[q])
            own = own + dd_ref[q].astype(F32)
        de_ref[z] = own.astype(BF)
        for d in range(1, n_z):
            dense_z(d).start()

    def dense_step3():
        for d in range(1, n_z):
            v = (z + d) % n_z
            arrived(de_ref.at[v], dz_sem.at[v])
        own = de_ref[0].astype(F32)
        for v in range(1, n_z):
            own = own + de_ref[v].astype(F32)
        df_ref[c * n_p + m] = own.astype(BF)
        for d in range(1, 4):
            dense_gather(d).start()

    def dense_step4():
        for d in range(1, 4):
            k = (o + d) % 4
            arrived(df_ref.at[c * n_p + o_other * 4 + k], dg_sem.at[k])
        for d in range(1, 4):
            dense_spread(d).start()
        dense_last(0).start()

    def dense_step5():
        for d in range(1, 4):
            a = (o_other + d) % 4
            arrived(four(c, a), dx_sem.at[a])
            dense_last(d).start()

    da_ref[...] = den_ref[pl.ds(pl.multiple_of(other * half, half), half), :].astype(BF)
    dense_core().start()
    mean1 = jnp.sum(first, 1, keepdims=True) / width
    mean2 = jnp.sum(second, 1, keepdims=True) / width
    for k in range(n_k):
        feats = slice(k * n_f, (k + 1) * n_f)
        span = slice(k * n_b, (k + 1) * n_b)
        gnormed = mm(gpre, winp_ref[feats, :], NT)
        inter_ref[span, :] = rstd * (gnormed - mean1 - inter_ref[span, :] * mean2)

    for q in range(4):
        for s in range(2):
            for d in range(1, 4):
                row_copy(q, s, d, ysend, xrecv).wait_send()
    pl.semaphore_wait(free_sem, 6)
    gw_ref[...] = jnp.zeros_like(gw_ref)
    dense_step1()

    def back_group(q, carry):
        pl.when(q == 2)(dense_step2)
        pl.when(q == 3)(dense_step3)

        def pair(j, inner):
            p = q * tile + j
            x3 = jnp.concatenate(
                [
                    xp_ref[p // 2, pl.ds(pl.multiple_of(p % 2 * 384 + part * 128, 128), 128), :]
                    for part in range(3)
                ],
                1,
            )
            gi = jnp.concatenate(
                [
                    inter_ref[pl.ds(p, n_k, stride=n_b), :],
                    inter_ref[pl.ds(64 + p, n_k, stride=n_b), :],
                ],
                0,
            ).astype(BF)
            gc = mm(gi, x3)
            gc = jnp.where(lane1, gc[:n_k], gc[n_k:]).astype(BF)
            srow = slope_row(p)
            gl = (srow * hpair).astype(BF)
            compact = mix_ref[p, :n_k, :]
            tail = jnp.concatenate([gc, gl], 0)
            right = jnp.concatenate(
                [
                    jnp.where(lane1, compact, 0.0).astype(BF),
                    jnp.where(lane1, 0.0, compact).astype(BF),
                    tail,
                ],
                0,
            )
            left = jnp.concatenate([gi, wt], 0)
            gp = mm(left, right, TN)
            gw_ref[...] += mm(tail, x3, NT)
            for part, at in ((0, 0), (2, 128), (1, 256)):
                split_ref[part, pl.ds(j, n_f, stride=tile), :] = gp[:, at : at + 128]
            return inner

        lax.fori_loop(0, tile, pair, 0, unroll=2)
        for part in range(3):
            y_ref[q, :, :, :, part * tile : (part + 1) * tile, :] = (
                split_ref[part].reshape(2, 4, 16, tile, 128).astype(BF)
            )
        for d in (1, 3, 2):
            for s in range(2):
                row_copy(q, s, d, gsend, grecv).start()
        keep_own(q)
        return carry

    lax.fori_loop(0, 64 // tile, back_group, 0)

    def small_core():
        return remote(sa_ref, sb_ref, ssend.at[0], sc_sem, sibling)

    def small_row(s, d):
        here = py if s else px
        return remote(
            sp_ref.at[s, here],
            sp_ref.at[s, here],
            ssend.at[s * 4 + d],
            sp_sem.at[s, here],
            in_row(s, d)[1],
        )

    def small_start(s):
        if s == 0:
            arrived(sb_ref, sc_sem)
            sp_ref[0, px] = sa_ref[...] + sb_ref[...]
        else:
            sp_ref[1, py] = small_sum(0)
        for d in range(1, 4):
            small_row(s, d).start()

    def small_sum(s):
        for d in range(1, 4):
            src = in_row(s, d)[0]
            arrived(sp_ref.at[s, src], sp_sem.at[s, src])
        return sp_ref[s, 0] + sp_ref[s, 1] + sp_ref[s, 2] + sp_ref[s, 3]

    def small_z(d):
        return remote(
            sz_ref.at[z], sz_ref.at[z], ssend.at[15 + d], sz_sem.at[z], at_z((z + d) % n_z)
        )

    sa_ref[:48, :] = gw_ref[...]
    small_core().start()
    dense_step4()

    def table_grad(s, i):
        hots, mains, rests = [], [], []
        row = lax.broadcasted_iota(jnp.int32, (rows, 128), 0)
        for src in range(4):
            hot = jnp.zeros((rows, 128), F32)
            for slot in range(2):
                ids = idt_ref[s, i // 4, i % 4, slot * 4 + src : slot * 4 + src + 1, :]
                hot = hot + jnp.where(row == ids, 1.0, 0.0)
            hots.append(hot.astype(BF))
            for k in range(8):
                mains.append(x_ref[k % 4, s, src, i, k // 4 * tile : (k // 4 + 1) * tile, :])
            for q in range(4):
                rests.append(x_ref[q, s, src, i, 2 * tile :, :])
        turned = pltpu.roll(jnp.concatenate(rests, 0).astype(F32), 64, 1).astype(BF)
        tails = []
        for src in range(4):
            tails += rests[src * 4 : src * 4 + 4]
            tails.append(turned[src * 64 : (src + 1) * 64])
        right = jnp.concatenate([jnp.concatenate(mains, 0), jnp.concatenate(tails, 0)], 1)
        sums = mm(jnp.concatenate(hots, 1), right)
        lane = lax.broadcasted_iota(jnp.int32, (256, 128), 1)
        tail = jnp.where(lane < 64, sums[low, 128:], pltpu.roll(sums[high, 128:], 64, 1))
        return sums[:, :128], tail

    def table_core(i):
        return remote(
            tz_ref.at[16 + i], tz_ref.at[i], t1send.at[i], t1recv.at[i], sibling
        )

    def table_along(d, v):
        return remote(
            xp_ref.at[v * 4 + (o + d) % 4],
            xp_ref.at[16 + o * 4 + v],
            t2send.at[d * 4 + v],
            t2recv.at[o * 4 + v],
            along(d),
        )

    def table_z(to):
        return remote(te_ref.at[to], tf_ref.at[z], t3send.at[to], t3recv.at[z], at_z(to))

    own_slot = 2 * c + zl

    def table_replica(k):
        device = (sibling, (zh, px, py, 1 - zl, c), (zh, px, py, 1 - zl, other))[k]
        return remote(
            tr_ref.at[own_slot], tr_ref.at[own_slot], t4send.at[k], t4recv.at[own_slot], device
        )

    for q in range(4):
        row_arrived(q, grecv)

    def for_sibling(n, carry):
        i = (zh + 1 + n // 4) % 4 * 4 + (o_other + 1 + n % 4) % 4
        main, tail = table_grad(other, i)
        tz_ref[16 + i, :rows, :] = main.astype(BF)
        tz_ref[16 + i, rest_rows, :] = tail.astype(BF)
        table_core(i).start()
        return carry

    def for_chip(n, carry):
        d, v = n % 4 + 1, (zh + 1 + n // 4) % 4
        i = v * 4 + (o + d) % 4
        main, tail = table_grad(c, i)
        arrived(tz_ref.at[i], t1recv.at[i])
        xp_ref[i, :rows, :] = (main + tz_ref[i, :rows, :].astype(F32)).astype(BF)
        xp_ref[i, rest_rows, :] = (tail + tz_ref[i, rest_rows, :].astype(F32)).astype(BF)

        @pl.when(d < 4)
        def _():
            table_along(d, v).start()

        return carry

    def by_owner(t, carry):
        pl.when(t == 1)(functools.partial(small_start, 0))
        pl.when(t == 3)(functools.partial(small_start, 1))

        @pl.when(t < 4)
        def _():
            lax.fori_loop(t * 4, t * 4 + 4, for_sibling, 0)

        @pl.when(t > 0)
        def _():
            lax.fori_loop(t * 4 - 4, t * 4, for_chip, 0)

        return carry

    lax.fori_loop(0, 5, by_owner, 0)
    dense_step5()
    sz_ref[z] = small_sum(1)
    for d in range(1, n_z):
        small_z(d).start()

    own = None
    for dv in (1, 2, 3, 0):
        v = (zh + dv) % 4
        for k in range(1, 4):
            at = (o + k) % 4 * 4 + v
            arrived(xp_ref.at[16 + at], t2recv.at[at])
        for flip in (1, 0):
            lo = (zl + flip) % 2
            span = pl.ds(pl.multiple_of(lo * 384, 384), 384)
            own = xp_ref[v * 4 + o, span, :].astype(F32)
            for k in range(1, 4):
                own = own + xp_ref[16 + (o + k) % 4 * 4 + v, span, :].astype(F32)
            if dv > 0 or flip > 0:
                te_ref[v * 2 + lo] = own.astype(BF)
                table_z(v * 2 + lo).start()

    for a in range(4):
        arrived(four(other, a), dh_sem.at[a])

    def final(first, count):
        pieces = []
        at = first
        while at < first + count:
            i, r = at // chunk, at % chunk
            n = min(chunk - r, first + count - at)
            pieces.append(df_ref[i, r : r + n, :])
            at += n
        return pieces[0] if len(pieces) == 1 else jnp.concatenate(pieces, 0)

    stores = []

    def store(src, dst, sem):
        copy = pltpu.make_async_copy(src, dst, sem)
        copy.start()
        stores.append(copy)

    for side in range(2):
        for k in range(n_k):
            block = final(side * 2048 + k * 128, 128)
            split_ref[side, pl.ds(k, n_f, stride=n_k), :] = mm(perm, block)
        store(
            split_ref.at[side],
            gwin_hbm.at[:, side * 128 : (side + 1) * 128],
            gwin_sem.at[side],
        )
    for i in range(n_head):
        span = slice(i * 256, (i + 1) * 256)
        split_ref[2, span, :] = final(AT_WOUT + i * 256, 256).astype(F32)
        store(
            split_ref.at[2, span],
            gwout_hbm.at[:, i * 128 : (i + 1) * 128],
            gwout_sem.at[i],
        )
    ghead_ref[:n_head, :] = final(AT_HEAD, 16).astype(F32)[:n_head]
    hp_ref[0] = final(AT_LIN, 32).astype(F32)
    hp_ref[1] = final(AT_LIN + 32, 32).astype(F32)
    even, odd = [hp_ref[0, pl.ds(i, 16, stride=2), :] for i in range(2)]
    even_rest, odd_rest = [hp_ref[1, pl.ds(i, 16, stride=2), :] for i in range(2)]
    turned = pltpu.roll(odd, 64, 1)
    lin_ref = split_ref.at[2, 1536:]
    lin_ref[pl.ds(0, 16, stride=3), :] = even
    lin_ref[pl.ds(1, 16, stride=3), :] = jnp.where(left64, even_rest, turned)
    lin_ref[pl.ds(2, 16, stride=3), :] = jnp.where(
        left64, turned, pltpu.roll(odd_rest, 64, 1)
    )
    ghead_ref[n_head:, :] = lin_ref[:48, :]

    for d in range(1, n_z):
        v = (z + d) % n_z
        arrived(tf_ref.at[v], t3recv.at[v])
        own = own + tf_ref[v].astype(F32)
    tr_ref[own_slot] = own.astype(BF)
    for k in range(3):
        table_replica(k).start()

    for d in range(1, n_z):
        v = (z + d) % n_z
        arrived(sz_ref.at[v], sz_sem.at[v])
    small = sz_ref[0]
    for v in range(1, n_z):
        small = small + sz_ref[v]
    out_loss_ref[...] = small[48:49, :1] * (scale * scale)
    natural = lax.dot_general(
        small[:48],
        perm.astype(F32),
        NT,
        precision=lax.Precision.HIGHEST,
        preferred_element_type=F32,
    )
    gproj_ref[...] = natural[:n_k]
    gcomp_ref[...] = natural[n_k:]

    for d in range(1, 4):
        k = (own_slot + d) % 4
        arrived(tr_ref.at[k], t4recv.at[k])
    for j in range(2):
        first, second = tr_ref[2 * j], tr_ref[2 * j + 1]
        main = jnp.concatenate([first, second[: rows - 384]], 0)
        rest = second[rows - 384 :]
        out_tab_ref[j, :128, :] = mm(eye, main, NT)
        out_tab_ref[j, 128:, low] = mm(eye[:64], rest, NT)
        out_tab_ref[j, 128:, high] = mm(eye[64:], rest, NT)
    for copy in stores:
        copy.wait()

    for q in range(4):
        for s in range(2):
            for d in range(1, 4):
                row_copy(q, s, d, gsend, grecv).wait_send()
    dense_core().wait_send()
    small_core().wait_send()
    for d in range(1, n_p):
        dense_plane(d).wait_send()
    for d in range(n_p):
        table_core(d).wait_send()
    for d in range(4):
        dense_last(d).wait_send()
    for d in range(1, 4):
        dense_gather(d).wait_send()
        dense_spread(d).wait_send()
        small_row(0, d).wait_send()
        small_row(1, d).wait_send()
    for d in range(1, n_z):
        dense_z(d).wait_send()
        small_z(d).wait_send()
        table_z((z + d) % n_z).wait_send()
    for d in range(1, 4):
        for v in range(4):
            table_along(d, v).wait_send()
    for k in range(3):
        table_replica(k).wait_send()


def whole(n):
    return [pl.BlockSpec(memory_space=pltpu.VMEM)] * n


def run_step(scale, *args):
    half = DEN_ROWS // 2
    chunk = half // 16
    blocks = (4, 2, 4, 16, 48, 128)
    dma = pltpu.SemaphoreType.DMA
    vmem = pltpu.VMEM
    anywhere = [pl.BlockSpec(memory_space=pl.ANY)]
    return pl.pallas_call(
        functools.partial(step_kernel, scale),
        out_shape=[
            jax.ShapeDtypeStruct((2, 192, 512), F32),
            jax.ShapeDtypeStruct((2048, 256), F32),
            jax.ShapeDtypeStruct((256, 768), F32),
            jax.ShapeDtypeStruct((16, 128), F32),
            jax.ShapeDtypeStruct((32, 128), F32),
            jax.ShapeDtypeStruct((54, 128), F32),
            jax.ShapeDtypeStruct((1, 1), F32),
        ],
        in_specs=whole(6) + anywhere * 2 + whole(2),
        out_specs=whole(1) + anywhere * 2 + whole(4),
        scratch_shapes=[
            vmem((2048, 256), BF),
            vmem((256, 768), BF),
            dma,
            dma,
            dma((2,)),
            dma((6,)),
            vmem((2, 4, 4, 8, 128), jnp.int32),
            vmem((2, 4, 4, 8, 128), jnp.int32),
            dma((2, 4)),
            vmem((2, 32, 128), F32),
            vmem((32, 768, 128), BF),
            vmem((2, 4, 4, 8, 128), jnp.int32),
            vmem((2, 128, 128), jnp.int32),
            vmem(blocks, BF),
            vmem(blocks, BF),
            vmem((2048, 256), BF),
            vmem((DEN_ROWS, 128), F32),
            vmem((48, 128), F32),
            vmem((3, 2048, 128), F32),
            vmem((32, 768, 128), BF),
            vmem((64, 48, 384), F32),
            vmem((2048, 128), F32),
            vmem((128, 2048), BF),
            vmem((64, 384), F32),
            vmem((128, 128), F32),
            vmem((half, 128), BF),
            vmem((half, 128), BF),
            vmem((16, chunk, 128), BF),
            vmem((16, chunk, 128), BF),
            vmem((8, chunk, 128), BF),
            vmem((32, chunk, 128), BF),
            vmem((8, 384, 128), BF),
            vmem((8, 384, 128), BF),
            vmem((4, 384, 128), BF),
            vmem((56, 128), F32),
            vmem((56, 128), F32),
            vmem((2, 4, 56, 128), F32),
            vmem((8, 56, 128), F32),
            dma((64,)),
            dma((32,)),
            dma((2, 4)),
            dma((4, 2, 4)),
            dma((4, 2, 4)),
            dma((4, 2, 4)),
            dma((4, 2, 4)),
            pltpu.SemaphoreType.REGULAR,
            dma,
            dma((36,)),
            dma((16,)),
            dma((8,)),
            dma((4,)),
            dma((4,)),
            dma((4,)),
            dma((16,)),
            dma((16,)),
            dma((20,)),
            dma((16,)),
            dma((8,)),
            dma((8,)),
            dma((3,)),
            dma((4,)),
            dma((24,)),
            dma,
            dma((2, 4)),
            dma((8,)),
        ],
        compiler_params=pltpu.CompilerParams(
            vmem_limit_bytes=VMEM_LIMIT, collective_id=0, has_side_effects=True
        ),
        name="step",
    )(*args)


def feature_order():
    at = np.arange(128)
    j, a, zh, b = at // 64, at // 16 % 4, at // 4 % 4, at % 4
    x, y = np.where(j == 0, a, b), np.where(j == 0, b, a)
    perm = np.zeros((128, 128), np.float32)
    perm[zh * 32 + x * 8 + y * 2 + j, at] = 1.0
    return perm


def finish_kernel(*refs):
    n = len(refs) // 2
    for src, dst in zip(refs[:n], refs[n:]):
        dst[...] = src[...]


def finish(*args):
    return pl.pallas_call(
        finish_kernel,
        out_shape=[jax.ShapeDtypeStruct(a.shape, a.dtype) for a in args],
        in_specs=whole(len(args)),
        out_specs=whole(len(args)),
        compiler_params=pltpu.CompilerParams(vmem_limit_bytes=VMEM_LIMIT),
        name="finish",
    )(*args)


def per_device(
    feature_ids, bag_lengths, click_labels, tables, projection, compress, w_in, w_out, w_head
):
    total = feature_ids.shape[0] * lax.axis_size("zl") * lax.axis_size("c")
    results = run_step(
        1.0 / math.sqrt(total),
        feature_ids[:, 0].transpose(1, 2, 0),
        bag_lengths[:, 0].T,
        tables.transpose(0, 2, 1),
        jnp.asarray(feature_order(), BF),
        projection.T,
        compress,
        w_in,
        w_out,
        w_head.reshape(-1, 128),
        click_labels.T,
    )
    table_grad, gwin, gwout, gproj, gcomp, ghead, loss = finish(*results)
    return (
        loss[0, 0],
        gproj.T,
        gcomp,
        gwin,
        gwout,
        ghead.reshape(-1),
        table_grad.transpose(0, 2, 1),
    )


def solution(mesh):
    fine = Mesh(mesh.devices.reshape(4, 4, 4, 2, 2), ("zh", "x", "y", "zl", "c"))
    emb = ("zh", "x", "y")
    rep = ("zl", "c")
    placed = (
        P(None, rep, emb, None),
        P(None, rep, emb),
        P(emb, rep),
        P(emb, None, None),
        P(),
        P(),
        P(),
        P(),
        P(),
    )
    return jax.shard_map(
        per_device,
        mesh=fine,
        in_specs=placed,
        out_specs=(P(), P(), P(), P(), P(), P(), P(emb, None, None)),
        check_vma=False,
    )
```
